128 devices in a mesh: snap: 2 (over core), tile: 64 (over z, y, x).
Axes of the slice: x: 4, y: 4, z: 4, core: 2. Of those that a mesh axis runs over, the one named last changes fastest.
Arguments:
- velocity: float32 [256, 2, 4096, 256], P('snap', None, 'tile'), may hold values from -48 to 48
- offsets: int32 [256, 2], P('snap'), may hold values from -16 to 16
- phase: int32 [256], P('snap'), may hold values from 0 to 71
Outputs:
- phase_mean: float32 [72, 2, 4096, 256], P('snap', None, 'tile')
- phase_moment: float32 [72, 3, 4096, 256], P('snap', None, 'tile')
The draws below stay inside these ranges and needn't reach their ends.
Inputs may be any that keep to these rules, and one draw needn't show every extreme that they name: `offsets`: column 0 shifts rows and column 1 shifts columns.
All inputs are finite; a program needn't handle non-finite values.
Results may differ from the reference program's by a relative error of at most 0.0003.
Values sent between devices are 32-bit elements; how exact they have to be, the bound alone decides.
A program may use at most 256 MiB of HBM per device.

```python
import math
import jax
import jax.numpy as jnp
import numpy as np
from jax import lax

ROWS_DEV = 64
IMG_W = 256
PHASES = 72
MAXS = 16
RAD = 8
HALO = 24
SNAPS = 256
HEIGHT = 4096
N_TILE = 64


def set_ends(values, own_key, least, top_value):
    shape = values.shape
    spot = [jax.random.randint(jax.random.fold_in(own_key, axis), (), 0, shape[axis]) for axis in range(len(shape))]
    values = values.at[tuple(spot)].set(least)
    longest = shape.index(max(shape))
    spot[longest] = (spot[longest] + 1) % shape[longest]
    return values.at[tuple(spot)].set(top_value)


def levels(stream_key, shape, split, low, top_value):
    gain = 1.0
    for axis_at, blocks in split:
        heights = jax.random.uniform(jax.random.fold_in(jax.random.fold_in(stream_key, 6), axis_at), (blocks,), jnp.float32, low / len(split), top_value / len(split))
        gain = gain * jnp.repeat(jnp.exp(heights), shape[axis_at] // blocks).reshape((-1,) + (1,) * (len(shape) - 1 - axis_at))
    return gain


def rank_bounds(number_of, slope):
    portions = [(1 << 20) // math.isqrt(grade ** slope) + 1 for grade in range(1, number_of + 1)]
    scale = 1 + sum(portions) // (1 << 30)
    return np.cumsum(np.array([max(1, weight // scale) for weight in portions]))


def skewed_ids(key, shape, count, lean):
    listing = rank_bounds(count, lean)
    pick = jax.random.randint(jax.random.fold_in(key, 1), shape, 0, int(listing[count - 1]))
    standing = jnp.searchsorted(jnp.asarray(listing, jnp.int32), pick, side="right")
    return jax.random.permutation(jax.random.fold_in(key, 2), count)[standing].astype(jnp.int32)


def gaussian(own_key, shape, scale, reach, shards=(), held_as=jnp.bfloat16):
    factor_of = levels(own_key, shape, shards, -0.22, 0.18) if shards else 1.0
    array = jax.random.normal(own_key, shape, jnp.float32) * scale * factor_of
    return jnp.minimum(jnp.maximum(array, -reach), reach).astype(held_as)


def setup_inputs(seed: int = 0) -> dict:
    key_list = jax.random.split(jax.random.key(seed), 4)
    return {
        "velocity": gaussian(key_list[0], (SNAPS, 2, HEIGHT, IMG_W), 8.0, 48.0, ((0, 2), (2, 64)), jnp.float32),
        "offsets": set_ends(jax.random.randint(key_list[1], (SNAPS, 2), 0 - MAXS, MAXS + 1), jax.random.fold_in(key_list[1], 1), 0 - MAXS, MAXS).astype(jnp.int32),
        "phase": set_ends(skewed_ids(key_list[2], (SNAPS,), PHASES, 2), jax.random.fold_in(key_list[2], 3), 0, PHASES - 1).astype(jnp.int32),
    }


def gauss_weights():
    steps = jnp.arange(2 * RAD + 1, dtype=jnp.float32) - RAD
    sigma = RAD / 2.0
    values = jnp.exp(-steps * steps / (2.0 * sigma * sigma))
    return values / jnp.sum(values)


def smooth_one(padded, shift_rows, shift_cols, first_row, out_rows, total_rows, weights):
    comps = padded.shape[0]
    width = padded.shape[2] - 2 * HALO
    start_r = (HALO - RAD + shift_rows).astype(jnp.int32)
    start_c = (HALO - RAD + shift_cols).astype(jnp.int32)
    window = lax.dynamic_slice(padded, (jnp.int32(0), start_r, start_c), (comps, out_rows + 2 * RAD, width + 2 * RAD))
    rows = first_row - RAD + jnp.arange(out_rows + 2 * RAD, dtype=jnp.int32)
    cols = jnp.arange(width + 2 * RAD, dtype=jnp.int32) - RAD
    row_ok = ((rows >= 0) & (rows < total_rows)).astype(window.dtype)
    col_ok = ((cols >= 0) & (cols < width)).astype(window.dtype)
    window = window * row_ok[None, :, None] * col_ok[None, None, :]
    vert = weights[0] * window[:, 0:out_rows, :]
    for tap in range(1, 2 * RAD + 1):
        vert = vert + weights[tap] * window[:, tap:tap + out_rows, :]
    horiz = weights[0] * vert[:, :, 0:width]
    for tap in range(1, 2 * RAD + 1):
        horiz = horiz + weights[tap] * vert[:, :, tap:tap + width]
    return horiz


def reference(velocity, offsets, phase):
    weights = gauss_weights()
    padded_all = jnp.pad(velocity, ((0, 0), (0, 0), (HALO, HALO), (HALO, HALO)))
    total_rows = velocity.shape[2]

    def one_block(block):
        first = (block * ROWS_DEV).astype(jnp.int32)
        slab = lax.dynamic_slice_in_dim(padded_all, first, ROWS_DEV + 2 * HALO, 2)
        smooth = jax.vmap(lambda pad_one, dy, dx: smooth_one(pad_one, dy, dx, first, ROWS_DEV, total_rows, weights))(slab, offsets[:, 0], offsets[:, 1])
        fields = jnp.concatenate([smooth, smooth[:, 0:1] * smooth[:, 0:1], smooth[:, 1:2] * smooth[:, 1:2], smooth[:, 0:1] * smooth[:, 1:2]], axis=1)
        return jax.ops.segment_sum(fields, phase, PHASES)

    blocks = lax.map(one_block, jnp.arange(N_TILE, dtype=jnp.int32))
    sums = jnp.transpose(blocks, (1, 2, 0, 3, 4)).reshape(PHASES, 5, total_rows, velocity.shape[3])
    count = jax.ops.segment_sum(jnp.ones(phase.shape, jnp.float32), phase, PHASES)
    scale = 1.0 / jnp.maximum(count, 1.0)
    phase_mean = sums[:, 0:2] * scale[:, None, None, None]
    phase_moment = sums[:, 2:5] * scale[:, None, None, None]
    return (phase_mean, phase_moment)
```

```python
import functools

import jax
import jax.numpy as jnp
import numpy as np
from jax import lax
from jax.experimental import pallas as pl
from jax.experimental.pallas import tpu as pltpu
from jax.sharding import PartitionSpec as P

PHASES = 72
HALF = PHASES // 2
RAD = 8
MAXS = 16
HALO = RAD + MAXS
ROWS = 64
WIDTH = 256
SNAPS = 128
EXT = ROWS + 2 * HALO
STEP = 4
GAP = 16
VMEM_BYTES = 56 * 1024 * 1024
FIRST = 32
FIRST_CUTS = (480,)
REST_CUTS = (608, 1016, 1184)
F32 = jnp.float32
BF16 = jnp.bfloat16
I32 = jnp.int32


def taps():
    steps = np.arange(2 * RAD + 1, dtype=np.float64) - RAD
    sigma = RAD / 2.0
    values = np.exp(-steps * steps / (2.0 * sigma * sigma))
    return values / values.sum()


def split_const(values):
    high = values.astype(BF16)
    low = (values - high.astype(np.float64)).astype(BF16)
    return high, low


def column_constant():
    weight = taps()
    source = np.arange(WIDTH)[:, None]
    target = np.arange(WIDTH)[None, :]
    distance = source - target
    band = np.where(np.abs(distance) <= RAD, weight[np.clip(distance + RAD, 0, 2 * RAD)], 0.0)
    return np.stack(split_const(band))


def row_constant():
    weight = taps()
    target = np.arange(EXT)[None, :, None] - HALO
    source = np.arange(ROWS)[None, None, :]
    shift = np.arange(-MAXS, MAXS + 1)[:, None, None]
    distance = source - shift - target
    band = np.where(np.abs(distance) <= RAD, weight[np.clip(distance + RAD, 0, 2 * RAD)], 0.0)
    seen = source - shift
    kinds = []
    for kind in range(3):
        keep = np.ones_like(seen, dtype=bool)
        if kind == 0:
            keep = seen >= 0
        if kind == 2:
            keep = seen < ROWS
        high, low = split_const(np.where(keep, band, 0.0))
        kinds.append(np.concatenate([high, low, high], axis=2))
    return np.stack(kinds)


def level_rows(need, level):
    return jnp.clip(need - 8 * level, 0, 8)


def needs(dy):
    return jnp.clip(RAD + dy, 0, HALO), jnp.clip(RAD - dy, 0, HALO)


def next_start(end):
    return end // 8 * 8 + 16


def split(value):
    high = value.astype(BF16)
    return high, (value - high.astype(F32)).astype(BF16)


def smooth_kernel(first, count, cuts, step, meta, vel, colop, rowop, *refs):
    pieces = len(cuts)
    y_refs, refs = refs[:3], refs[3:]
    out_up, out_dn = refs[:pieces], refs[pieces:2 * pieces]
    pos_ref = refs[2 * pieces]
    acc_out = refs[2 * pieces + 1]
    xs_hi, xs_lo, stack, ext, acc, up, dn, cursor, sem = refs[2 * pieces + 2:]
    at = pl.program_id(0)
    last = pl.num_programs(0) - 1

    @pl.when(at == 0)
    def _():
        def count_rows(n, sums):
            dy = meta[first + n]
            out = list(sums)
            for side, need in enumerate(needs(dy)):
                for level in range(3):
                    out[3 * side + level] += level_rows(need, level)
            return tuple(out)

        sums = lax.fori_loop(0, count, count_rows, (I32(0),) * 6)
        for side in range(2):
            start = I32(0)
            for level in range(3):
                cursor[3 * side + level] = start
                start = next_start(start + sums[3 * side + level])
        acc[...] = jnp.zeros_like(acc)

    lane = lax.broadcasted_iota(I32, (1, WIDTH), 1)
    for b in range(step):
        n = first + at * step + b
        dx = meta[SNAPS + n]
        rolled = pltpu.roll(vel[b].reshape(2 * ROWS, WIDTH), lax.rem(WIDTH - dx, WIDTH), 1)
        moved = lane + dx
        high, low = split(jnp.where((moved >= 0) & (moved < WIDTH), rolled, 0.0))
        xs_hi[2 * ROWS * b:2 * ROWS * (b + 1)] = high
        xs_lo[2 * ROWS * b:2 * ROWS * (b + 1)] = low
    dot = functools.partial(jnp.dot, preferred_element_type=F32)
    for b in range(step):
        part = slice(2 * ROWS * b, 2 * ROWS * (b + 1))
        horizontal = dot(xs_hi[part], colop[0]) + dot(xs_hi[part], colop[1]) + dot(xs_lo[part], colop[0])
        high, low = split(horizontal)
        for comp in range(2):
            rows = slice(ROWS * comp, ROWS * (comp + 1))
            stack[b, comp, 0:ROWS] = high[rows]
            stack[b, comp, ROWS:2 * ROWS] = high[rows]
            stack[b, comp, 2 * ROWS:3 * ROWS] = low[rows]
    for b in range(step):
        n = first + at * step + b
        oper = rowop[0, meta[n] + MAXS]
        for comp in range(2):
            ext[b, comp] = dot(oper, stack[b, comp])
    row = lax.broadcasted_iota(I32, (8, WIDTH), 0)
    for b in range(step):
        local = at * step + b
        n = first + local
        for level in range(3):
            top = HALO + 8 * level
            bottom = HALO + ROWS - 8 - 8 * level
            y_refs[level][b, 0] = ext[b, :, top:top + 8]
            y_refs[level][b, 1] = ext[b, :, bottom:bottom + 8]
        phase = meta[2 * SNAPS + n]
        u = ext[b, 0, 2 * HALO:2 * HALO + 16]
        v = ext[b, 1, 2 * HALO:2 * HALO + 16]
        for at_field, field in enumerate((u, v, u * u, v * v, u * v)):
            acc[phase, at_field, 0] += field[0:8]
            acc[phase, at_field, 1] += field[8:16]
        for side, need in enumerate(needs(meta[n])):
            buffer = (up, dn)[side]
            for level in range(3):
                slot = 3 * side + level
                have = level_rows(need, level)
                pos = cursor[slot]
                cursor[slot] = pos + have
                pos_ref[6 * local + slot] = pos
                skew = lax.rem(pos, 8)
                base = pl.multiple_of(pos - skew, 8)
                source = 16 - 8 * level if side == 0 else HALO + ROWS + 8 * level
                turn = lax.rem(skew + have, 8) if side == 0 else skew
                for comp in range(2):
                    tile = pltpu.roll(ext[b, comp, source:source + 8], turn, 0)
                    old = buffer[comp, pl.ds(base, 8)]
                    buffer[comp, pl.ds(base, 8)] = jnp.where(row < skew, old, tile)
                    buffer[comp, pl.ds(base + 8, 8)] = tile

    @pl.when(at == last)
    def _():
        copies = [pltpu.make_async_copy(acc, acc_out, sem.at[0])]
        low = 0
        for piece, high in enumerate(cuts):
            for side in range(2):
                copies.append(pltpu.make_async_copy(
                    (up, dn)[side].at[:, low:high], (out_up, out_dn)[side][piece], sem.at[1 + 2 * piece + side]))
            low = high
        for copy in copies:
            copy.start()
        for copy in copies:
            copy.wait()


def smooth_part(meta, velocity, colop, rowop, kind_at, first, count, cuts):
    pieces = len(cuts)
    sizes = [high - low for low, high in zip((0,) + cuts[:-1], cuts)]
    any_space = pl.BlockSpec(memory_space=pl.ANY)
    steps = count // STEP
    piece_shapes = [jax.ShapeDtypeStruct((2, size, WIDTH), F32) for size in sizes]
    strip = jax.ShapeDtypeStruct((count, 2, 2, 8, WIDTH), F32)
    room = cuts[-1] + GAP
    out = pl.pallas_call(
        functools.partial(smooth_kernel, first, count, cuts, STEP),
        grid_spec=pltpu.PrefetchScalarGridSpec(
            num_scalar_prefetch=1,
            grid=(steps,),
            in_specs=[
                pl.BlockSpec((STEP, 2, ROWS, WIDTH), lambda i, m: (first // STEP + i, 0, 0, 0)),
                pl.BlockSpec((2, WIDTH, WIDTH), lambda i, m: (0, 0, 0)),
                pl.BlockSpec((1, 2 * MAXS + 1, EXT, 3 * ROWS), lambda i, m: (m[kind_at], 0, 0, 0)),
            ],
            out_specs=[pl.BlockSpec((STEP, 2, 2, 8, WIDTH), lambda i, m: (i, 0, 0, 0, 0))] * 3
            + [any_space] * (2 * pieces)
            + [pl.BlockSpec(memory_space=pltpu.SMEM), any_space],
            scratch_shapes=[
                pltpu.VMEM((STEP * 2 * ROWS, WIDTH), BF16),
                pltpu.VMEM((STEP * 2 * ROWS, WIDTH), BF16),
                pltpu.VMEM((STEP, 2, 3 * ROWS, WIDTH), BF16),
                pltpu.VMEM((STEP, 2, EXT, WIDTH), F32),
                pltpu.VMEM((PHASES, 5, 2, 8, WIDTH), F32),
                pltpu.VMEM((2, room, WIDTH), F32),
                pltpu.VMEM((2, room, WIDTH), F32),
                pltpu.SMEM((8,), I32),
                pltpu.SemaphoreType.DMA((1 + 2 * pieces,)),
            ],
        ),
        out_shape=[strip] * 3 + piece_shapes * 2
        + [jax.ShapeDtypeStruct((count * 6,), I32), jax.ShapeDtypeStruct((PHASES, 5, 2, 8, WIDTH), F32)],
        compiler_params=pltpu.CompilerParams(vmem_limit_bytes=VMEM_BYTES),
        name="smooth_part",
    )(meta, velocity, colop, rowop)
    return out[:3], out[3:3 + pieces], out[3 + pieces:3 + 2 * pieces], out[-2], out[-1]


def finish_kernel(level, parts, meta, *refs):
    count = len(parts)
    pos_refs, refs = refs[:count], refs[count:]
    y_refs, refs = refs[:count], refs[count:]
    piece_refs = []
    for _, _, cuts in parts:
        piece_refs.append((refs[:len(cuts)], refs[len(cuts):2 * len(cuts)]))
        refs = refs[2 * len(cuts):]
    mine, theirs, refs = refs[0], refs[1], refs[2:]
    acc, refs = refs[0], refs[1:]
    y_bufs, refs = refs[:count], refs[count:]
    buffers, refs = [refs[2 * k:2 * k + 2] for k in range(count)], refs[2 * count:]
    sem = refs[0]
    loads = []
    for k, (_, _, cuts) in enumerate(parts):
        loads.append(pltpu.make_async_copy(y_refs[k], y_bufs[k], sem.at[len(loads)]))
        low = 0
        for piece, high in enumerate(cuts):
            for side in range(2):
                loads.append(pltpu.make_async_copy(
                    piece_refs[k][side][piece], buffers[k][side].at[:, low:high], sem.at[len(loads)]))
            low = high
    for copy in loads:
        copy.start()
    acc[...] = jnp.zeros_like(acc)
    for copy in loads:
        copy.wait()
    row = lax.broadcasted_iota(I32, (8, WIDTH), 0)
    for k, (first, size, _) in enumerate(parts):
        def one(local, k=k, first=first):
            n = first + local
            phase = meta[2 * SNAPS + n]
            for place in range(2):
                side = 1 - place
                have = level_rows(needs(meta[n])[side], level)
                pos = pos_refs[k][6 * local + 3 * side + level]
                skew = lax.rem(pos, 8)
                base = pl.multiple_of(pos - skew, 8)
                fields = []
                for comp in range(2):
                    window = buffers[k][side][comp, pl.ds(base, 16)]
                    if place == 0:
                        tile = pltpu.roll(window, lax.rem(16 - skew, 16), 0)[0:8]
                        keep = row < have
                    else:
                        tile = pltpu.roll(window, lax.rem(24 - skew - have, 16), 0)[0:8]
                        keep = row >= 8 - have
                    fields.append(y_bufs[k][local, place, comp] + jnp.where(keep, tile, 0.0))
                u, v = fields
                for at_field, field in enumerate((u, v, u * u, v * v, u * v)):
                    acc[phase, at_field, place] += field

        def several(i, carry, one=one):
            for b in range(4):
                one(4 * i + b)
            return carry

        lax.fori_loop(0, size // 4, several, 0)
    stores = [pltpu.make_async_copy(acc.at[HALF:PHASES], theirs, sem.at[0]),
              pltpu.make_async_copy(acc.at[0:HALF], mine, sem.at[1])]
    for copy in stores:
        copy.start()
    for copy in stores:
        copy.wait()


def finish_level(level, meta, parts):
    any_space = pl.BlockSpec(memory_space=pl.ANY)
    smem = pl.BlockSpec(memory_space=pltpu.SMEM)
    shape = jax.ShapeDtypeStruct((HALF, 5, 2, 8, WIDTH), F32)
    plan = [(first, count, level_cuts(cuts, level)) for first, count, cuts, *_ in parts]
    positions = [part[3] for part in parts]
    strips = [part[4][level] for part in parts]
    packs = [piece for part in parts for side in part[5:7] for piece in side[:len(level_cuts(part[2], level))]]
    scratch = [pltpu.VMEM((PHASES, 5, 2, 8, WIDTH), F32)]
    scratch += [pltpu.VMEM((count, 2, 2, 8, WIDTH), F32) for _, count, _ in plan]
    for _, _, cuts in plan:
        scratch += [pltpu.VMEM((2, cuts[-1] + GAP, WIDTH), F32)] * 2
    scratch.append(pltpu.SemaphoreType.DMA((len(strips) + len(packs) + 2,)))
    return pl.pallas_call(
        functools.partial(finish_kernel, level, plan),
        in_specs=[smem] * (1 + len(positions)) + [any_space] * (len(strips) + len(packs)),
        out_specs=[any_space] * 2,
        out_shape=[shape] * 2,
        scratch_shapes=scratch,
        compiler_params=pltpu.CompilerParams(vmem_limit_bytes=VMEM_BYTES),
        name="finish_level",
    )(meta, *positions, *strips, *packs)


def scale_kernel(block, scale, mine, other, *refs):
    mean, moment = refs[-2:]
    start = pl.program_id(0) * block

    def one(p, carry):
        factor = scale[start + p]
        total = (mine[p, :, 0] + other[p, :, 0]) * factor
        mean[p] = total[0:2]
        moment[p] = total[2:5]
        return carry

    lax.fori_loop(0, block, one, 0)


def scale_level(level, scale, mine, other, before):
    block = 18
    any_space = pl.BlockSpec(memory_space=pl.ANY)
    total = pl.BlockSpec((block, 5, 1, 8, WIDTH), lambda i, side, s: (i, 0, side, 0, 0))

    def place(i, side, s):
        return (i, 0, level + side * (7 - 2 * level), 0)

    return pl.pallas_call(
        functools.partial(scale_kernel, block),
        grid_spec=pltpu.PrefetchScalarGridSpec(
            num_scalar_prefetch=1,
            grid=(HALF // block, 2),
            in_specs=[total, total] + [any_space] * len(before),
            out_specs=[pl.BlockSpec((block, 2, 8, WIDTH), place), pl.BlockSpec((block, 3, 8, WIDTH), place)],
        ),
        out_shape=[jax.ShapeDtypeStruct((HALF, 2, ROWS, WIDTH), F32), jax.ShapeDtypeStruct((HALF, 3, ROWS, WIDTH), F32)],
        input_output_aliases={3: 0, 4: 1} if before else {},
        compiler_params=pltpu.CompilerParams(vmem_limit_bytes=VMEM_BYTES),
        name="scale_level",
    )(scale, mine, other, *before)


def to_partner(value):
    return lax.ppermute(value, "snap", [(0, 1), (1, 0)])


def to_above(value):
    size = lax.axis_size("tile")
    return lax.ppermute(value, "tile", [(i + 1, i) for i in range(size - 1)])


def to_below(value):
    size = lax.axis_size("tile")
    return lax.ppermute(value, "tile", [(i, i + 1) for i in range(size - 1)])


def level_cuts(cuts, level):
    return cuts[:level + 1] if len(cuts) == 3 else cuts


def all_fit(dy, first, cuts, count):
    good = True
    for need in needs(dy[first:first + count]):
        end = I32(0)
        for level in range(3):
            end = next_start(end + jnp.sum(level_rows(need, level)))
            good &= end <= level_cuts(cuts, level)[-1]
    return good


def send(up_pieces, dn_pieces):
    from_below = [to_above(piece) for piece in up_pieces]
    from_above = [to_below(piece) for piece in dn_pieces]
    return from_below, from_above


def per_device(velocity, offsets, phase):
    snap = lax.axis_index("snap")
    tile = lax.axis_index("tile")
    dy, dx = offsets[:, 0].astype(I32), offsets[:, 1].astype(I32)
    turned = lax.rem(phase.astype(I32) + PHASES - HALF * snap, PHASES)
    kind = jnp.where(tile == 0, 0, jnp.where(tile == lax.axis_size("tile") - 1, 2, 1)).astype(I32)
    meta = jnp.concatenate([dy, dx, turned, kind[None]])
    colop = jnp.asarray(column_constant())
    rowop = jnp.asarray(row_constant())
    smooth = functools.partial(smooth_part, meta, velocity, colop, rowop, 3 * SNAPS)

    onehot = (turned[:, None] == jnp.arange(PHASES, dtype=I32)[None, :]).astype(I32)
    own = jnp.sum(onehot, axis=0)
    fits = all_fit(dy, 0, FIRST_CUTS, FIRST) & all_fit(dy, FIRST, REST_CUTS, SNAPS - FIRST)
    message = jnp.concatenate([own[HALF:], fits.astype(I32)[None]])
    reply = to_partner(message)
    scale = 1.0 / jnp.maximum((own[:HALF] + reply[:HALF]).astype(F32), 1.0)
    fits = fits & (reply[HALF] > 0)

    strips_a, up_a, dn_a, pos_a, middle_a = smooth(0, FIRST, FIRST_CUTS)
    below_a, above_a = send(up_a, dn_a)
    strips_b, up_b, dn_b, pos_b, middle_b = smooth(FIRST, SNAPS - FIRST, REST_CUTS)

    def tail(parts, middles, scale):
        mine = sum(middle[:HALF] for middle in middles)
        theirs = sum(middle[HALF:] for middle in middles)
        before = scale_level(3, scale, mine, to_partner(theirs), ())
        for level in range(3):
            mine, theirs = finish_level(level, meta, parts)
            before = scale_level(level, scale, mine, to_partner(theirs), before)
        return tuple(before)

    def fast(scale, middle_a, middle_b, strips_a, pos_a, below_a, above_a, strips_b, pos_b, up_b, dn_b):
        below_b, above_b = send(up_b, dn_b)
        parts = [(0, FIRST, FIRST_CUTS, pos_a, strips_a, below_a, above_a),
                 (FIRST, SNAPS - FIRST, REST_CUTS, pos_b, strips_b, below_b, above_b)]
        return tail(parts, [middle_a, middle_b], scale)

    def full(scale, *_):
        cuts = (HALO * SNAPS + 4 * GAP,)
        strips, up, dn, pos, middle = smooth(0, SNAPS, cuts)
        below, above = send(up, dn)
        return tail([(0, SNAPS, cuts, pos, strips, below, above)], [middle], scale)

    return lax.cond(fits, fast, full, scale, middle_a, middle_b, strips_a, pos_a, below_a, above_a, strips_b, pos_b, up_b, dn_b)


def solution(mesh):
    in_specs = (P("snap", None, "tile", None), P("snap", None), P("snap"))
    out_specs = (P("snap", None, "tile", None), P("snap", None, "tile", None))
    return jax.shard_map(
        per_device, mesh=mesh, in_specs=in_specs, out_specs=out_specs, check_vma=False
    )
```

```python
import functools

import jax
import jax.numpy as jnp
import numpy as np
from jax import lax
from jax.experimental import pallas as pl
from jax.experimental.pallas import tpu as pltpu
from jax.sharding import PartitionSpec as P

PHASES = 72
HALF = PHASES // 2
RAD = 8
MAXS = 16
HALO = RAD + MAXS
ROWS = 64
WIDTH = 256
SNAPS = 128
EXT = ROWS + 2 * HALO
GROUP = 4
FIRST_STEP = 8
REST_STEP = 16
GAP = 16
VMEM_BYTES = 56 * 1024 * 1024
FIRST = 32
FIRST_CUTS = (480,)
REST_CUTS = (608, 1016, 1184)
F32 = jnp.float32
BF16 = jnp.bfloat16
I32 = jnp.int32


def taps():
    steps = np.arange(2 * RAD + 1, dtype=np.float64) - RAD
    sigma = RAD / 2.0
    values = np.exp(-steps * steps / (2.0 * sigma * sigma))
    return values / values.sum()


def split_const(values):
    high = values.astype(BF16)
    low = (values - high.astype(np.float64)).astype(BF16)
    return high, low


def column_constant():
    weight = taps()
    source = np.arange(WIDTH)[:, None]
    target = np.arange(WIDTH)[None, :]
    distance = source - target
    band = np.where(np.abs(distance) <= RAD, weight[np.clip(distance + RAD, 0, 2 * RAD)], 0.0)
    return np.stack(split_const(band))


def row_constant():
    weight = taps()
    target = np.arange(EXT)[None, :, None] - HALO
    source = np.arange(ROWS)[None, None, :]
    shift = np.arange(-MAXS, MAXS + 1)[:, None, None]
    distance = source - shift - target
    band = np.where(np.abs(distance) <= RAD, weight[np.clip(distance + RAD, 0, 2 * RAD)], 0.0)
    seen = source - shift
    kinds = []
    for kind in range(3):
        keep = np.ones_like(seen, dtype=bool)
        if kind == 0:
            keep = seen >= 0
        if kind == 2:
            keep = seen < ROWS
        high, low = split_const(np.where(keep, band, 0.0))
        kinds.append(np.concatenate([high, low, high], axis=2))
    return np.stack(kinds)


def level_rows(need, level):
    return jnp.clip(need - 8 * level, 0, 8)


def needs(dy):
    return jnp.clip(RAD + dy, 0, HALO), jnp.clip(RAD - dy, 0, HALO)


def next_start(end):
    return end // 8 * 8 + 16


def split(value):
    high = value.astype(BF16)
    return high, (value - high.astype(F32)).astype(BF16)


def smooth_kernel(first, count, cuts, step, earlier, meta, *refs):
    pieces = len(cuts)
    vel, colop, rowop, refs = *refs[:3], refs[3:]
    if earlier is not None:
        early_strip, refs = refs[0], refs[1:]
    strips = 3 if earlier is not None else 4
    y_refs, refs = refs[:strips], refs[strips:]
    out_up, out_dn = refs[:pieces], refs[pieces:2 * pieces]
    pos_ref, refs = refs[2 * pieces], refs[2 * pieces + 1:]
    if earlier is not None:
        mine, theirs, early_buf, acc, refs = *refs[:4], refs[4:]
    xs_hi, xs_lo, stack, ext, up, dn, cursor, sem = refs
    at = pl.program_id(0)
    last = pl.num_programs(0) - 1
    row = lax.broadcasted_iota(I32, (8, WIDTH), 0)
    lane = lax.broadcasted_iota(I32, (1, WIDTH), 1)
    dot = functools.partial(jnp.dot, preferred_element_type=F32)

    def add_fields(phase, place, u, v):
        for at_field, field in enumerate((u, v, u * u, v * v, u * v)):
            acc[phase, at_field, place] += field

    @pl.when(at == 0)
    def _():
        def count_rows(n, sums):
            dy = meta[first + n]
            out = list(sums)
            for side, need in enumerate(needs(dy)):
                for level in range(3):
                    out[3 * side + level] += level_rows(need, level)
            return tuple(out)

        sums = lax.fori_loop(0, count, count_rows, (I32(0),) * 6)
        for side in range(2):
            start = I32(0)
            for level in range(3):
                cursor[3 * side + level] = start
                start = next_start(start + sums[3 * side + level])
        if earlier is not None:
            load = pltpu.make_async_copy(early_strip, early_buf, sem.at[0])
            load.start()
            acc[...] = jnp.zeros_like(acc)
            load.wait()

            def one_early(n, carry):
                phase = meta[2 * SNAPS + earlier + n]
                for place in range(2):
                    add_fields(phase, place, early_buf[n, place, 0], early_buf[n, place, 1])
                return carry

            lax.fori_loop(0, first - earlier, one_early, 0)

    def group(g, carry):
        for b in range(GROUP):
            n = first + at * step + GROUP * g + b
            dx = meta[SNAPS + n]
            rolled = pltpu.roll(vel[GROUP * g + b].reshape(2 * ROWS, WIDTH), lax.rem(WIDTH - dx, WIDTH), 1)
            moved = lane + dx
            high, low = split(jnp.where((moved >= 0) & (moved < WIDTH), rolled, 0.0))
            xs_hi[2 * ROWS * b:2 * ROWS * (b + 1)] = high
            xs_lo[2 * ROWS * b:2 * ROWS * (b + 1)] = low
        horizontal = dot(xs_hi[...], colop[0]) + dot(xs_hi[...], colop[1]) + dot(xs_lo[...], colop[0])
        high, low = split(horizontal)
        for b in range(GROUP):
            for comp in range(2):
                rows = slice(ROWS * (2 * b + comp), ROWS * (2 * b + comp + 1))
                stack[b, comp, 0:ROWS] = high[rows]
                stack[b, comp, ROWS:2 * ROWS] = high[rows]
                stack[b, comp, 2 * ROWS:3 * ROWS] = low[rows]
        for b in range(GROUP):
            n = first + at * step + GROUP * g + b
            oper = rowop[0, meta[n] + MAXS]
            for comp in range(2):
                ext[b, comp] = dot(oper, stack[b, comp])
        for b in range(GROUP):
            inner = GROUP * g + b
            local = at * step + inner
            n = first + local
            for level in range(strips):
                top = HALO + 8 * level
                bottom = HALO + ROWS - 8 - 8 * level
                y_refs[level][inner, 0] = ext[b, :, top:top + 8]
                y_refs[level][inner, 1] = ext[b, :, bottom:bottom + 8]
            if earlier is not None:
                phase = meta[2 * SNAPS + n]
                for place in range(2):
                    rows = slice(2 * HALO + 8 * place, 2 * HALO + 8 * place + 8)
                    add_fields(phase, place, ext[b, 0, rows], ext[b, 1, rows])
            for side, need in enumerate(needs(meta[n])):
                buffer = (up, dn)[side]
                for level in range(3):
                    slot = 3 * side + level
                    have = level_rows(need, level)
                    pos = cursor[slot]
                    cursor[slot] = pos + have
                    pos_ref[6 * local + slot] = pos
                    skew = lax.rem(pos, 8)
                    base = pl.multiple_of(pos - skew, 8)
                    source = 16 - 8 * level if side == 0 else HALO + ROWS + 8 * level
                    turn = lax.rem(skew + have, 8) if side == 0 else skew
                    for comp in range(2):
                        tile = pltpu.roll(ext[b, comp, source:source + 8], turn, 0)
                        old = buffer[comp, pl.ds(base, 8)]
                        buffer[comp, pl.ds(base, 8)] = jnp.where(row < skew, old, tile)
                        buffer[comp, pl.ds(base + 8, 8)] = tile
        return carry

    lax.fori_loop(0, step // GROUP, group, 0)

    @pl.when(at == last)
    def _():
        copies = []
        low = 0
        for piece, high in enumerate(cuts):
            for side in range(2):
                copies.append(pltpu.make_async_copy(
                    (up, dn)[side].at[:, low:high], (out_up, out_dn)[side][piece], sem.at[len(copies)]))
            low = high
        if earlier is not None:
            copies.append(pltpu.make_async_copy(acc.at[0:HALF], mine, sem.at[len(copies)]))
            copies.append(pltpu.make_async_copy(acc.at[HALF:PHASES], theirs, sem.at[len(copies)]))
        for copy in copies:
            copy.start()
        for copy in copies:
            copy.wait()


def smooth_part(meta, velocity, colop, rowop, first, count, cuts, step, earlier, early_strip):
    pieces = len(cuts)
    sizes = [high - low for low, high in zip((0,) + cuts[:-1], cuts)]
    any_space = pl.BlockSpec(memory_space=pl.ANY)
    piece_shapes = [jax.ShapeDtypeStruct((2, size, WIDTH), F32) for size in sizes]
    strip = jax.ShapeDtypeStruct((count, 2, 2, 8, WIDTH), F32)
    total = jax.ShapeDtypeStruct((HALF, 5, 2, 8, WIDTH), F32)
    room = cuts[-1] + GAP
    strips = 3 if earlier is not None else 4
    sums = earlier is not None
    sum_scratch = [pltpu.VMEM((max(first - earlier, 1), 2, 2, 8, WIDTH), F32),
                   pltpu.VMEM((PHASES, 5, 2, 8, WIDTH), F32)] if sums else []
    out = pl.pallas_call(
        functools.partial(smooth_kernel, first, count, cuts, step, earlier),
        grid_spec=pltpu.PrefetchScalarGridSpec(
            num_scalar_prefetch=1,
            grid=(count // step,),
            in_specs=[
                pl.BlockSpec((step, 2, ROWS, WIDTH), lambda i, m: (first // step + i, 0, 0, 0)),
                pl.BlockSpec((2, WIDTH, WIDTH), lambda i, m: (0, 0, 0)),
                pl.BlockSpec((1, 2 * MAXS + 1, EXT, 3 * ROWS), lambda i, m: (m[3 * SNAPS], 0, 0, 0)),
            ] + [any_space] * sums,
            out_specs=[pl.BlockSpec((step, 2, 2, 8, WIDTH), lambda i, m: (i, 0, 0, 0, 0))] * strips
            + [any_space] * (2 * pieces)
            + [pl.BlockSpec(memory_space=pltpu.SMEM)] + [any_space] * (2 * sums),
            scratch_shapes=sum_scratch + [
                pltpu.VMEM((GROUP * 2 * ROWS, WIDTH), BF16),
                pltpu.VMEM((GROUP * 2 * ROWS, WIDTH), BF16),
                pltpu.VMEM((GROUP, 2, 3 * ROWS, WIDTH), BF16),
                pltpu.VMEM((GROUP, 2, EXT, WIDTH), F32),
                pltpu.VMEM((2, room, WIDTH), F32),
                pltpu.VMEM((2, room, WIDTH), F32),
                pltpu.SMEM((8,), I32),
                pltpu.SemaphoreType.DMA((2 + 2 * pieces,)),
            ],
        ),
        out_shape=[strip] * strips + piece_shapes * 2
        + [jax.ShapeDtypeStruct((count * 6,), I32)] + [total] * (2 * sums),
        compiler_params=pltpu.CompilerParams(vmem_limit_bytes=VMEM_BYTES),
        name="smooth_part",
    )(meta, velocity, colop, rowop, *([early_strip] if sums else []))
    up, dn = out[strips:strips + pieces], out[strips + pieces:strips + 2 * pieces]
    return out[:strips], up, dn, out[strips + 2 * pieces], out[strips + 2 * pieces + 1:]


def finish_kernel(level, parts, meta, *refs):
    count = len(parts)
    pos_refs, refs = refs[:count], refs[count:]
    y_refs, refs = refs[:count], refs[count:]
    piece_refs = []
    for _, _, cuts in parts:
        piece_refs.append((refs[:len(cuts)], refs[len(cuts):2 * len(cuts)]))
        refs = refs[2 * len(cuts):]
    mine, theirs, refs = refs[0], refs[1], refs[2:]
    acc, refs = refs[0], refs[1:]
    y_bufs, refs = refs[:count], refs[count:]
    buffers, refs = [refs[2 * k:2 * k + 2] for k in range(count)], refs[2 * count:]
    sem = refs[0]
    chunk = 32
    loads, waits = [], []
    for k, (_, size, cuts) in enumerate(parts):
        here = []
        low = 0
        for piece, high in enumerate(cuts):
            for side in range(2):
                here.append((piece_refs[k][side][piece], buffers[k][side].at[:, low:high]))
            low = high
        for start in range(0, size, chunk):
            here.append((y_refs[k].at[start:start + chunk], y_bufs[k].at[start:start + chunk]))
            group = []
            for source, target in here:
                group.append(pltpu.make_async_copy(source, target, sem.at[len(loads)]))
                loads.append(group[-1])
            waits.append((k, start, group))
            here = []
    for copy in loads:
        copy.start()
    acc[...] = jnp.zeros_like(acc)
    row = lax.broadcasted_iota(I32, (8, WIDTH), 0)
    for k, start, group in waits:
        for copy in group:
            copy.wait()

        def one(local, k=k):
            n = parts[k][0] + local
            phase = meta[2 * SNAPS + n]
            for place in range(2):
                side = 1 - place
                have = level_rows(needs(meta[n])[side], level)
                pos = pos_refs[k][6 * local + 3 * side + level]
                skew = lax.rem(pos, 8)
                base = pl.multiple_of(pos - skew, 8)
                fields = []
                for comp in range(2):
                    window = buffers[k][side][comp, pl.ds(base, 16)]
                    if place == 0:
                        tile = pltpu.roll(window, lax.rem(16 - skew, 16), 0)[0:8]
                        keep = row < have
                    else:
                        tile = pltpu.roll(window, lax.rem(24 - skew - have, 16), 0)[0:8]
                        keep = row >= 8 - have
                    fields.append(y_bufs[k][local, place, comp] + jnp.where(keep, tile, 0.0))
                u, v = fields
                for at_field, field in enumerate((u, v, u * u, v * v, u * v)):
                    acc[phase, at_field, place] += field

        def several(i, carry, one=one, start=start):
            for b in range(4):
                one(start + 4 * i + b)
            return carry

        lax.fori_loop(0, chunk // 4, several, 0)
    stores = [pltpu.make_async_copy(acc.at[HALF:PHASES], theirs, sem.at[0]),
              pltpu.make_async_copy(acc.at[0:HALF], mine, sem.at[1])]
    for copy in stores:
        copy.start()
    for copy in stores:
        copy.wait()


def finish_level(level, meta, parts):
    any_space = pl.BlockSpec(memory_space=pl.ANY)
    smem = pl.BlockSpec(memory_space=pltpu.SMEM)
    shape = jax.ShapeDtypeStruct((HALF, 5, 2, 8, WIDTH), F32)
    plan = [(first, count, level_cuts(cuts, level)) for first, count, cuts, *_ in parts]
    positions = [part[3] for part in parts]
    strips = [part[4][level] for part in parts]
    packs = [piece for part in parts for side in part[5:7] for piece in side[:len(level_cuts(part[2], level))]]
    scratch = [pltpu.VMEM((PHASES, 5, 2, 8, WIDTH), F32)]
    scratch += [pltpu.VMEM((count, 2, 2, 8, WIDTH), F32) for _, count, _ in plan]
    for _, _, cuts in plan:
        scratch += [pltpu.VMEM((2, cuts[-1] + GAP, WIDTH), F32)] * 2
    scratch.append(pltpu.SemaphoreType.DMA((SNAPS // 32 + len(packs) + 2,)))
    return pl.pallas_call(
        functools.partial(finish_kernel, level, plan),
        in_specs=[smem] * (1 + len(positions)) + [any_space] * (len(strips) + len(packs)),
        out_specs=[any_space] * 2,
        out_shape=[shape] * 2,
        scratch_shapes=scratch,
        compiler_params=pltpu.CompilerParams(vmem_limit_bytes=VMEM_BYTES),
        name="finish_level",
    )(meta, *positions, *strips, *packs)


def scale_kernel(block, scale, mine, other, *refs):
    mean, moment = refs[-2:]
    start = pl.program_id(0) * block

    def one(p, carry):
        factor = scale[start + p]
        total = (mine[p, :, 0] + other[p, :, 0]) * factor
        mean[p] = total[0:2]
        moment[p] = total[2:5]
        return carry

    lax.fori_loop(0, block, one, 0)


def scale_level(level, scale, mine, other, before):
    block = 6
    any_space = pl.BlockSpec(memory_space=pl.ANY)
    total = pl.BlockSpec((block, 5, 1, 8, WIDTH), lambda i, side, s: (i, 0, side, 0, 0))

    def place(i, side, s):
        return (i, 0, level + side * (7 - 2 * level), 0)

    return pl.pallas_call(
        functools.partial(scale_kernel, block),
        grid_spec=pltpu.PrefetchScalarGridSpec(
            num_scalar_prefetch=1,
            grid=(HALF // block, 2),
            in_specs=[total, total] + [any_space] * len(before),
            out_specs=[pl.BlockSpec((block, 2, 8, WIDTH), place), pl.BlockSpec((block, 3, 8, WIDTH), place)],
        ),
        out_shape=[jax.ShapeDtypeStruct((HALF, 2, ROWS, WIDTH), F32), jax.ShapeDtypeStruct((HALF, 3, ROWS, WIDTH), F32)],
        input_output_aliases={3: 0, 4: 1} if before else {},
        compiler_params=pltpu.CompilerParams(vmem_limit_bytes=VMEM_BYTES),
        name="scale_level",
    )(scale, mine, other, *before)


def to_partner(value):
    return lax.ppermute(value, "snap", [(0, 1), (1, 0)])


def to_above(value):
    size = lax.axis_size("tile")
    return lax.ppermute(value, "tile", [(i + 1, i) for i in range(size - 1)])


def to_below(value):
    size = lax.axis_size("tile")
    return lax.ppermute(value, "tile", [(i, i + 1) for i in range(size - 1)])


def level_cuts(cuts, level):
    return cuts[:level + 1] if len(cuts) == 3 else cuts


def excess(dy, first, cuts, count):
    need = jnp.stack(needs(dy[first:first + count]))
    over = []
    end = jnp.zeros((2,), I32)
    for level in range(3):
        end = next_start(end + jnp.sum(level_rows(need, level), axis=1))
        over.append(end - level_cuts(cuts, level)[-1])
    return jnp.concatenate(over)


def send(up_pieces, dn_pieces):
    from_below = [to_above(piece) for piece in up_pieces]
    from_above = [to_below(piece) for piece in dn_pieces]
    return from_below, from_above


def per_device(velocity, offsets, phase):
    snap = lax.axis_index("snap")
    tile = lax.axis_index("tile")
    dy, dx = offsets[:, 0].astype(I32), offsets[:, 1].astype(I32)
    turned = lax.rem(phase.astype(I32) + PHASES - HALF * snap, PHASES)
    kind = jnp.where(tile == 0, 0, jnp.where(tile == lax.axis_size("tile") - 1, 2, 1)).astype(I32)
    meta = jnp.concatenate([dy, dx, turned, kind[None]])
    colop = jnp.asarray(column_constant())
    rowop = jnp.asarray(row_constant())
    smooth = functools.partial(smooth_part, meta, velocity, colop, rowop)
    strips_a, up_a, dn_a, pos_a, _ = smooth(0, FIRST, FIRST_CUTS, FIRST_STEP, None, None)
    below_a, above_a = send(up_a, dn_a)

    onehot = (turned[:, None] == jnp.arange(PHASES, dtype=I32)[None, :]).astype(I32)
    own = jnp.sum(onehot, axis=0)
    over = jnp.max(jnp.concatenate([excess(dy, 0, FIRST_CUTS, FIRST), excess(dy, FIRST, REST_CUTS, SNAPS - FIRST)]))
    message = jnp.concatenate([own, jnp.full((8,), over, I32)])
    reply = to_partner(message)
    scale = 1.0 / jnp.maximum((message[:HALF] + reply[HALF:PHASES]).astype(F32), 1.0)
    over = jnp.max(jnp.maximum(message[PHASES:], reply[PHASES:]))

    strips_b, up_b, dn_b, pos_b, sums_b = smooth(FIRST, SNAPS - FIRST, REST_CUTS, REST_STEP, 0, strips_a[3])

    def tail(parts, sums, scale):
        before, waiting = (), [(3, sums[0], to_partner(sums[1]))]
        here = meta
        for level in range(3):
            if level:
                at, mine, other = waiting.pop(0)
                before = scale_level(at, scale, mine, other, before)
                here, before = lax.optimization_barrier((here, before))
            mine, theirs = finish_level(level, here, parts)
            waiting.append((level, mine, to_partner(theirs)))
        for at, mine, other in waiting:
            before = scale_level(at, scale, mine, other, before)
        return tuple(before)

    def fast(scale, sums_b, strips_a, pos_a, below_a, above_a, strips_b, pos_b, up_b, dn_b):
        below_b, above_b = send(up_b, dn_b)
        parts = [(0, FIRST, FIRST_CUTS, pos_a, strips_a, below_a, above_a),
                 (FIRST, SNAPS - FIRST, REST_CUTS, pos_b, strips_b, below_b, above_b)]
        return tail(parts, sums_b, scale)

    def full(scale, *_):
        cuts = (HALO * SNAPS + 4 * GAP,)
        empty = jnp.zeros((1, 2, 2, 8, WIDTH), F32)
        strips, up, dn, pos, sums = smooth(0, SNAPS, cuts, FIRST_STEP, 0, empty)
        below, above = send(up, dn)
        return tail([(0, SNAPS, cuts, pos, strips, below, above)], sums, scale)

    return lax.cond(over <= 0, fast, full, scale, sums_b, strips_a, pos_a, below_a, above_a, strips_b, pos_b, up_b, dn_b)


def solution(mesh):
    in_specs = (P("snap", None, "tile", None), P("snap", None), P("snap"))
    out_specs = (P("snap", None, "tile", None), P("snap", None, "tile", None))
    return jax.shard_map(
        per_device, mesh=mesh, in_specs=in_specs, out_specs=out_specs, check_vma=False
    )
```

```python
import functools

import jax
import jax.numpy as jnp
import numpy as np
from jax import lax
from jax.experimental import pallas as pl
from jax.experimental.pallas import tpu as pltpu
from jax.sharding import PartitionSpec as P

PHASES = 72
HALF = PHASES // 2
RAD = 8
MAXS = 16
HALO = RAD + MAXS
ROWS = 64
WIDTH = 256
SNAPS = 128
EXT = ROWS + 2 * HALO
GROUP = 8
CHUNK = 64
GAP = 16
MIB = 1024 * 1024
FIRST = 32
FIRST_CUTS = (480,)
REST_CUTS = (608, 1016, 1184)
F32 = jnp.float32
BF16 = jnp.bfloat16
I32 = jnp.int32


def taps():
    steps = np.arange(2 * RAD + 1, dtype=np.float64) - RAD
    sigma = RAD / 2.0
    values = np.exp(-steps * steps / (2.0 * sigma * sigma))
    return values / values.sum()


def split_const(values):
    high = values.astype(BF16)
    low = (values - high.astype(np.float64)).astype(BF16)
    return high, low


def column_constant():
    weight = taps()
    source = np.arange(WIDTH)[:, None]
    target = np.arange(WIDTH)[None, :]
    distance = source - target
    band = np.where(np.abs(distance) <= RAD, weight[np.clip(distance + RAD, 0, 2 * RAD)], 0.0)
    return np.stack(split_const(band))


def row_constant():
    weight = taps()
    target = np.arange(EXT)[None, :, None] - HALO
    source = np.arange(ROWS)[None, None, :]
    shift = np.arange(-MAXS, MAXS + 1)[:, None, None]
    distance = source - shift - target
    band = np.where(np.abs(distance) <= RAD, weight[np.clip(distance + RAD, 0, 2 * RAD)], 0.0)
    seen = source - shift
    kinds = []
    for kind in range(3):
        keep = np.ones_like(seen, dtype=bool)
        if kind == 0:
            keep = seen >= 0
        if kind == 2:
            keep = seen < ROWS
        high, low = split_const(np.where(keep, band, 0.0))
        kinds.append(np.concatenate([high, low, high], axis=2))
    return np.stack(kinds)


def level_rows(need, level):
    return jnp.clip(need - 8 * level, 0, 8)


def needs(dy):
    return jnp.clip(RAD + dy, 0, HALO), jnp.clip(RAD - dy, 0, HALO)


def next_start(end):
    return (end & -8) + 16


def split(value):
    high = value.astype(BF16)
    return high, (value - high.astype(F32)).astype(BF16)


def smooth_kernel(first, count, cuts, earlier, meta, *refs):
    pieces = len(cuts)
    groups = count // GROUP
    vel, colop, rowop, refs = *refs[:3], refs[3:]
    if earlier is not None:
        early_strip, refs = refs[0], refs[1:]
    strips = 3 if earlier is not None else 4
    y_refs, refs = refs[:strips], refs[strips:]
    out_up, out_dn = refs[:pieces], refs[pieces:2 * pieces]
    pos_ref, refs = refs[2 * pieces], refs[2 * pieces + 1:]
    if earlier is not None:
        mine, theirs, early_buf, acc, refs = *refs[:4], refs[4:]
    vel_buf, oper_buf, col_buf, refs = *refs[:3], refs[3:]
    y_bufs, refs = refs[:strips], refs[strips:]
    xs_hi, xs_lo, stack, up, dn, cursor, load_sem, store_sem, sem = refs
    row = lax.broadcasted_iota(I32, (8, WIDTH), 0)
    lane = lax.broadcasted_iota(I32, (1, WIDTH), 1)
    dot = functools.partial(jnp.dot, preferred_element_type=F32)

    def load(g):
        return pltpu.make_async_copy(
            vel.at[pl.ds(first + GROUP * g, GROUP)], vel_buf.at[pl.ds(GROUP * g, GROUP)], load_sem.at[g])

    def store(g, level):
        part = pl.ds(GROUP * g, GROUP)
        return pltpu.make_async_copy(y_bufs[level].at[part], y_refs[level].at[part], store_sem.at[g, level])

    def add_fields(phase, place, u, v):
        for at_field, field in enumerate((u, v, u * u, v * v, u * v)):
            acc[phase, at_field, place] += field

    load(0).start()
    tables = [pltpu.make_async_copy(colop, col_buf, sem.at[0]),
              pltpu.make_async_copy(rowop.at[meta[3 * SNAPS]], oper_buf, sem.at[1])]
    for copy in tables:
        copy.start()
    for g in range(1, groups):
        load(g).start()
    if earlier is not None:
        early = pltpu.make_async_copy(early_strip, early_buf, sem.at[2])
        early.start()
        acc[...] = jnp.zeros_like(acc)

    def count_rows(n, sums):
        dy = meta[first + n]
        out = list(sums)
        for side, need in enumerate(needs(dy)):
            for level in range(3):
                out[3 * side + level] += level_rows(need, level)
        return tuple(out)

    sums = lax.fori_loop(0, count, count_rows, (I32(0),) * 6)
    for side in range(2):
        start = I32(0)
        for level in range(3):
            cursor[3 * side + level] = start
            start = next_start(start + sums[3 * side + level])
    if earlier is not None:
        early.wait()

        def one_early(n, carry):
            phase = meta[2 * SNAPS + earlier + n]
            for place in range(2):
                add_fields(phase, place, early_buf[n, place, 0], early_buf[n, place, 1])
            return carry

        lax.fori_loop(0, first - earlier, one_early, 0)
    for copy in tables:
        copy.wait()

    def group(g, carry):
        load(g).wait()
        for b in range(GROUP):
            n = first + GROUP * g + b
            dx = meta[SNAPS + n]
            rolled = pltpu.roll(vel_buf[GROUP * g + b].reshape(2 * ROWS, WIDTH), (WIDTH - dx) & (WIDTH - 1), 1)
            moved = lane + dx
            high, low = split(jnp.where((moved >= 0) & (moved < WIDTH), rolled, 0.0))
            xs_hi[2 * ROWS * b:2 * ROWS * (b + 1)] = high
            xs_lo[2 * ROWS * b:2 * ROWS * (b + 1)] = low
        horizontal = dot(xs_hi[...], col_buf[0]) + dot(xs_hi[...], col_buf[1]) + dot(xs_lo[...], col_buf[0])
        high, low = split(horizontal)
        for b in range(GROUP):
            for comp in range(2):
                rows = slice(ROWS * (2 * b + comp), ROWS * (2 * b + comp + 1))
                stack[b, comp, 0:ROWS] = high[rows]
                stack[b, comp, ROWS:2 * ROWS] = high[rows]
                stack[b, comp, 2 * ROWS:3 * ROWS] = low[rows]
        for b in range(GROUP):
            local = GROUP * g + b
            n = first + local
            oper = oper_buf[meta[n] + MAXS]
            ext = [dot(oper, stack[b, comp]) for comp in range(2)]
            for level in range(strips):
                for comp in range(2):
                    top = HALO + 8 * level
                    bottom = HALO + ROWS - 8 - 8 * level
                    y_bufs[level][local, 0, comp] = ext[comp][top:top + 8]
                    y_bufs[level][local, 1, comp] = ext[comp][bottom:bottom + 8]
            if earlier is not None:
                phase = meta[2 * SNAPS + n]
                for place in range(2):
                    rows = slice(2 * HALO + 8 * place, 2 * HALO + 8 * place + 8)
                    add_fields(phase, place, ext[0][rows], ext[1][rows])
            for side, need in enumerate(needs(meta[n])):
                buffer = (up, dn)[side]
                for level in range(3):
                    slot = 3 * side + level
                    have = level_rows(need, level)
                    pos = cursor[slot]
                    cursor[slot] = pos + have
                    pos_ref[6 * local + slot] = pos
                    skew = pos & 7
                    base = pl.multiple_of(pos - skew, 8)
                    source = 16 - 8 * level if side == 0 else HALO + ROWS + 8 * level
                    turn = (skew + have) & 7 if side == 0 else skew
                    for comp in range(2):
                        tile = pltpu.roll(ext[comp][source:source + 8], turn, 0)
                        old = buffer[comp, pl.ds(base, 8)]
                        buffer[comp, pl.ds(base, 8)] = jnp.where(row < skew, old, tile)
                        buffer[comp, pl.ds(base + 8, 8)] = tile
        for level in range(strips):
            store(g, level).start()
        return carry

    lax.fori_loop(0, groups, group, 0)
    copies = []
    low = 0
    for piece, high in enumerate(cuts):
        for side in range(2):
            copies.append(pltpu.make_async_copy(
                (up, dn)[side].at[:, low:high], (out_up, out_dn)[side][piece], sem.at[3 + len(copies)]))
        low = high
    if earlier is not None:
        copies.append(pltpu.make_async_copy(acc.at[0:HALF], mine, sem.at[3 + len(copies)]))
        copies.append(pltpu.make_async_copy(acc.at[HALF:PHASES], theirs, sem.at[3 + len(copies)]))
    for copy in copies:
        copy.start()
    for g in range(groups):
        for level in range(strips):
            store(g, level).wait()
    for copy in copies:
        copy.wait()


def smooth_part(meta, velocity, colop, rowop, first, count, cuts, earlier, early_strip):
    pieces = len(cuts)
    sizes = [high - low for low, high in zip((0,) + cuts[:-1], cuts)]
    any_space = pl.BlockSpec(memory_space=pl.ANY)
    smem = pl.BlockSpec(memory_space=pltpu.SMEM)
    piece_shapes = [jax.ShapeDtypeStruct((2, size, WIDTH), F32) for size in sizes]
    strip = jax.ShapeDtypeStruct((count, 2, 2, 8, WIDTH), F32)
    total = jax.ShapeDtypeStruct((HALF, 5, 2, 8, WIDTH), F32)
    room = cuts[-1] + GAP
    sums = earlier is not None
    strips = 3 if sums else 4
    sum_scratch = [pltpu.VMEM((max(first - earlier, 1), 2, 2, 8, WIDTH), F32),
                   pltpu.VMEM((PHASES, 5, 2, 8, WIDTH), F32)] if sums else []
    out = pl.pallas_call(
        functools.partial(smooth_kernel, first, count, cuts, earlier),
        in_specs=[smem] + [any_space] * (3 + sums),
        out_specs=[any_space] * (strips + 2 * pieces) + [smem] + [any_space] * (2 * sums),
        scratch_shapes=sum_scratch + [
            pltpu.VMEM((count, 2, ROWS, WIDTH), F32),
            pltpu.VMEM((2 * MAXS + 1, EXT, 3 * ROWS), BF16),
            pltpu.VMEM((2, WIDTH, WIDTH), BF16),
        ] + [pltpu.VMEM((count, 2, 2, 8, WIDTH), F32)] * strips + [
            pltpu.VMEM((GROUP * 2 * ROWS, WIDTH), BF16),
            pltpu.VMEM((GROUP * 2 * ROWS, WIDTH), BF16),
            pltpu.VMEM((GROUP, 2, 3 * ROWS, WIDTH), BF16),
            pltpu.VMEM((2, room, WIDTH), F32),
            pltpu.VMEM((2, room, WIDTH), F32),
            pltpu.SMEM((8,), I32),
            pltpu.SemaphoreType.DMA((count // GROUP,)),
            pltpu.SemaphoreType.DMA((count // GROUP, strips)),
            pltpu.SemaphoreType.DMA((5 + 2 * pieces,)),
        ],
        out_shape=[strip] * strips + piece_shapes * 2
        + [jax.ShapeDtypeStruct((count * 6,), I32)] + [total] * (2 * sums),
        compiler_params=pltpu.CompilerParams(vmem_limit_bytes=(10 + (count + 1) * 3 // 8) * 1024 * 1024),
        name="smooth_part",
    )(meta, velocity, colop, rowop, *([early_strip] if sums else []))
    up, dn = out[strips:strips + pieces], out[strips + pieces:strips + 2 * pieces]
    return out[:strips], up, dn, out[strips + 2 * pieces], out[strips + 2 * pieces + 1:]


def finish_kernel(level, parts, meta, *refs):
    count = len(parts)
    pos_refs, refs = refs[:count], refs[count:]
    y_refs, refs = refs[:count], refs[count:]
    piece_refs = []
    for _, _, cuts in parts:
        piece_refs.append((refs[:len(cuts)], refs[len(cuts):2 * len(cuts)]))
        refs = refs[2 * len(cuts):]
    mine, theirs, refs = refs[0], refs[1], refs[2:]
    acc, refs = refs[0], refs[1:]
    y_bufs, refs = refs[:count], refs[count:]
    buffers, refs = [refs[2 * k:2 * k + 2] for k in range(count)], refs[2 * count:]
    sem = refs[0]
    chunk = 32
    plans = []
    at_sem = 0
    for k, (_, size, cuts) in enumerate(parts):
        here = []
        low = 0
        for piece, high in enumerate(cuts):
            for side in range(2):
                begin = pos_refs[k][3 * side + level]
                end = pos_refs[k][6 * (size - 1) + 3 * side + level] + 16
                for row_at in range(low, high, CHUNK):
                    stop = min(row_at + CHUNK, high)
                    copy = pltpu.make_async_copy(
                        piece_refs[k][side][piece].at[:, row_at - low:stop - low],
                        buffers[k][side].at[:, row_at:stop], sem.at[at_sem])
                    here.append((copy, (begin < stop) & (end > row_at)))
                    at_sem += 1
            low = high
        for start in range(0, size, chunk):
            copy = pltpu.make_async_copy(
                y_refs[k].at[start:start + chunk], y_bufs[k].at[start:start + chunk], sem.at[at_sem])
            at_sem += 1
            plans.append((k, start, here + [(copy, None)]))
            here = []

    def each(group, action):
        for copy, needed in group:
            if needed is None:
                action(copy)
            else:
                pl.when(needed)(functools.partial(action, copy))

    for _, _, group in plans:
        each(group, lambda copy: copy.start())
    acc[...] = jnp.zeros_like(acc)
    row = lax.broadcasted_iota(I32, (8, WIDTH), 0)
    for k, start, group in plans:
        each(group, lambda copy: copy.wait())

        def one(local, k=k):
            n = parts[k][0] + local
            phase = meta[2 * SNAPS + n]
            for place in range(2):
                side = 1 - place
                have = level_rows(needs(meta[n])[side], level)
                pos = pos_refs[k][6 * local + 3 * side + level]
                skew = pos & 7
                base = pl.multiple_of(pos - skew, 8)
                fields = []
                turn = skew if place == 0 else (skew + have) & 7
                keep = row < have if place == 0 else row >= 8 - have
                for comp in range(2):
                    lower = buffers[k][side][comp, pl.ds(base, 8)]
                    upper = buffers[k][side][comp, pl.ds(base + 8, 8)]
                    tile = pltpu.roll(jnp.where(row >= skew, lower, upper), (8 - turn) & 7, 0)
                    fields.append(y_bufs[k][local, place, comp] + jnp.where(keep, tile, 0.0))
                u, v = fields
                for at_field, field in enumerate((u, v, u * u, v * v, u * v)):
                    acc[phase, at_field, place] += field

        def several(i, carry, one=one, start=start):
            for b in range(4):
                one(start + 4 * i + b)
            return carry

        lax.fori_loop(0, chunk // 4, several, 0)
    stores = [pltpu.make_async_copy(acc.at[HALF:PHASES], theirs, sem.at[0]),
              pltpu.make_async_copy(acc.at[0:HALF], mine, sem.at[1])]
    for copy in stores:
        copy.start()
    for copy in stores:
        copy.wait()


def finish_level(level, meta, parts):
    any_space = pl.BlockSpec(memory_space=pl.ANY)
    smem = pl.BlockSpec(memory_space=pltpu.SMEM)
    shape = jax.ShapeDtypeStruct((HALF, 5, 2, 8, WIDTH), F32)
    plan = [(first, count, level_cuts(cuts, level)) for first, count, cuts, *_ in parts]
    positions = [part[3] for part in parts]
    strips = [part[4][level] for part in parts]
    packs = [piece for part in parts for side in part[5:7] for piece in side[:len(level_cuts(part[2], level))]]
    scratch = [pltpu.VMEM((PHASES, 5, 2, 8, WIDTH), F32)]
    scratch += [pltpu.VMEM((count, 2, 2, 8, WIDTH), F32) for _, count, _ in plan]
    for _, _, cuts in plan:
        scratch += [pltpu.VMEM((2, cuts[-1] + GAP, WIDTH), F32)] * 2
    chunks = sum(2 * (-(-(high - low) // CHUNK)) for _, _, cuts in plan for low, high in zip((0,) + cuts[:-1], cuts))
    scratch.append(pltpu.SemaphoreType.DMA((SNAPS // 32 + chunks + 2,)))
    bytes_used = 4 * WIDTH * sum(2 * 2 * (cuts[-1] + GAP) for _, _, cuts in plan)
    return pl.pallas_call(
        functools.partial(finish_kernel, level, plan),
        in_specs=[smem] * (1 + len(positions)) + [any_space] * (len(strips) + len(packs)),
        out_specs=[any_space] * 2,
        out_shape=[shape] * 2,
        scratch_shapes=scratch,
        compiler_params=pltpu.CompilerParams(vmem_limit_bytes=12 * MIB + bytes_used),
        name="finish_level",
    )(meta, *positions, *strips, *packs)


def scale_kernel(level, block, scale, mine, other, *refs):
    mean, moment, a_buf, b_buf, mean_buf, moment_buf, sem = refs[-7:]
    count = HALF // block
    loads, stores = [], []
    for k in range(count):
        part = slice(block * k, block * (k + 1))
        loads.append([pltpu.make_async_copy(mine.at[part], a_buf.at[part], sem.at[2 * k]),
                      pltpu.make_async_copy(other.at[part], b_buf.at[part], sem.at[2 * k + 1])])
        group = []
        for place in range(2):
            rows = slice(8 * level, 8 * level + 8) if place == 0 else slice(ROWS - 8 - 8 * level, ROWS - 8 * level)
            for which, (buf, out) in enumerate(((mean_buf, mean), (moment_buf, moment))):
                group.append(pltpu.make_async_copy(
                    buf.at[place, part], out.at[part, :, rows], sem.at[2 * count + 4 * k + 2 * place + which]))
        stores.append(group)
    for copies in loads:
        for copy in copies:
            copy.start()
    for k in range(count):
        for copy in loads[k]:
            copy.wait()

        def one(p, carry):
            factor = scale[p]
            for place in range(2):
                total = (a_buf[p, :, place] + b_buf[p, :, place]) * factor
                mean_buf[place, p] = total[0:2]
                moment_buf[place, p] = total[2:5]
            return carry

        lax.fori_loop(block * k, block * (k + 1), one, 0)
        for copy in stores[k]:
            copy.start()
    for copies in stores:
        for copy in copies:
            copy.wait()


def scale_level(level, scale, mine, other, before):
    block = 18
    count = HALF // block
    any_space = pl.BlockSpec(memory_space=pl.ANY)
    return pl.pallas_call(
        functools.partial(scale_kernel, level, block),
        in_specs=[pl.BlockSpec(memory_space=pltpu.SMEM)] + [any_space] * (2 + len(before)),
        out_specs=[pl.BlockSpec(memory_space=pltpu.HBM)] * 2,
        out_shape=[jax.ShapeDtypeStruct((HALF, 2, ROWS, WIDTH), F32), jax.ShapeDtypeStruct((HALF, 3, ROWS, WIDTH), F32)],
        scratch_shapes=[
            pltpu.VMEM((HALF, 5, 2, 8, WIDTH), F32),
            pltpu.VMEM((HALF, 5, 2, 8, WIDTH), F32),
            pltpu.VMEM((2, HALF, 2, 8, WIDTH), F32),
            pltpu.VMEM((2, HALF, 3, 8, WIDTH), F32),
            pltpu.SemaphoreType.DMA((6 * count,)),
        ],
        input_output_aliases={3: 0, 4: 1} if before else {},
        compiler_params=pltpu.CompilerParams(vmem_limit_bytes=10 * MIB),
        name="scale_level",
    )(scale, mine, other, *before)


def to_partner(value):
    return lax.ppermute(value, "snap", [(0, 1), (1, 0)])


def to_above(value):
    size = lax.axis_size("tile")
    return lax.ppermute(value, "tile", [(i + 1, i) for i in range(size - 1)])


def to_below(value):
    size = lax.axis_size("tile")
    return lax.ppermute(value, "tile", [(i, i + 1) for i in range(size - 1)])


def level_cuts(cuts, level):
    return cuts[:level + 1] if len(cuts) == 3 else cuts


def excess(dy, first, cuts, count):
    need = jnp.stack(needs(dy[first:first + count]))
    over = []
    end = jnp.zeros((2,), I32)
    for level in range(3):
        end = next_start(end + jnp.sum(level_rows(need, level), axis=1))
        over.append(end - level_cuts(cuts, level)[-1])
    return jnp.concatenate(over)


def send(up_pieces, dn_pieces):
    from_below = [to_above(piece) for piece in up_pieces]
    from_above = [to_below(piece) for piece in dn_pieces]
    return from_below, from_above


def per_device(velocity, offsets, phase):
    snap = lax.axis_index("snap")
    tile = lax.axis_index("tile")
    dy, dx = offsets[:, 0].astype(I32), offsets[:, 1].astype(I32)
    turned = lax.rem(phase.astype(I32) + PHASES - HALF * snap, PHASES)
    kind = jnp.where(tile == 0, 0, jnp.where(tile == lax.axis_size("tile") - 1, 2, 1)).astype(I32)
    meta = jnp.concatenate([dy, dx, turned, kind[None]])
    colop = jnp.asarray(column_constant())
    rowop = jnp.asarray(row_constant())
    smooth = functools.partial(smooth_part, meta, velocity, colop, rowop)
    strips_a, up_a, dn_a, pos_a, _ = smooth(0, FIRST, FIRST_CUTS, None, None)
    below_a, above_a = send(up_a, dn_a)

    onehot = (turned[:, None] == jnp.arange(PHASES, dtype=I32)[None, :]).astype(I32)
    own = jnp.sum(onehot, axis=0)
    over = jnp.max(jnp.concatenate([excess(dy, 0, FIRST_CUTS, FIRST), excess(dy, FIRST, REST_CUTS, SNAPS - FIRST)]))
    message = jnp.concatenate([own, jnp.full((8,), over, I32)])
    reply = to_partner(message)
    scale = 1.0 / jnp.maximum((message[:HALF] + reply[HALF:PHASES]).astype(F32), 1.0)
    over = jnp.max(jnp.maximum(message[PHASES:], reply[PHASES:]))

    strips_b, up_b, dn_b, pos_b, sums_b = smooth(FIRST, SNAPS - FIRST, REST_CUTS, 0, strips_a[3])

    def tail(parts, sums, scale):
        before = scale_level(3, scale, sums[0], to_partner(sums[1]), ())
        here, before = lax.optimization_barrier((meta, before))
        waiting = []
        for level in range(3):
            mine, theirs = finish_level(level, here, parts)
            waiting.append((level, mine, to_partner(theirs)))
        for at, mine, other in waiting:
            before = scale_level(at, scale, mine, other, before)
        return tuple(before)

    def fast(scale, sums_b, strips_a, pos_a, below_a, above_a, strips_b, pos_b, up_b, dn_b):
        below_b, above_b = send(up_b, dn_b)
        parts = [(0, FIRST, FIRST_CUTS, pos_a, strips_a, below_a, above_a),
                 (FIRST, SNAPS - FIRST, REST_CUTS, pos_b, strips_b, below_b, above_b)]
        return tail(parts, sums_b, scale)

    def full(scale, *_):
        cuts = (HALO * SNAPS + 4 * GAP,)
        empty = jnp.zeros((1, 2, 2, 8, WIDTH), F32)
        strips, up, dn, pos, sums = smooth(0, SNAPS, cuts, 0, empty)
        below, above = send(up, dn)
        return tail([(0, SNAPS, cuts, pos, strips, below, above)], sums, scale)

    return lax.cond(over <= 0, fast, full, scale, sums_b, strips_a, pos_a, below_a, above_a, strips_b, pos_b, up_b, dn_b)


def solution(mesh):
    in_specs = (P("snap", None, "tile", None), P("snap", None), P("snap"))
    out_specs = (P("snap", None, "tile", None), P("snap", None, "tile", None))
    return jax.shard_map(
        per_device, mesh=mesh, in_specs=in_specs, out_specs=out_specs, check_vma=False
    )
```

```python
import functools

import jax
import jax.numpy as jnp
import numpy as np
from jax import lax
from jax.experimental import pallas as pl
from jax.experimental.pallas import tpu as pltpu
from jax.sharding import PartitionSpec as P

PHASES = 72
HALF = PHASES // 2
RAD = 8
MAXS = 16
HALO = RAD + MAXS
ROWS = 64
WIDTH = 256
SNAPS = 128
EXT = ROWS + 2 * HALO
GROUP = 8
CHUNK = 128
GAP = 16
MIB = 1024 * 1024
FIRST_CUTS = (640,)
REST_CUTS = (512, 984)
FULL_CUTS = (3072 + 64,)
GROUPS = SNAPS // 8
F32 = jnp.float32
BF16 = jnp.bfloat16
I32 = jnp.int32


def taps():
    steps = np.arange(2 * RAD + 1, dtype=np.float64) - RAD
    sigma = RAD / 2.0
    values = np.exp(-steps * steps / (2.0 * sigma * sigma))
    return values / values.sum()


def split_const(values):
    high = values.astype(BF16)
    low = (values - high.astype(np.float64)).astype(BF16)
    return high, low


def column_constant():
    weight = taps()
    source = np.arange(WIDTH)[:, None]
    target = np.arange(WIDTH)[None, :]
    distance = source - target
    band = np.where(np.abs(distance) <= RAD, weight[np.clip(distance + RAD, 0, 2 * RAD)], 0.0)
    high, low = split_const(band)
    return np.concatenate([high, low, high], axis=0)


def row_constant():
    weight = taps()
    target = np.arange(EXT)[None, :, None] - HALO
    source = np.arange(ROWS)[None, None, :]
    shift = np.arange(-MAXS, MAXS + 1)[:, None, None]
    distance = source - shift - target
    band = np.where(np.abs(distance) <= RAD, weight[np.clip(distance + RAD, 0, 2 * RAD)], 0.0)
    seen = source - shift
    kinds = []
    for kind in range(3):
        keep = np.ones_like(seen, dtype=bool)
        if kind == 0:
            keep = seen >= 0
        if kind == 2:
            keep = seen < ROWS
        high, low = split_const(np.where(keep, band, 0.0))
        kinds.append(np.concatenate([high, low, high], axis=2))
    return np.stack(kinds)


def level_rows(need, level):
    return jnp.clip(need - 8 * level, 0, 8)


def needs(dy):
    return jnp.clip(RAD + dy, 0, HALO), jnp.clip(RAD - dy, 0, HALO)


def next_start(end):
    return (end & -8) + 16


def split(value):
    high = value.astype(BF16)
    return high, (value - high.astype(F32)).astype(BF16)


def smooth_kernel(part, cuts, meta, plan, *refs):
    pieces = len(cuts)
    vel, colop, rowop, refs = *refs[:3], refs[3:]
    y_refs, refs = refs[:4], refs[4:]
    out_up, out_dn = refs[:pieces], refs[pieces:2 * pieces]
    pos_ref, plan_ref, refs = *refs[2 * pieces:2 * pieces + 2], refs[2 * pieces + 2:]
    vel_buf, oper_buf, col_buf, refs = *refs[:3], refs[3:]
    y_bufs, refs = refs[:4], refs[4:]
    xs, stack, up, dn, cursor, load_sem, store_sem, sem = refs
    row = lax.broadcasted_iota(I32, (8, WIDTH), 0)
    lane = lax.broadcasted_iota(I32, (1, WIDTH), 1)
    dot = functools.partial(jnp.dot, preferred_element_type=F32)

    def load(g):
        rows = pl.ds(GROUP * g, GROUP)
        return pltpu.make_async_copy(vel.at[rows], vel_buf.at[rows], load_sem.at[g])

    def store(g, level):
        rows = pl.ds(GROUP * g, GROUP)
        return pltpu.make_async_copy(y_bufs[level].at[rows], y_refs[level].at[rows], store_sem.at[g, level])

    def loop(low, high, body):
        lax.fori_loop(low, high, lambda g, carry: (body(g), carry)[1], 0)

    def ends(sums):
        starts, stops = [], []
        for side in range(2):
            start = I32(0)
            for level in range(3):
                starts.append(start)
                start = next_start(start + sums[3 * side + level])
                stops.append(start)
        return starts, stops

    def count_group(g, sums):
        for b in range(GROUP):
            sums = list(sums)
            for side, need in enumerate(needs(meta[GROUP * g + b])):
                for level in range(3):
                    sums[3 * side + level] += level_rows(need, level)
        return tuple(sums)

    tables = [pltpu.make_async_copy(colop, col_buf, sem.at[0]),
              pltpu.make_async_copy(rowop.at[meta[3 * SNAPS]], oper_buf, sem.at[1])]
    zero = (I32(0),) * 6
    if part == 0:
        load(0).start()
        for copy in tables:
            copy.start()
        for g in range(1, 4):
            load(g).start()

        def add_group(g, carry):
            sums, taken, count, going = carry
            sums = count_group(g, sums)
            stops = ends(sums)[1]
            going = going & (jnp.maximum(stops[2], stops[5]) <= cuts[-1]).astype(I32)
            taken = tuple(jnp.where(going > 0, new, old) for new, old in zip(sums, taken))
            return sums, taken, count + going, going

        sums, taken, count, _ = lax.fori_loop(0, GROUPS, add_group, (zero, zero, I32(0), I32(1)))
        begin, end = I32(0), count
        starts = ends(taken)[0]
        rest_starts, rest_stops = ends([whole - some for whole, some in zip(sums, taken)])
        over = I32(0)
        for side in range(2):
            for level in range(3):
                limit = level_cuts(REST_CUTS, level)[-1]
                over = jnp.maximum(over, rest_stops[3 * side + level] - limit)
        for k in range(8):
            plan_ref[k] = rest_starts[k] if k < 6 else count
            plan_ref[8 + k] = over
        loop(4, end, lambda g: load(g).start())
    elif part == 1:
        begin, end = plan[6], I32(GROUPS)
        loop(begin, end, lambda g: load(g).start())
        for copy in tables:
            copy.start()
        starts = [plan[k] for k in range(6)]
    else:
        begin, end = I32(0), I32(GROUPS)
        loop(begin, end, lambda g: load(g).start())
        for copy in tables:
            copy.start()
        starts = ends(lax.fori_loop(0, GROUPS, count_group, zero))[0]
    if part:
        for k in range(16):
            plan_ref[k] = I32(GROUPS)
    for k in range(6):
        cursor[k] = starts[k]
    for copy in tables:
        copy.wait()

    def group(g):
        load(g).wait()
        for b in range(GROUP):
            n = GROUP * g + b
            dx = meta[SNAPS + n]
            rolled = pltpu.roll(vel_buf[n].reshape(2 * ROWS, WIDTH), (WIDTH - dx) & (WIDTH - 1), 1)
            moved = lane + dx
            high, low = split(jnp.where((moved >= 0) & (moved < WIDTH), rolled, 0.0))
            rows = slice(2 * ROWS * b, 2 * ROWS * (b + 1))
            xs[rows, 0:WIDTH] = high
            xs[rows, WIDTH:2 * WIDTH] = high
            xs[rows, 2 * WIDTH:3 * WIDTH] = low
        high, low = split(dot(xs[...], col_buf[...]))
        for b in range(GROUP):
            for comp in range(2):
                rows = slice(ROWS * (2 * b + comp), ROWS * (2 * b + comp + 1))
                stack[b, comp, 0:ROWS] = high[rows]
                stack[b, comp, ROWS:2 * ROWS] = high[rows]
                stack[b, comp, 2 * ROWS:3 * ROWS] = low[rows]
        for b in range(GROUP):
            n = GROUP * g + b
            oper = oper_buf[meta[n] + MAXS]
            ext = [dot(oper, stack[b, comp]) for comp in range(2)]
            for level in range(4):
                for comp in range(2):
                    top = HALO + 8 * level
                    bottom = HALO + ROWS - 8 - 8 * level
                    y_bufs[level][n, 0, comp] = ext[comp][top:top + 8]
                    y_bufs[level][n, 1, comp] = ext[comp][bottom:bottom + 8]
            for side, need in enumerate(needs(meta[n])):
                buffer = (up, dn)[side]
                for level in range(3):
                    slot = 3 * side + level
                    have = level_rows(need, level)
                    here = cursor[slot]
                    cursor[slot] = here + have
                    pos = jnp.minimum(here, cuts[-1] - 16)
                    pos_ref[6 * n + slot] = pos
                    skew = pos & 7
                    base = pl.multiple_of(pos - skew, 8)
                    source = 16 - 8 * level if side == 0 else HALO + ROWS + 8 * level
                    turn = (skew + have) & 7 if side == 0 else skew
                    for comp in range(2):
                        tile = pltpu.roll(ext[comp][source:source + 8], turn, 0)
                        old = buffer[comp, pl.ds(base, 8)]
                        buffer[comp, pl.ds(base, 8)] = jnp.where(row < skew, old, tile)
                        buffer[comp, pl.ds(base + 8, 8)] = tile
        for level in range(4):
            store(g, level).start()

    loop(begin, end, group)
    copies = []
    low = 0
    for piece, high in enumerate(cuts):
        for side in range(2):
            copies.append(pltpu.make_async_copy(
                (up, dn)[side].at[:, low:high], (out_up, out_dn)[side][piece], sem.at[2 + len(copies)]))
        low = high
    for copy in copies:
        copy.start()
    if part == 0:
        for g in range(4):
            pl.when(g >= end)(load(g).wait)

    def stored(g):
        for level in range(4):
            store(g, level).wait()

    loop(begin, end, stored)
    for copy in copies:
        copy.wait()


def smooth_part(part, meta, plan, velocity, colop, rowop, cuts):
    pieces = len(cuts)
    sizes = [high - low for low, high in zip((0,) + cuts[:-1], cuts)]
    any_space = pl.BlockSpec(memory_space=pl.ANY)
    smem = pl.BlockSpec(memory_space=pltpu.SMEM)
    piece_shapes = [jax.ShapeDtypeStruct((2, size, WIDTH), F32) for size in sizes]
    strip = jax.ShapeDtypeStruct((SNAPS, 2, 2, 8, WIDTH), F32)
    room = cuts[-1] + GAP
    out = pl.pallas_call(
        functools.partial(smooth_kernel, part, cuts),
        in_specs=[smem] * 2 + [any_space] * 3,
        out_specs=[any_space] * (4 + 2 * pieces) + [smem, smem],
        scratch_shapes=[
            pltpu.VMEM((SNAPS, 2, ROWS, WIDTH), F32),
            pltpu.VMEM((2 * MAXS + 1, EXT, 3 * ROWS), BF16),
            pltpu.VMEM((3 * WIDTH, WIDTH), BF16),
        ] + [pltpu.VMEM((SNAPS, 2, 2, 8, WIDTH), F32)] * 4 + [
            pltpu.VMEM((GROUP * 2 * ROWS, 3 * WIDTH), BF16),
            pltpu.VMEM((GROUP, 2, 3 * ROWS, WIDTH), BF16),
            pltpu.VMEM((2, room, WIDTH), F32),
            pltpu.VMEM((2, room, WIDTH), F32),
            pltpu.SMEM((8,), I32),
            pltpu.SemaphoreType.DMA((GROUPS,)),
            pltpu.SemaphoreType.DMA((GROUPS, 4)),
            pltpu.SemaphoreType.DMA((2 + 2 * pieces,)),
        ],
        out_shape=[strip] * 4 + piece_shapes * 2
        + [jax.ShapeDtypeStruct((SNAPS * 6,), I32), jax.ShapeDtypeStruct((16,), I32)],
        compiler_params=pltpu.CompilerParams(vmem_limit_bytes=56 * MIB),
        name="smooth_part",
    )(meta, plan, velocity, colop, rowop)
    return out[:4], out[4:4 + pieces], out[4 + pieces:4 + 2 * pieces], out[-2], out[-1]


def finish_kernel(level, cuts, meta, plan, *refs):
    parts = len(cuts)
    pos_refs, strips, refs = refs[:parts], refs[parts:2 * parts], refs[2 * parts:]
    pieces = []
    for k in range(parts):
        many = len(cuts[k])
        pieces.append((refs[:many], refs[many:2 * many]))
        refs = refs[2 * many:]
    mine, theirs, acc, y_buf, *refs = refs
    buffers, (y_sem, sem) = refs[:-2], refs[-2:]
    middle = plan[6] if parts == 2 else I32(GROUPS)
    ranges = [(I32(0), middle), (middle, I32(GROUPS))][:parts]

    def loop(low, high, body):
        lax.fori_loop(low, high, lambda g, carry: (body(g), carry)[1], 0)

    def load(k, g):
        rows = pl.ds(GROUP * g, GROUP)
        return pltpu.make_async_copy(strips[k].at[rows], y_buf.at[rows], y_sem.at[g])

    packs = [[] for _ in range(parts)]
    total = 0
    for k in range(parts):
        low = 0
        first, last = ranges[k]
        for piece, high in enumerate(cuts[k]):
            for side in range(2):
                slot = 3 * side + level
                begin = pos_refs[k][6 * GROUP * jnp.minimum(first, GROUPS - 1) + slot]
                end = pos_refs[k][6 * (GROUP * jnp.maximum(last, 1) - 1) + slot] + 16
                for row_at in range(low, high, CHUNK):
                    stop = min(row_at + CHUNK, high)
                    copy = pltpu.make_async_copy(
                        pieces[k][side][piece].at[:, row_at - low:stop - low],
                        buffers[2 * k + side].at[:, row_at:stop], sem.at[total])
                    total += 1
                    packs[k].append((copy, (first < last) & (begin < stop) & (end > row_at)))
            low = high
    for k in range(parts):
        for copy, needed in packs[k]:
            pl.when(needed)(copy.start)
        loop(*ranges[k], lambda g, k=k: load(k, g).start())
    acc[...] = jnp.zeros_like(acc)
    row = lax.broadcasted_iota(I32, (8, WIDTH), 0)

    def one(n, k):
        phase = meta[2 * SNAPS + n]
        for place in range(2):
            fields = [y_buf[n, place, comp] for comp in range(2)]
            if cuts[k]:
                side = 1 - place
                have = level_rows(needs(meta[n])[side], level)
                pos = pos_refs[k][6 * n + 3 * side + level]
                skew = pos & 7
                base = pl.multiple_of(pos - skew, 8)
                turn = skew if place == 0 else (skew + have) & 7
                keep = row < have if place == 0 else row >= 8 - have
                for comp in range(2):
                    lower = buffers[2 * k + side][comp, pl.ds(base, 8)]
                    upper = buffers[2 * k + side][comp, pl.ds(base + 8, 8)]
                    tile = pltpu.roll(jnp.where(row >= skew, lower, upper), (8 - turn) & 7, 0)
                    fields[comp] += jnp.where(keep, tile, 0.0)
            u, v = fields
            for at_field, field in enumerate((u, v, u * u, v * v, u * v)):
                acc[phase, at_field, place] += field

    def group(g, k):
        load(k, g).wait()
        for b in range(GROUP):
            one(GROUP * g + b, k)

    for k in range(parts):
        for copy, needed in packs[k]:
            pl.when(needed)(copy.wait)
        loop(*ranges[k], lambda g, k=k: group(g, k))
    stores = [pltpu.make_async_copy(acc.at[HALF:PHASES], theirs, y_sem.at[0]),
              pltpu.make_async_copy(acc.at[0:HALF], mine, y_sem.at[1])]
    for copy in stores:
        copy.start()
    for copy in stores:
        copy.wait()


def finish_level(level, meta, plan, parts):
    any_space = pl.BlockSpec(memory_space=pl.ANY)
    smem = pl.BlockSpec(memory_space=pltpu.SMEM)
    shape = jax.ShapeDtypeStruct((HALF, 5, 2, 8, WIDTH), F32)
    cuts = [level_cuts(part[2], level) if level < 3 else () for part in parts]
    packs = [piece for part, some in zip(parts, cuts) for side in part[3:5] for piece in side[:len(some)]]
    chunks = sum(2 * (-(-(high - low) // CHUNK)) for some in cuts for low, high in zip((0,) + some[:-1], some))
    rooms = [some[-1] + GAP for some in cuts if some]
    return pl.pallas_call(
        functools.partial(finish_kernel, level, cuts),
        in_specs=[smem] * (2 + len(parts)) + [any_space] * (len(parts) + len(packs)),
        out_specs=[any_space] * 2,
        out_shape=[shape] * 2,
        scratch_shapes=[
            pltpu.VMEM((PHASES, 5, 2, 8, WIDTH), F32),
            pltpu.VMEM((SNAPS, 2, 2, 8, WIDTH), F32),
        ] + [pltpu.VMEM((2, room, WIDTH), F32) for room in rooms for _ in range(2)] + [
            pltpu.SemaphoreType.DMA((GROUPS,)),
            pltpu.SemaphoreType.DMA((max(chunks, 1),)),
        ],
        compiler_params=pltpu.CompilerParams(vmem_limit_bytes=12 * MIB + 16 * WIDTH * sum(rooms)),
        name="finish_level",
    )(meta, plan, *[part[0] for part in parts], *[part[1][level] for part in parts], *packs)


def scale_kernel(level, block, scale, mine, other, *refs):
    mean, moment, a_buf, b_buf, mean_buf, moment_buf, sem = refs[-7:]
    count = HALF // block
    loads, stores = [], []
    for k in range(count):
        part = slice(block * k, block * (k + 1))
        loads.append([pltpu.make_async_copy(mine.at[part], a_buf.at[part], sem.at[2 * k]),
                      pltpu.make_async_copy(other.at[part], b_buf.at[part], sem.at[2 * k + 1])])
        group = []
        for place in range(2):
            rows = slice(8 * level, 8 * level + 8) if place == 0 else slice(ROWS - 8 - 8 * level, ROWS - 8 * level)
            for which, (buf, out) in enumerate(((mean_buf, mean), (moment_buf, moment))):
                group.append(pltpu.make_async_copy(
                    buf.at[place, part], out.at[part, :, rows], sem.at[2 * count + 4 * k + 2 * place + which]))
        stores.append(group)
    for copies in loads:
        for copy in copies:
            copy.start()
    for k in range(count):
        for copy in loads[k]:
            copy.wait()

        def one(p, carry):
            factor = scale[p]
            for place in range(2):
                total = (a_buf[p, :, place] + b_buf[p, :, place]) * factor
                mean_buf[place, p] = total[0:2]
                moment_buf[place, p] = total[2:5]
            return carry

        lax.fori_loop(block * k, block * (k + 1), one, 0)
        for copy in stores[k]:
            copy.start()
    for copies in stores:
        for copy in copies:
            copy.wait()


def scale_level(level, scale, mine, other, before):
    block = 18
    count = HALF // block
    any_space = pl.BlockSpec(memory_space=pl.ANY)
    return pl.pallas_call(
        functools.partial(scale_kernel, level, block),
        in_specs=[pl.BlockSpec(memory_space=pltpu.SMEM)] + [any_space] * (2 + len(before)),
        out_specs=[pl.BlockSpec(memory_space=pltpu.HBM)] * 2,
        out_shape=[jax.ShapeDtypeStruct((HALF, 2, ROWS, WIDTH), F32), jax.ShapeDtypeStruct((HALF, 3, ROWS, WIDTH), F32)],
        scratch_shapes=[
            pltpu.VMEM((HALF, 5, 2, 8, WIDTH), F32),
            pltpu.VMEM((HALF, 5, 2, 8, WIDTH), F32),
            pltpu.VMEM((2, HALF, 2, 8, WIDTH), F32),
            pltpu.VMEM((2, HALF, 3, 8, WIDTH), F32),
            pltpu.SemaphoreType.DMA((6 * count,)),
        ],
        input_output_aliases={3: 0, 4: 1} if before else {},
        compiler_params=pltpu.CompilerParams(vmem_limit_bytes=10 * MIB),
        name="scale_level",
    )(scale, mine, other, *before)


def to_partner(value):
    return lax.ppermute(value, "snap", [(0, 1), (1, 0)])


def to_above(value):
    size = lax.axis_size("tile")
    return lax.ppermute(value, "tile", [(i + 1, i) for i in range(size - 1)])


def to_below(value):
    size = lax.axis_size("tile")
    return lax.ppermute(value, "tile", [(i, i + 1) for i in range(size - 1)])


def level_cuts(cuts, level):
    return cuts[:level + 1]


def send(up_pieces, dn_pieces):
    from_below = [to_above(piece) for piece in up_pieces]
    from_above = [to_below(piece) for piece in dn_pieces]
    return from_below, from_above


def per_device(velocity, offsets, phase):
    snap = lax.axis_index("snap")
    tile = lax.axis_index("tile")
    dy, dx = offsets[:, 0].astype(I32), offsets[:, 1].astype(I32)
    turned = lax.rem(phase.astype(I32) + PHASES - HALF * snap, PHASES)
    kind = jnp.where(tile == 0, 0, jnp.where(tile == lax.axis_size("tile") - 1, 2, 1)).astype(I32)
    meta = jnp.concatenate([dy, dx, turned, kind[None]])
    colop = jnp.asarray(column_constant())
    rowop = jnp.asarray(row_constant())
    onehot = (turned[:, None] == jnp.arange(PHASES, dtype=I32)[None, :]).astype(I32)
    own = jnp.sum(onehot, axis=0)

    smooth = functools.partial(smooth_part, velocity=velocity, colop=colop, rowop=rowop)

    def full(scale, *_):
        strips, up, dn, positions, plan = smooth(2, meta, jnp.zeros((16,), I32), cuts=FULL_CUTS)
        below, above = send(up, dn)
        before = ()
        for level in (3, 0, 1, 2):
            mine, theirs = finish_level(level, meta, plan, [(positions, strips, FULL_CUTS, below, above)])
            before = scale_level(level, scale, mine, to_partner(theirs), before)
        return tuple(before)

    def fast(scale, mine, theirs, plan, strips_a, pos_a, below_a, above_a, strips_b, pos_b, up_b, dn_b):
        rest = (up_b[1], dn_b[1])
        below_b, above_b = send(up_b[:1], dn_b[:1])
        other = to_partner(theirs)
        more = send(rest[0:1], rest[1:2])
        before = scale_level(3, scale, mine, other, ())
        here, before = lax.optimization_barrier((meta, tuple(before)))
        parts = [(pos_a, strips_a, FIRST_CUTS, below_a, above_a),
                 (pos_b, strips_b, REST_CUTS, below_b + more[0], above_b + more[1])]
        totals = [finish_level(level, here, plan, parts) for level in range(3)]
        for level, (mine, theirs) in enumerate(totals):
            before = scale_level(level, scale, mine, to_partner(theirs), before)
        return tuple(before)

    strips_a, up_a, dn_a, pos_a, plan = smooth(0, meta, jnp.zeros((16,), I32), cuts=FIRST_CUTS)
    below_a, above_a = send(up_a, dn_a)
    message = jnp.concatenate([own, plan[8:]])
    reply = to_partner(message)
    strips_b, up_b, dn_b, pos_b, _ = smooth(1, meta, plan, cuts=REST_CUTS)
    mine, theirs = finish_level(3, meta, plan, [(pos_a, strips_a, (), (), ()), (pos_b, strips_b, (), (), ())])
    scale = 1.0 / jnp.maximum((message[:HALF] + reply[HALF:PHASES]).astype(F32), 1.0)
    over = jnp.maximum(message[PHASES], reply[PHASES])
    return lax.cond(over <= 0, fast, full, scale, mine, theirs,
                    plan, strips_a, pos_a, below_a, above_a, strips_b, pos_b, up_b, dn_b)


def solution(mesh):
    in_specs = (P("snap", None, "tile", None), P("snap", None), P("snap"))
    out_specs = (P("snap", None, "tile", None), P("snap", None, "tile", None))
    return jax.shard_map(
        per_device, mesh=mesh, in_specs=in_specs, out_specs=out_specs, check_vma=False
    )
```

```python
import functools

import jax
import jax.numpy as jnp
import numpy as np
from jax import lax
from jax.experimental import pallas as pl
from jax.experimental.pallas import tpu as pltpu
from jax.sharding import PartitionSpec as P

PHASES = 72
HALF = PHASES // 2
RAD = 8
MAXS = 16
HALO = RAD + MAXS
ROWS = 64
WIDTH = 256
SNAPS = 128
EXT = ROWS + 2 * HALO
GROUP = 8
CHUNK = 128
GAP = 16
MIB = 1024 * 1024
FIRST_CUTS = (640,)
REST_CUTS = (984,)
FULL_CUTS = (3072 + 64,)
GROUPS = SNAPS // 8
F32 = jnp.float32
BF16 = jnp.bfloat16
I32 = jnp.int32


def taps():
    steps = np.arange(2 * RAD + 1, dtype=np.float64) - RAD
    sigma = RAD / 2.0
    values = np.exp(-steps * steps / (2.0 * sigma * sigma))
    return values / values.sum()


def split_const(values):
    high = values.astype(BF16)
    low = (values - high.astype(np.float64)).astype(BF16)
    return high, low


def column_constant():
    weight = taps()
    source = np.arange(WIDTH)[:, None]
    target = np.arange(WIDTH)[None, :]
    distance = source - target
    band = np.where(np.abs(distance) <= RAD, weight[np.clip(distance + RAD, 0, 2 * RAD)], 0.0)
    high, low = split_const(band)
    return np.concatenate([high, low, high], axis=0)


def row_constant():
    weight = taps()
    target = np.arange(EXT)[None, :, None] - HALO
    source = np.arange(ROWS)[None, None, :]
    shift = np.arange(-MAXS, MAXS + 1)[:, None, None]
    distance = source - shift - target
    band = np.where(np.abs(distance) <= RAD, weight[np.clip(distance + RAD, 0, 2 * RAD)], 0.0)
    seen = source - shift
    kinds = []
    for kind in range(3):
        keep = np.ones_like(seen, dtype=bool)
        if kind == 0:
            keep = seen >= 0
        if kind == 2:
            keep = seen < ROWS
        high, low = split_const(np.where(keep, band, 0.0))
        kinds.append(np.concatenate([high, low, high], axis=2))
    return np.stack(kinds)


def level_rows(need, level):
    return jnp.clip(need - 8 * level, 0, 8)


def needs(dy):
    return jnp.clip(RAD + dy, 0, HALO), jnp.clip(RAD - dy, 0, HALO)


def next_start(end):
    return (end & -8) + 16


def split(value):
    high = value.astype(BF16)
    return high, (value - high.astype(F32)).astype(BF16)


def smooth_kernel(part, cuts, meta, plan, *refs):
    pieces = len(cuts)
    vel, colop, rowop, refs = *refs[:3], refs[3:]
    if part == 1:
        early, refs = refs[0], refs[1:]
    strips = 3 if part else 4
    y_refs, refs = refs[:strips], refs[strips:]
    if part:
        mine, theirs, refs = refs[0], refs[1], refs[2:]
    out_up, out_dn = refs[:pieces], refs[pieces:2 * pieces]
    pos_ref, plan_ref, refs = *refs[2 * pieces:2 * pieces + 2], refs[2 * pieces + 2:]
    vel_buf, oper_buf, col_buf, refs = *refs[:3], refs[3:]
    y_bufs, refs = refs[:4], refs[4:]
    if part:
        acc, refs = refs[0], refs[1:]
    xs, stack, up, dn, cursor, load_sem, store_sem, sem = refs
    row = lax.broadcasted_iota(I32, (8, WIDTH), 0)
    lane = lax.broadcasted_iota(I32, (1, WIDTH), 1)
    dot = functools.partial(jnp.dot, preferred_element_type=F32)

    def load(g):
        rows = pl.ds(GROUP * g, GROUP)
        return pltpu.make_async_copy(vel.at[rows], vel_buf.at[rows], load_sem.at[g])

    def store(g, level):
        rows = pl.ds(GROUP * g, GROUP)
        return pltpu.make_async_copy(y_bufs[level].at[rows], y_refs[level].at[rows], store_sem.at[g, level])

    def load_early(g):
        rows = pl.ds(GROUP * g, GROUP)
        return pltpu.make_async_copy(early.at[rows], y_bufs[3].at[rows], store_sem.at[g, 3])

    def add_fields(n, place, u, v):
        phase = meta[2 * SNAPS + n]
        for at_field, field in enumerate((u, v, u * u, v * v, u * v)):
            acc[phase, at_field, place] += field

    def loop(low, high, body):
        lax.fori_loop(low, high, lambda g, carry: (body(g), carry)[1], 0)

    def ends(sums):
        starts, stops = [], []
        for side in range(2):
            start = I32(0)
            for level in range(3):
                starts.append(start)
                start = next_start(start + sums[3 * side + level])
                stops.append(start)
        return starts, stops

    def count_group(g, sums):
        for b in range(GROUP):
            sums = list(sums)
            for side, need in enumerate(needs(meta[GROUP * g + b])):
                for level in range(3):
                    sums[3 * side + level] += level_rows(need, level)
        return tuple(sums)

    tables = [pltpu.make_async_copy(colop, col_buf, sem.at[0]),
              pltpu.make_async_copy(rowop.at[meta[3 * SNAPS]], oper_buf, sem.at[1])]
    zero = (I32(0),) * 6
    if part == 0:
        load(0).start()
        for copy in tables:
            copy.start()
        for g in range(1, 4):
            load(g).start()

        def add_group(g, carry):
            sums, taken, count, going = carry
            sums = count_group(g, sums)
            stops = ends(sums)[1]
            going = going & (jnp.maximum(stops[2], stops[5]) <= cuts[-1]).astype(I32)
            taken = tuple(jnp.where(going > 0, new, old) for new, old in zip(sums, taken))
            return sums, taken, count + going, going

        sums, taken, count, _ = lax.fori_loop(0, GROUPS, add_group, (zero, zero, I32(0), I32(1)))
        begin, end = I32(0), count
        starts = ends(taken)[0]
        rest_starts, rest_stops = ends([whole - some for whole, some in zip(sums, taken)])
        over = I32(0)
        for side in range(2):
            for level in range(3):
                limit = level_cuts(REST_CUTS, level)[-1]
                over = jnp.maximum(over, rest_stops[3 * side + level] - limit)
        for k in range(8):
            plan_ref[k] = rest_starts[k] if k < 6 else count
            plan_ref[8 + k] = over
        loop(4, end, lambda g: load(g).start())
    elif part == 1:
        begin, end = plan[6], I32(GROUPS)
        loop(begin, end, lambda g: load(g).start())
        for copy in tables:
            copy.start()
        loop(0, begin, lambda g: load_early(g).start())
        starts = [plan[k] for k in range(6)]
    else:
        begin, end = I32(0), I32(GROUPS)
        loop(begin, end, lambda g: load(g).start())
        for copy in tables:
            copy.start()
        starts = ends(lax.fori_loop(0, GROUPS, count_group, zero))[0]
    if part:
        acc[...] = jnp.zeros_like(acc)
        for k in range(16):
            plan_ref[k] = I32(GROUPS)
    for k in range(6):
        cursor[k] = starts[k]
    for copy in tables:
        copy.wait()

    def group(g):
        load(g).wait()
        for b in range(GROUP):
            n = GROUP * g + b
            dx = meta[SNAPS + n]
            rolled = pltpu.roll(vel_buf[n].reshape(2 * ROWS, WIDTH), (WIDTH - dx) & (WIDTH - 1), 1)
            moved = lane + dx
            high, low = split(jnp.where((moved >= 0) & (moved < WIDTH), rolled, 0.0))
            rows = slice(2 * ROWS * b, 2 * ROWS * (b + 1))
            xs[rows, 0:WIDTH] = high
            xs[rows, WIDTH:2 * WIDTH] = high
            xs[rows, 2 * WIDTH:3 * WIDTH] = low
        high, low = split(dot(xs[...], col_buf[...]))
        for b in range(GROUP):
            for comp in range(2):
                rows = slice(ROWS * (2 * b + comp), ROWS * (2 * b + comp + 1))
                stack[b, comp, 0:ROWS] = high[rows]
                stack[b, comp, ROWS:2 * ROWS] = high[rows]
                stack[b, comp, 2 * ROWS:3 * ROWS] = low[rows]
        for b in range(GROUP):
            n = GROUP * g + b
            oper = oper_buf[meta[n] + MAXS]
            ext = [dot(oper, stack[b, comp]) for comp in range(2)]
            for level in range(strips):
                for comp in range(2):
                    top = HALO + 8 * level
                    bottom = HALO + ROWS - 8 - 8 * level
                    y_bufs[level][n, 0, comp] = ext[comp][top:top + 8]
                    y_bufs[level][n, 1, comp] = ext[comp][bottom:bottom + 8]
            if part:
                for place in range(2):
                    rows = slice(2 * HALO + 8 * place, 2 * HALO + 8 * place + 8)
                    add_fields(n, place, ext[0][rows], ext[1][rows])
            for side, need in enumerate(needs(meta[n])):
                buffer = (up, dn)[side]
                for level in range(3):
                    slot = 3 * side + level
                    have = level_rows(need, level)
                    here = cursor[slot]
                    cursor[slot] = here + have
                    pos = jnp.minimum(here, cuts[-1] - 16)
                    pos_ref[6 * n + slot] = pos
                    skew = pos & 7
                    base = pl.multiple_of(pos - skew, 8)
                    source = 16 - 8 * level if side == 0 else HALO + ROWS + 8 * level
                    turn = (skew + have) & 7 if side == 0 else skew
                    for comp in range(2):
                        tile = pltpu.roll(ext[comp][source:source + 8], turn, 0)
                        old = buffer[comp, pl.ds(base, 8)]
                        buffer[comp, pl.ds(base, 8)] = jnp.where(row < skew, old, tile)
                        buffer[comp, pl.ds(base + 8, 8)] = tile
        for level in range(strips):
            store(g, level).start()

    loop(begin, end, group)
    copies = []
    low = 0
    for piece, high in enumerate(cuts):
        for side in range(2):
            copies.append(pltpu.make_async_copy(
                (up, dn)[side].at[:, low:high], (out_up, out_dn)[side][piece], sem.at[2 + len(copies)]))
        low = high
    for copy in copies:
        copy.start()
    if part:
        def add_early(g):
            load_early(g).wait()
            for n in range(GROUP):
                for place in range(2):
                    add_fields(GROUP * g + n, place, y_bufs[3][GROUP * g + n, place, 0], y_bufs[3][GROUP * g + n, place, 1])

        if part == 1:
            loop(0, begin, add_early)
        sums_out = [pltpu.make_async_copy(acc.at[HALF:PHASES], theirs, sem.at[2 + len(copies)]),
                    pltpu.make_async_copy(acc.at[0:HALF], mine, sem.at[3 + len(copies)])]
        for copy in sums_out:
            copy.start()
        copies += sums_out
    else:
        for g in range(4):
            pl.when(g >= end)(load(g).wait)

    def stored(g):
        for level in range(strips):
            store(g, level).wait()

    loop(begin, end, stored)
    for copy in copies:
        copy.wait()


def smooth_part(part, meta, plan, velocity, colop, rowop, cuts, early=()):
    pieces = len(cuts)
    sizes = [high - low for low, high in zip((0,) + cuts[:-1], cuts)]
    any_space = pl.BlockSpec(memory_space=pltpu.HBM)
    smem = pl.BlockSpec(memory_space=pltpu.SMEM)
    piece_shapes = [jax.ShapeDtypeStruct((2, size, WIDTH), F32) for size in sizes]
    strip = jax.ShapeDtypeStruct((SNAPS, 2, 2, 8, WIDTH), F32)
    room = cuts[-1] + GAP
    total = jax.ShapeDtypeStruct((HALF, 5, 2, 8, WIDTH), F32)
    strips, sums = (3, 2) if part else (4, 0)
    out = pl.pallas_call(
        functools.partial(smooth_kernel, part, cuts),
        in_specs=[smem] * 2 + [any_space] * (3 + len(early)),
        out_specs=[any_space] * (strips + sums + 2 * pieces) + [smem, smem],
        scratch_shapes=[
            pltpu.VMEM((SNAPS, 2, ROWS, WIDTH), F32),
            pltpu.VMEM((2 * MAXS + 1, EXT, 3 * ROWS), BF16),
            pltpu.VMEM((3 * WIDTH, WIDTH), BF16),
        ] + [pltpu.VMEM((SNAPS, 2, 2, 8, WIDTH), F32)] * 4
        + ([pltpu.VMEM((PHASES, 5, 2, 8, WIDTH), F32)] if part else []) + [
            pltpu.VMEM((GROUP * 2 * ROWS, 3 * WIDTH), BF16),
            pltpu.VMEM((GROUP, 2, 3 * ROWS, WIDTH), BF16),
            pltpu.VMEM((2, room, WIDTH), F32),
            pltpu.VMEM((2, room, WIDTH), F32),
            pltpu.SMEM((8,), I32),
            pltpu.SemaphoreType.DMA((GROUPS,)),
            pltpu.SemaphoreType.DMA((GROUPS, 4)),
            pltpu.SemaphoreType.DMA((4 + 2 * pieces,)),
        ],
        out_shape=[strip] * strips + [total] * sums + piece_shapes * 2
        + [jax.ShapeDtypeStruct((SNAPS * 6,), I32), jax.ShapeDtypeStruct((16,), I32)],
        compiler_params=pltpu.CompilerParams(vmem_limit_bytes=62 * MIB),
        name="smooth_part",
    )(meta, plan, velocity, colop, rowop, *early)
    packs = out[strips + sums:]
    return out[:strips], out[strips:strips + sums], packs[:pieces], packs[pieces:2 * pieces], out[-2], out[-1]


def finish_kernel(level, cuts, meta, plan, *refs):
    parts = len(cuts)
    pos_refs, strips, refs = refs[:parts], refs[parts:2 * parts], refs[2 * parts:]
    pieces = []
    for k in range(parts):
        many = len(cuts[k])
        pieces.append((refs[:many], refs[many:2 * many]))
        refs = refs[2 * many:]
    mine, theirs, acc, y_buf, *refs = refs
    buffers, (y_sem, sem) = refs[:-2], refs[-2:]
    middle = plan[6] if parts == 2 else I32(GROUPS)
    ranges = [(I32(0), middle), (middle, I32(GROUPS))][:parts]

    def loop(low, high, body):
        lax.fori_loop(low, high, lambda g, carry: (body(g), carry)[1], 0)

    def load(k, g):
        rows = pl.ds(GROUP * g, GROUP)
        return pltpu.make_async_copy(strips[k].at[rows], y_buf.at[rows], y_sem.at[g])

    packs = [[] for _ in range(parts)]
    total = 0
    for k in range(parts):
        low = 0
        first, last = ranges[k]
        for piece, high in enumerate(cuts[k]):
            for side in range(2):
                slot = 3 * side + level
                begin = pos_refs[k][6 * GROUP * jnp.minimum(first, GROUPS - 1) + slot]
                end = pos_refs[k][6 * (GROUP * jnp.maximum(last, 1) - 1) + slot] + 16
                for row_at in range(low, high, CHUNK):
                    stop = min(row_at + CHUNK, high)
                    copy = pltpu.make_async_copy(
                        pieces[k][side][piece].at[:, row_at - low:stop - low],
                        buffers[2 * k + side].at[:, row_at:stop], sem.at[total])
                    total += 1
                    packs[k].append((copy, (first < last) & (begin < stop) & (end > row_at)))
            low = high
    for k in range(parts):
        for copy, needed in packs[k]:
            pl.when(needed)(copy.start)
        loop(*ranges[k], lambda g, k=k: load(k, g).start())
    acc[...] = jnp.zeros_like(acc)
    row = lax.broadcasted_iota(I32, (8, WIDTH), 0)

    def one(n, k):
        phase = meta[2 * SNAPS + n]
        for place in range(2):
            fields = [y_buf[n, place, comp] for comp in range(2)]
            if cuts[k]:
                side = 1 - place
                have = level_rows(needs(meta[n])[side], level)
                pos = pos_refs[k][6 * n + 3 * side + level]
                skew = pos & 7
                base = pl.multiple_of(pos - skew, 8)
                turn = skew if place == 0 else (skew + have) & 7
                known = jnp.where(meta[3 * SNAPS] == 2 * place, 0, have)
                keep = row < known if place == 0 else row >= 8 - known
                for comp in range(2):
                    lower = buffers[2 * k + side][comp, pl.ds(base, 8)]
                    upper = buffers[2 * k + side][comp, pl.ds(base + 8, 8)]
                    tile = pltpu.roll(jnp.where(row >= skew, lower, upper), (8 - turn) & 7, 0)
                    fields[comp] += jnp.where(keep, tile, 0.0)
            u, v = fields
            for at_field, field in enumerate((u, v, u * u, v * v, u * v)):
                acc[phase, at_field, place] += field

    def group(g, k):
        load(k, g).wait()
        for b in range(GROUP):
            one(GROUP * g + b, k)

    for k in range(parts):
        for copy, needed in packs[k]:
            pl.when(needed)(copy.wait)
        loop(*ranges[k], lambda g, k=k: group(g, k))
    stores = [pltpu.make_async_copy(acc.at[HALF:PHASES], theirs, y_sem.at[0]),
              pltpu.make_async_copy(acc.at[0:HALF], mine, y_sem.at[1])]
    for copy in stores:
        copy.start()
    for copy in stores:
        copy.wait()


def finish_level(level, meta, plan, parts):
    any_space = pl.BlockSpec(memory_space=pltpu.HBM)
    smem = pl.BlockSpec(memory_space=pltpu.SMEM)
    shape = jax.ShapeDtypeStruct((HALF, 5, 2, 8, WIDTH), F32)
    cuts = [level_cuts(part[2], level) if level < 3 else () for part in parts]
    packs = [piece for part, some in zip(parts, cuts) for side in part[3:5] for piece in side[:len(some)]]
    chunks = sum(2 * (-(-(high - low) // CHUNK)) for some in cuts for low, high in zip((0,) + some[:-1], some))
    rooms = [some[-1] + GAP for some in cuts if some]
    return pl.pallas_call(
        functools.partial(finish_kernel, level, cuts),
        in_specs=[smem] * (2 + len(parts)) + [any_space] * (len(parts) + len(packs)),
        out_specs=[any_space] * 2,
        out_shape=[shape] * 2,
        scratch_shapes=[
            pltpu.VMEM((PHASES, 5, 2, 8, WIDTH), F32),
            pltpu.VMEM((SNAPS, 2, 2, 8, WIDTH), F32),
        ] + [pltpu.VMEM((2, room, WIDTH), F32) for room in rooms for _ in range(2)] + [
            pltpu.SemaphoreType.DMA((GROUPS,)),
            pltpu.SemaphoreType.DMA((max(chunks, 1),)),
        ],
        compiler_params=pltpu.CompilerParams(vmem_limit_bytes=62 * MIB),
        name="finish_level",
    )(meta, plan, *[part[0] for part in parts], *[part[1][level] for part in parts], *packs)


def scale_kernel(levels, block, message, reply, *refs):
    many = len(levels)
    mines, others = refs[:many], refs[many:2 * many]
    mean, moment, a_buf, b_buf, load_sem, store_sem = refs[-6:]
    parts = [(k, slice(start, start + block)) for k in range(many) for start in range(0, HALF, block)]
    loads, stores = [], []
    for at, (k, part) in enumerate(parts):
        loads.append([pltpu.make_async_copy(mines[k].at[part], a_buf.at[k, part], load_sem.at[2 * at]),
                      pltpu.make_async_copy(others[k].at[part], b_buf.at[k, part], load_sem.at[2 * at + 1])])
        group = []
        for place in range(2):
            first = 8 * levels[k] if place == 0 else ROWS - 8 - 8 * levels[k]
            rows = slice(first, first + 8)
            for which, (fields, out) in enumerate(((slice(0, 2), mean), (slice(2, 5), moment))):
                group.append(pltpu.make_async_copy(
                    a_buf.at[k, part, fields, place], out.at[part, :, rows], store_sem.at[4 * at + 2 * place + which]))
        stores.append(group)
    for copies in loads:
        for copy in copies:
            copy.start()
    for at, (k, part) in enumerate(parts):
        for copy in loads[at]:
            copy.wait()

        def one(p, carry, k=k):
            count = jnp.full((8, WIDTH), message[0, p] + reply[0, HALF + p], I32).astype(F32)
            a_buf[k, p] = (a_buf[k, p] + b_buf[k, p]) * (1.0 / jnp.maximum(count, 1.0))
            return carry

        lax.fori_loop(part.start, part.stop, one, 0, unroll=2)
        for copy in stores[at]:
            copy.start()
    for copies in stores:
        for copy in copies:
            copy.wait()


def scale_levels(levels, counts, pairs, before):
    block = 18
    many = len(levels)
    parts = many * HALF // block
    smem = pl.BlockSpec(memory_space=pltpu.SMEM)
    hbm = pl.BlockSpec(memory_space=pltpu.HBM)
    buffer = pltpu.VMEM((many, HALF, 5, 2, 8, WIDTH), F32)
    return pl.pallas_call(
        functools.partial(scale_kernel, levels, block),
        in_specs=[smem] * 2 + [hbm] * (2 * many + len(before)),
        out_specs=[hbm] * 2,
        out_shape=[jax.ShapeDtypeStruct((HALF, 2, ROWS, WIDTH), F32), jax.ShapeDtypeStruct((HALF, 3, ROWS, WIDTH), F32)],
        scratch_shapes=[buffer, buffer, pltpu.SemaphoreType.DMA((2 * parts,)), pltpu.SemaphoreType.DMA((4 * parts,))],
        input_output_aliases={2 + 2 * many: 0, 3 + 2 * many: 1} if before else {},
        compiler_params=pltpu.CompilerParams(vmem_limit_bytes=62 * MIB),
        name="scale_levels",
    )(*counts, *[pair[0] for pair in pairs], *[pair[1] for pair in pairs], *before)


def exchange_kernel(up, dn, theirs, message, below, above, other, reply, send_sem, recv_sem):
    snap, tile = lax.axis_index("snap"), lax.axis_index("tile")
    size = lax.axis_size("tile")
    to_up = (snap, lax.rem(tile + size - 1, size))
    to_dn = (snap, lax.rem(tile + 1, size))
    to_core = (1 - snap, tile)
    barrier = pltpu.get_barrier_semaphore()
    for target in (to_up, to_dn, to_core):
        pl.semaphore_signal(barrier, inc=1, device_id=target, device_id_type=pl.DeviceIdType.MESH)
    pl.semaphore_wait(barrier, 3)
    copies = []
    for source, landing, target in ((up, below, to_up), (dn, above, to_dn), (theirs, other, to_core), (message, reply, to_core)):
        copies.append(pltpu.make_async_remote_copy(
            src_ref=source, dst_ref=landing, send_sem=send_sem.at[len(copies)], recv_sem=recv_sem.at[len(copies)],
            device_id=target, device_id_type=pl.DeviceIdType.MESH))
    for copy in copies:
        copy.start()
    for copy in copies:
        copy.wait()


def exchange(up, dn, theirs, message):
    any_space = pl.BlockSpec(memory_space=pltpu.HBM)
    return pl.pallas_call(
        exchange_kernel,
        in_specs=[any_space] * 4,
        out_specs=[any_space] * 4,
        out_shape=[jax.ShapeDtypeStruct(value.shape, value.dtype) for value in (up, dn, theirs, message)],
        scratch_shapes=[pltpu.SemaphoreType.DMA((4,)), pltpu.SemaphoreType.DMA((4,))],
        compiler_params=pltpu.CompilerParams(collective_id=0, has_side_effects=True, vmem_limit_bytes=62 * MIB),
        name="exchange",
    )(up, dn, theirs, message)


def to_partner(value):
    return lax.ppermute(value, "snap", [(0, 1), (1, 0)])


def to_above(value):
    size = lax.axis_size("tile")
    return lax.ppermute(value, "tile", [(i + 1, i) for i in range(size - 1)])


def to_below(value):
    size = lax.axis_size("tile")
    return lax.ppermute(value, "tile", [(i, i + 1) for i in range(size - 1)])


def level_cuts(cuts, level):
    return cuts[:level + 1]


def send(up_pieces, dn_pieces):
    from_below = [to_above(piece) for piece in up_pieces]
    from_above = [to_below(piece) for piece in dn_pieces]
    return from_below, from_above


def per_device(velocity, offsets, phase):
    snap = lax.axis_index("snap")
    tile = lax.axis_index("tile")
    dy, dx = offsets[:, 0].astype(I32), offsets[:, 1].astype(I32)
    turned = lax.rem(phase.astype(I32) + PHASES - HALF * snap, PHASES)
    kind = jnp.where(tile == 0, 0, jnp.where(tile == lax.axis_size("tile") - 1, 2, 1)).astype(I32)
    meta = jnp.concatenate([dy, dx, turned, kind[None]])
    colop = jnp.asarray(column_constant())
    rowop = jnp.asarray(row_constant())
    onehot = (turned[:, None] == jnp.arange(PHASES, dtype=I32)[None, :]).astype(I32)
    own = jnp.sum(onehot, axis=0)

    smooth = functools.partial(smooth_part, velocity=velocity, colop=colop, rowop=rowop)

    def full(counts, *_):
        strips, sums, up, dn, positions, plan = smooth(2, meta, jnp.zeros((16,), I32), cuts=FULL_CUTS)
        below, above = send(up, dn)
        totals = [finish_level(level, meta, plan, [(positions, strips, FULL_CUTS, below, above)]) for level in range(3)]
        totals = [(mine, to_partner(theirs)) for mine, theirs in (sums, *totals)]
        before = scale_levels((3, 0), counts, totals[:2], ())
        return tuple(scale_levels((1, 2), counts, totals[2:], before))

    def last(counts, mine, other, mean, moment):
        return tuple(scale_levels((2,), counts, [(mine, other)], (mean, moment)))

    strips_a, _, up_a, dn_a, pos_a, plan = smooth(0, meta, jnp.zeros((16,), I32), cuts=FIRST_CUTS)
    below_a, above_a = send(up_a, dn_a)
    message = jnp.broadcast_to(jnp.concatenate([own, plan[8:], jnp.zeros((48,), I32)])[None], (8, 128))
    strips_b, sums, up_b, dn_b, pos_b, _ = smooth(1, meta, plan, cuts=REST_CUTS, early=(strips_a[3],))
    below_b, above_b, other, reply = exchange(up_b[0], dn_b[0], sums[1], message)
    counts = (message, reply)
    over = jnp.max(jnp.maximum(message, reply)[0:1, PHASES:PHASES + 8])
    parts = [(pos_a, strips_a, FIRST_CUTS, below_a, above_a), (pos_b, strips_b, REST_CUTS, [below_b], [above_b])]
    totals = [finish_level(level, meta, plan, parts) for level in range(3)]
    totals = [(sums[0], other)] + [(mine, to_partner(theirs)) for mine, theirs in totals]
    before = scale_levels((3, 0, 1), counts, totals[:3], ())
    return lax.cond(over <= 0, last, full, counts, *totals[3], *before)


def solution(mesh):
    in_specs = (P("snap", None, "tile", None), P("snap", None), P("snap"))
    out_specs = (P("snap", None, "tile", None), P("snap", None, "tile", None))
    return jax.shard_map(
        per_device, mesh=mesh, in_specs=in_specs, out_specs=out_specs, check_vma=False
    )
```

```python
import functools

import jax
import jax.numpy as jnp
import numpy as np
from jax import lax
from jax.experimental import pallas as pl
from jax.experimental.pallas import tpu as pltpu
from jax.sharding import PartitionSpec as P

PHASES = 72
HALF = PHASES // 2
RAD = 8
MAXS = 16
HALO = RAD + MAXS
ROWS = 64
WIDTH = 256
SNAPS = 128
EXT = ROWS + 2 * HALO
GROUP = 8
CHUNK = 128
GAP = 16
MIB = 1024 * 1024
FIRST_CUTS = (640,)
REST_CUTS = (512, 984)
FULL_CUTS = (3072 + 64,)
GROUPS = SNAPS // 8
F32 = jnp.float32
BF16 = jnp.bfloat16
I32 = jnp.int32


def taps():
    steps = np.arange(2 * RAD + 1, dtype=np.float64) - RAD
    sigma = RAD / 2.0
    values = np.exp(-steps * steps / (2.0 * sigma * sigma))
    return values / values.sum()


def split_const(values):
    high = values.astype(BF16)
    low = (values - high.astype(np.float64)).astype(BF16)
    return high, low


def column_constant():
    weight = taps()
    source = np.arange(WIDTH)[:, None]
    target = np.arange(WIDTH)[None, :]
    distance = source - target
    band = np.where(np.abs(distance) <= RAD, weight[np.clip(distance + RAD, 0, 2 * RAD)], 0.0)
    high, low = split_const(band)
    return np.concatenate([high, low, high], axis=0)


def row_constant():
    weight = taps()
    target = np.arange(EXT)[None, :, None] - HALO
    source = np.arange(ROWS)[None, None, :]
    shift = np.arange(-MAXS, MAXS + 1)[:, None, None]
    distance = source - shift - target
    band = np.where(np.abs(distance) <= RAD, weight[np.clip(distance + RAD, 0, 2 * RAD)], 0.0)
    seen = source - shift
    kinds = []
    for kind in range(3):
        keep = np.ones_like(seen, dtype=bool)
        if kind == 0:
            keep = seen >= 0
        if kind == 2:
            keep = seen < ROWS
        high, low = split_const(np.where(keep, band, 0.0))
        kinds.append(np.concatenate([high, low, high], axis=2))
    return np.stack(kinds)


def level_rows(need, level):
    return jnp.clip(need - 8 * level, 0, 8)


def needs(dy):
    return jnp.clip(RAD + dy, 0, HALO), jnp.clip(RAD - dy, 0, HALO)


def next_start(end):
    return (end & -8) + 16


def split(value):
    high = value.astype(BF16)
    return high, (value - high.astype(F32)).astype(BF16)


def smooth_kernel(part, cuts, meta, plan, *refs):
    pieces = len(cuts)
    vel, colop, rowop, refs = *refs[:3], refs[3:]
    if part == 1:
        early, refs = refs[0], refs[1:]
    strips = 3 if part else 4
    y_refs, refs = refs[:strips], refs[strips:]
    if part:
        mine, theirs, refs = refs[0], refs[1], refs[2:]
    out_up, out_dn = refs[:pieces], refs[pieces:2 * pieces]
    pos_ref, plan_ref, refs = *refs[2 * pieces:2 * pieces + 2], refs[2 * pieces + 2:]
    vel_buf, oper_buf, col_buf, refs = *refs[:3], refs[3:]
    y_bufs, refs = refs[:4], refs[4:]
    if part:
        acc, refs = refs[0], refs[1:]
    xs, stack, up, dn, cursor, load_sem, store_sem, sem = refs
    row = lax.broadcasted_iota(I32, (8, WIDTH), 0)
    lane = lax.broadcasted_iota(I32, (1, WIDTH), 1)
    dot = functools.partial(jnp.dot, preferred_element_type=F32)

    def load(g):
        rows = pl.ds(GROUP * g, GROUP)
        return pltpu.make_async_copy(vel.at[rows], vel_buf.at[rows], load_sem.at[g])

    def store(g, level):
        rows = pl.ds(GROUP * g, GROUP)
        return pltpu.make_async_copy(y_bufs[level].at[rows], y_refs[level].at[rows], store_sem.at[g, level])

    def load_early(g):
        rows = pl.ds(GROUP * g, GROUP)
        return pltpu.make_async_copy(early.at[rows], y_bufs[3].at[rows], store_sem.at[g, 3])

    def add_fields(n, place, u, v):
        phase = meta[2 * SNAPS + n]
        for at_field, field in enumerate((u, v, u * u, v * v, u * v)):
            acc[phase, at_field, place] += field

    def loop(low, high, body):
        lax.fori_loop(low, high, lambda g, carry: (body(g), carry)[1], 0)

    def ends(sums):
        starts, stops = [], []
        for side in range(2):
            start = I32(0)
            for level in range(3):
                starts.append(start)
                start = next_start(start + sums[3 * side + level])
                stops.append(start)
        return starts, stops

    def count_group(g, sums):
        for b in range(GROUP):
            sums = list(sums)
            for side, need in enumerate(needs(meta[GROUP * g + b])):
                for level in range(3):
                    sums[3 * side + level] += level_rows(need, level)
        return tuple(sums)

    tables = [pltpu.make_async_copy(colop, col_buf, sem.at[0]),
              pltpu.make_async_copy(rowop.at[meta[3 * SNAPS]], oper_buf, sem.at[1])]
    zero = (I32(0),) * 6
    if part == 0:
        load(0).start()
        for copy in tables:
            copy.start()
        for g in range(1, 4):
            load(g).start()

        def add_group(g, carry):
            sums, taken, count, going = carry
            sums = count_group(g, sums)
            stops = ends(sums)[1]
            going = going & (jnp.maximum(stops[2], stops[5]) <= cuts[-1]).astype(I32)
            taken = tuple(jnp.where(going > 0, new, old) for new, old in zip(sums, taken))
            return sums, taken, count + going, going

        sums, taken, count, _ = lax.fori_loop(0, GROUPS, add_group, (zero, zero, I32(0), I32(1)))
        begin, end = I32(0), count
        starts = ends(taken)[0]
        rest_starts, rest_stops = ends([whole - some for whole, some in zip(sums, taken)])
        over = I32(0)
        for side in range(2):
            for level in range(3):
                limit = level_cuts(REST_CUTS, level)[-1]
                over = jnp.maximum(over, rest_stops[3 * side + level] - limit)
        for k in range(8):
            plan_ref[k] = rest_starts[k] if k < 6 else count
            plan_ref[8 + k] = over
        loop(4, end, lambda g: load(g).start())
    elif part == 1:
        begin, end = plan[6], I32(GROUPS)
        loop(begin, end, lambda g: load(g).start())
        for copy in tables:
            copy.start()
        loop(0, begin, lambda g: load_early(g).start())
        starts = [plan[k] for k in range(6)]
    else:
        begin, end = I32(0), I32(GROUPS)
        loop(begin, end, lambda g: load(g).start())
        for copy in tables:
            copy.start()
        starts = ends(lax.fori_loop(0, GROUPS, count_group, zero))[0]
    if part:
        acc[...] = jnp.zeros_like(acc)
        for k in range(16):
            plan_ref[k] = I32(GROUPS)
    for k in range(6):
        cursor[k] = starts[k]
    for copy in tables:
        copy.wait()

    def group(g):
        load(g).wait()
        for b in range(GROUP):
            n = GROUP * g + b
            dx = meta[SNAPS + n]
            rolled = pltpu.roll(vel_buf[n].reshape(2 * ROWS, WIDTH), (WIDTH - dx) & (WIDTH - 1), 1)
            moved = lane + dx
            high, low = split(jnp.where((moved >= 0) & (moved < WIDTH), rolled, 0.0))
            rows = slice(2 * ROWS * b, 2 * ROWS * (b + 1))
            xs[rows, 0:WIDTH] = high
            xs[rows, WIDTH:2 * WIDTH] = high
            xs[rows, 2 * WIDTH:3 * WIDTH] = low
        high, low = split(dot(xs[...], col_buf[...]))
        for b in range(GROUP):
            for comp in range(2):
                rows = slice(ROWS * (2 * b + comp), ROWS * (2 * b + comp + 1))
                stack[b, comp, 0:ROWS] = high[rows]
                stack[b, comp, ROWS:2 * ROWS] = high[rows]
                stack[b, comp, 2 * ROWS:3 * ROWS] = low[rows]
        for b in range(GROUP):
            n = GROUP * g + b
            oper = oper_buf[meta[n] + MAXS]
            ext = [dot(oper, stack[b, comp]) for comp in range(2)]
            for level in range(strips):
                for comp in range(2):
                    top = HALO + 8 * level
                    bottom = HALO + ROWS - 8 - 8 * level
                    y_bufs[level][n, 0, comp] = ext[comp][top:top + 8]
                    y_bufs[level][n, 1, comp] = ext[comp][bottom:bottom + 8]
            if part:
                for place in range(2):
                    rows = slice(2 * HALO + 8 * place, 2 * HALO + 8 * place + 8)
                    add_fields(n, place, ext[0][rows], ext[1][rows])
            for side, need in enumerate(needs(meta[n])):
                buffer = (up, dn)[side]
                for level in range(3):
                    slot = 3 * side + level
                    have = level_rows(need, level)
                    here = cursor[slot]
                    cursor[slot] = here + have
                    pos = jnp.minimum(here, cuts[-1] - 16)
                    pos_ref[6 * n + slot] = pos
                    skew = pos & 7
                    base = pl.multiple_of(pos - skew, 8)
                    source = 16 - 8 * level if side == 0 else HALO + ROWS + 8 * level
                    turn = (skew + have) & 7 if side == 0 else skew
                    for comp in range(2):
                        tile = pltpu.roll(ext[comp][source:source + 8], turn, 0)
                        old = buffer[comp, pl.ds(base, 8)]
                        buffer[comp, pl.ds(base, 8)] = jnp.where(row < skew, old, tile)
                        buffer[comp, pl.ds(base + 8, 8)] = tile
        for level in range(strips):
            store(g, level).start()

    loop(begin, end, group)
    copies = []
    low = 0
    for piece, high in enumerate(cuts):
        for side in range(2):
            copies.append(pltpu.make_async_copy(
                (up, dn)[side].at[:, low:high], (out_up, out_dn)[side][piece], sem.at[2 + len(copies)]))
        low = high
    for copy in copies:
        copy.start()
    if part:
        def add_early(g):
            load_early(g).wait()
            for n in range(GROUP):
                for place in range(2):
                    add_fields(GROUP * g + n, place, y_bufs[3][GROUP * g + n, place, 0], y_bufs[3][GROUP * g + n, place, 1])

        if part == 1:
            loop(0, begin, add_early)
        sums_out = [pltpu.make_async_copy(acc.at[HALF:PHASES], theirs, sem.at[2 + len(copies)]),
                    pltpu.make_async_copy(acc.at[0:HALF], mine, sem.at[3 + len(copies)])]
        for copy in sums_out:
            copy.start()
        copies += sums_out
    else:
        for g in range(4):
            pl.when(g >= end)(load(g).wait)

    def stored(g):
        for level in range(strips):
            store(g, level).wait()

    loop(begin, end, stored)
    for copy in copies:
        copy.wait()


def smooth_part(part, meta, plan, velocity, colop, rowop, cuts, early=()):
    pieces = len(cuts)
    sizes = [high - low for low, high in zip((0,) + cuts[:-1], cuts)]
    any_space = pl.BlockSpec(memory_space=pltpu.HBM)
    smem = pl.BlockSpec(memory_space=pltpu.SMEM)
    piece_shapes = [jax.ShapeDtypeStruct((2, size, WIDTH), F32) for size in sizes]
    strip = jax.ShapeDtypeStruct((SNAPS, 2, 2, 8, WIDTH), F32)
    room = cuts[-1] + GAP
    total = jax.ShapeDtypeStruct((HALF, 5, 2, 8, WIDTH), F32)
    strips, sums = (3, 2) if part else (4, 0)
    out = pl.pallas_call(
        functools.partial(smooth_kernel, part, cuts),
        in_specs=[smem] * 2 + [any_space] * (3 + len(early)),
        out_specs=[any_space] * (strips + sums + 2 * pieces) + [smem, smem],
        scratch_shapes=[
            pltpu.VMEM((SNAPS, 2, ROWS, WIDTH), F32),
            pltpu.VMEM((2 * MAXS + 1, EXT, 3 * ROWS), BF16),
            pltpu.VMEM((3 * WIDTH, WIDTH), BF16),
        ] + [pltpu.VMEM((SNAPS, 2, 2, 8, WIDTH), F32)] * 4
        + ([pltpu.VMEM((PHASES, 5, 2, 8, WIDTH), F32)] if part else []) + [
            pltpu.VMEM((GROUP * 2 * ROWS, 3 * WIDTH), BF16),
            pltpu.VMEM((GROUP, 2, 3 * ROWS, WIDTH), BF16),
            pltpu.VMEM((2, room, WIDTH), F32),
            pltpu.VMEM((2, room, WIDTH), F32),
            pltpu.SMEM((8,), I32),
            pltpu.SemaphoreType.DMA((GROUPS,)),
            pltpu.SemaphoreType.DMA((GROUPS, 4)),
            pltpu.SemaphoreType.DMA((4 + 2 * pieces,)),
        ],
        out_shape=[strip] * strips + [total] * sums + piece_shapes * 2
        + [jax.ShapeDtypeStruct((SNAPS * 6,), I32), jax.ShapeDtypeStruct((16,), I32)],
        compiler_params=pltpu.CompilerParams(vmem_limit_bytes=62 * MIB),
        name="smooth_part",
    )(meta, plan, velocity, colop, rowop, *early)
    packs = out[strips + sums:]
    return out[:strips], out[strips:strips + sums], packs[:pieces], packs[pieces:2 * pieces], out[-2], out[-1]


def finish_kernel(level, cuts, meta, plan, *refs):
    parts = len(cuts)
    pos_refs, strips, refs = refs[:parts], refs[parts:2 * parts], refs[2 * parts:]
    pieces = []
    for k in range(parts):
        many = len(cuts[k])
        pieces.append((refs[:many], refs[many:2 * many]))
        refs = refs[2 * many:]
    mine, theirs, acc, y_buf, *refs = refs
    buffers, (y_sem, sem) = refs[:-2], refs[-2:]
    middle = plan[6] if parts == 2 else I32(GROUPS)
    ranges = [(I32(0), middle), (middle, I32(GROUPS))][:parts]

    def loop(low, high, body):
        lax.fori_loop(low, high, lambda g, carry: (body(g), carry)[1], 0)

    def load(k, g):
        rows = pl.ds(GROUP * g, GROUP)
        return pltpu.make_async_copy(strips[k].at[rows], y_buf.at[rows], y_sem.at[g])

    packs = [[] for _ in range(parts)]
    total = 0
    for k in range(parts):
        low = 0
        first, last = ranges[k]
        for piece, high in enumerate(cuts[k]):
            for side in range(2):
                slot = 3 * side + level
                begin = pos_refs[k][6 * GROUP * jnp.minimum(first, GROUPS - 1) + slot]
                end = pos_refs[k][6 * (GROUP * jnp.maximum(last, 1) - 1) + slot] + 16
                for row_at in range(low, high, CHUNK):
                    stop = min(row_at + CHUNK, high)
                    copy = pltpu.make_async_copy(
                        pieces[k][side][piece].at[:, row_at - low:stop - low],
                        buffers[2 * k + side].at[:, row_at:stop], sem.at[total])
                    total += 1
                    packs[k].append((copy, (first < last) & (begin < stop) & (end > row_at)))
            low = high
    for k in range(parts):
        for copy, needed in packs[k]:
            pl.when(needed)(copy.start)
        loop(*ranges[k], lambda g, k=k: load(k, g).start())
    acc[...] = jnp.zeros_like(acc)
    row = lax.broadcasted_iota(I32, (8, WIDTH), 0)

    def one(n, k):
        phase = meta[2 * SNAPS + n]
        for place in range(2):
            fields = [y_buf[n, place, comp] for comp in range(2)]
            if cuts[k]:
                side = 1 - place
                have = level_rows(needs(meta[n])[side], level)
                pos = pos_refs[k][6 * n + 3 * side + level]
                skew = pos & 7
                base = pl.multiple_of(pos - skew, 8)
                turn = skew if place == 0 else (skew + have) & 7
                known = jnp.where(meta[3 * SNAPS] == 2 * place, 0, have)
                keep = row < known if place == 0 else row >= 8 - known
                for comp in range(2):
                    lower = buffers[2 * k + side][comp, pl.ds(base, 8)]
                    upper = buffers[2 * k + side][comp, pl.ds(base + 8, 8)]
                    tile = pltpu.roll(jnp.where(row >= skew, lower, upper), (8 - turn) & 7, 0)
                    fields[comp] += jnp.where(keep, tile, 0.0)
            u, v = fields
            for at_field, field in enumerate((u, v, u * u, v * v, u * v)):
                acc[phase, at_field, place] += field

    def group(g, k):
        load(k, g).wait()
        for b in range(GROUP):
            one(GROUP * g + b, k)

    for k in range(parts):
        for copy, needed in packs[k]:
            pl.when(needed)(copy.wait)
        loop(*ranges[k], lambda g, k=k: group(g, k))
    stores = [pltpu.make_async_copy(acc.at[HALF:PHASES], theirs, y_sem.at[0]),
              pltpu.make_async_copy(acc.at[0:HALF], mine, y_sem.at[1])]
    for copy in stores:
        copy.start()
    for copy in stores:
        copy.wait()


def finish_level(level, meta, plan, parts):
    any_space = pl.BlockSpec(memory_space=pltpu.HBM)
    smem = pl.BlockSpec(memory_space=pltpu.SMEM)
    shape = jax.ShapeDtypeStruct((HALF, 5, 2, 8, WIDTH), F32)
    cuts = [level_cuts(part[2], level) if level < 3 else () for part in parts]
    packs = [piece for part, some in zip(parts, cuts) for side in part[3:5] for piece in side[:len(some)]]
    chunks = sum(2 * (-(-(high - low) // CHUNK)) for some in cuts for low, high in zip((0,) + some[:-1], some))
    rooms = [some[-1] + GAP for some in cuts if some]
    return pl.pallas_call(
        functools.partial(finish_kernel, level, cuts),
        in_specs=[smem] * (2 + len(parts)) + [any_space] * (len(parts) + len(packs)),
        out_specs=[any_space] * 2,
        out_shape=[shape] * 2,
        scratch_shapes=[
            pltpu.VMEM((PHASES, 5, 2, 8, WIDTH), F32),
            pltpu.VMEM((SNAPS, 2, 2, 8, WIDTH), F32),
        ] + [pltpu.VMEM((2, room, WIDTH), F32) for room in rooms for _ in range(2)] + [
            pltpu.SemaphoreType.DMA((GROUPS,)),
            pltpu.SemaphoreType.DMA((max(chunks, 1),)),
        ],
        compiler_params=pltpu.CompilerParams(vmem_limit_bytes=62 * MIB if level == 0 else 12 * MIB + 16 * WIDTH * sum(rooms)),
        name="finish_level",
    )(meta, plan, *[part[0] for part in parts], *[part[1][level] for part in parts], *packs)


def scale_kernel(levels, block, message, reply, *refs):
    many = len(levels)
    mines, others = refs[:many], refs[many:2 * many]
    mean, moment, a_buf, b_buf, load_sem, store_sem = refs[-6:]
    parts = [(k, slice(start, start + block)) for k in range(many) for start in range(0, HALF, block)]
    loads, stores = [], []
    for at, (k, part) in enumerate(parts):
        loads.append([pltpu.make_async_copy(mines[k].at[part], a_buf.at[k, part], load_sem.at[2 * at]),
                      pltpu.make_async_copy(others[k].at[part], b_buf.at[k, part], load_sem.at[2 * at + 1])])
        group = []
        for place in range(2):
            first = 8 * levels[k] if place == 0 else ROWS - 8 - 8 * levels[k]
            rows = slice(first, first + 8)
            for which, (fields, out) in enumerate(((slice(0, 2), mean), (slice(2, 5), moment))):
                group.append(pltpu.make_async_copy(
                    a_buf.at[k, part, fields, place], out.at[part, :, rows], store_sem.at[4 * at + 2 * place + which]))
        stores.append(group)
    for copies in loads:
        for copy in copies:
            copy.start()
    for at, (k, part) in enumerate(parts):
        for copy in loads[at]:
            copy.wait()

        def one(p, carry, k=k):
            count = jnp.full((8, WIDTH), message[0, p] + reply[0, HALF + p], I32).astype(F32)
            a_buf[k, p] = (a_buf[k, p] + b_buf[k, p]) * (1.0 / jnp.maximum(count, 1.0))
            return carry

        lax.fori_loop(part.start, part.stop, one, 0, unroll=2)
        for copy in stores[at]:
            copy.start()
    for copies in stores:
        for copy in copies:
            copy.wait()


def scale_levels(levels, counts, pairs, before):
    block = 18
    many = len(levels)
    parts = many * HALF // block
    smem = pl.BlockSpec(memory_space=pltpu.SMEM)
    hbm = pl.BlockSpec(memory_space=pltpu.HBM)
    buffer = pltpu.VMEM((many, HALF, 5, 2, 8, WIDTH), F32)
    return pl.pallas_call(
        functools.partial(scale_kernel, levels, block),
        in_specs=[smem] * 2 + [hbm] * (2 * many + len(before)),
        out_specs=[hbm] * 2,
        out_shape=[jax.ShapeDtypeStruct((HALF, 2, ROWS, WIDTH), F32), jax.ShapeDtypeStruct((HALF, 3, ROWS, WIDTH), F32)],
        scratch_shapes=[buffer, buffer, pltpu.SemaphoreType.DMA((2 * parts,)), pltpu.SemaphoreType.DMA((4 * parts,))],
        input_output_aliases={2 + 2 * many: 0, 3 + 2 * many: 1} if before else {},
        compiler_params=pltpu.CompilerParams(vmem_limit_bytes=(2 + 6 * many) * MIB),
        name="scale_levels",
    )(*counts, *[pair[0] for pair in pairs], *[pair[1] for pair in pairs], *before)


def exchange_kernel(up, dn, theirs, message, below, above, other, reply, send_sem, recv_sem):
    snap, tile = lax.axis_index("snap"), lax.axis_index("tile")
    size = lax.axis_size("tile")
    to_up = (snap, lax.rem(tile + size - 1, size))
    to_dn = (snap, lax.rem(tile + 1, size))
    to_core = (1 - snap, tile)
    barrier = pltpu.get_barrier_semaphore()
    for target in (to_up, to_dn, to_core):
        pl.semaphore_signal(barrier, inc=1, device_id=target, device_id_type=pl.DeviceIdType.MESH)
    pl.semaphore_wait(barrier, 3)
    copies = []
    for source, landing, target in ((up, below, to_up), (dn, above, to_dn), (theirs, other, to_core), (message, reply, to_core)):
        copies.append(pltpu.make_async_remote_copy(
            src_ref=source, dst_ref=landing, send_sem=send_sem.at[len(copies)], recv_sem=recv_sem.at[len(copies)],
            device_id=target, device_id_type=pl.DeviceIdType.MESH))
    for copy in copies:
        copy.start()
    for copy in copies:
        copy.wait()


def exchange(up, dn, theirs, message):
    any_space = pl.BlockSpec(memory_space=pltpu.HBM)
    return pl.pallas_call(
        exchange_kernel,
        in_specs=[any_space] * 4,
        out_specs=[any_space] * 4,
        out_shape=[jax.ShapeDtypeStruct(value.shape, value.dtype) for value in (up, dn, theirs, message)],
        scratch_shapes=[pltpu.SemaphoreType.DMA((4,)), pltpu.SemaphoreType.DMA((4,))],
        compiler_params=pltpu.CompilerParams(collective_id=0, has_side_effects=True, vmem_limit_bytes=62 * MIB),
        name="exchange",
    )(up, dn, theirs, message)


def to_partner(value):
    return lax.ppermute(value, "snap", [(0, 1), (1, 0)])


def to_above(value):
    size = lax.axis_size("tile")
    return lax.ppermute(value, "tile", [(i + 1, i) for i in range(size - 1)])


def to_below(value):
    size = lax.axis_size("tile")
    return lax.ppermute(value, "tile", [(i, i + 1) for i in range(size - 1)])


def level_cuts(cuts, level):
    return cuts[:level + 1]


def send(up_pieces, dn_pieces):
    from_below = [to_above(piece) for piece in up_pieces]
    from_above = [to_below(piece) for piece in dn_pieces]
    return from_below, from_above


def per_device(velocity, offsets, phase):
    snap = lax.axis_index("snap")
    tile = lax.axis_index("tile")
    dy, dx = offsets[:, 0].astype(I32), offsets[:, 1].astype(I32)
    turned = lax.rem(phase.astype(I32) + PHASES - HALF * snap, PHASES)
    kind = jnp.where(tile == 0, 0, jnp.where(tile == lax.axis_size("tile") - 1, 2, 1)).astype(I32)
    meta = jnp.concatenate([dy, dx, turned, kind[None]])
    colop = jnp.asarray(column_constant())
    rowop = jnp.asarray(row_constant())
    onehot = (turned[:, None] == jnp.arange(PHASES, dtype=I32)[None, :]).astype(I32)
    own = jnp.sum(onehot, axis=0)

    smooth = functools.partial(smooth_part, velocity=velocity, colop=colop, rowop=rowop)

    def full(counts, *_):
        strips, sums, up, dn, positions, plan = smooth(2, meta, jnp.zeros((16,), I32), cuts=FULL_CUTS)
        below, above = send(up, dn)
        totals = [finish_level(level, meta, plan, [(positions, strips, FULL_CUTS, below, above)]) for level in range(3)]
        totals = [(mine, to_partner(theirs)) for mine, theirs in (sums, *totals)]
        before = scale_levels((3, 0), counts, totals[:2], ())
        return tuple(scale_levels((1, 2), counts, totals[2:], before))

    def last(counts, mine, other, mean, moment):
        return tuple(scale_levels((2,), counts, [(mine, other)], (mean, moment)))

    strips_a, _, up_a, dn_a, pos_a, plan = smooth(0, meta, jnp.zeros((16,), I32), cuts=FIRST_CUTS)
    below_a, above_a = send(up_a, dn_a)
    message = jnp.broadcast_to(jnp.concatenate([own, plan[8:], jnp.zeros((48,), I32)])[None], (8, 128))
    strips_b, sums, up_b, dn_b, pos_b, _ = smooth(1, meta, plan, cuts=REST_CUTS, early=(strips_a[3],))
    below_b, above_b, other, reply = exchange(up_b[0], dn_b[0], sums[1], message)
    (up_b, dn_b), here, below_b, above_b, other = lax.optimization_barrier(((up_b[1], dn_b[1]), meta, below_b, above_b, other))
    more = send([up_b], [dn_b])
    counts = (message, reply)
    over = jnp.max(jnp.maximum(message, reply)[0:1, PHASES:PHASES + 8])
    parts = [(pos_a, strips_a, FIRST_CUTS, below_a, above_a),
             (pos_b, strips_b, REST_CUTS, [below_b, *more[0]], [above_b, *more[1]])]
    totals = [finish_level(0, here, plan, parts)]
    totals[0], other = lax.optimization_barrier((tuple(totals[0]), other))
    before = scale_levels((3,), counts, [(sums[0], other)], ())
    totals[0] = (totals[0][0], to_partner(totals[0][1]))
    before = scale_levels((0,), counts, totals[:1], before)
    here, before = lax.optimization_barrier((here, tuple(before)))
    totals = [finish_level(level, here, plan, parts) for level in (1, 2)]
    totals = [(mine, to_partner(theirs)) for mine, theirs in totals]
    before = scale_levels((1,), counts, totals[:1], before)
    return lax.cond(over <= 0, last, full, counts, *totals[1], *before)


def solution(mesh):
    in_specs = (P("snap", None, "tile", None), P("snap", None), P("snap"))
    out_specs = (P("snap", None, "tile", None), P("snap", None, "tile", None))
    return jax.shard_map(
        per_device, mesh=mesh, in_specs=in_specs, out_specs=out_specs, check_vma=False
    )
```

```python
import functools

import jax
import jax.numpy as jnp
import numpy as np
from jax import lax
from jax.experimental import pallas as pl
from jax.experimental.pallas import tpu as pltpu
from jax.sharding import PartitionSpec as P

PHASES = 72
HALF = PHASES // 2
RAD = 8
MAXS = 16
HALO = RAD + MAXS
ROWS = 64
WIDTH = 256
SNAPS = 128
EXT = ROWS + 2 * HALO
GROUP = 8
CHUNK = 128
BLOCK = 18
SPLIT = 6
GAP = 16
MIB = 1024 * 1024
FIRST_CUTS = (640,)
REST_CUTS = (1008,)
FULL_CUTS = (3072 + 64,)
GROUPS = SNAPS // 8
F32 = jnp.float32
BF16 = jnp.bfloat16
I32 = jnp.int32


def taps():
    steps = np.arange(2 * RAD + 1, dtype=np.float64) - RAD
    sigma = RAD / 2.0
    values = np.exp(-steps * steps / (2.0 * sigma * sigma))
    return values / values.sum()


def split_const(values):
    high = values.astype(BF16)
    low = (values - high.astype(np.float64)).astype(BF16)
    return high, low


def column_constant():
    weight = taps()
    source = np.arange(WIDTH)[:, None]
    target = np.arange(WIDTH)[None, :]
    distance = source - target
    band = np.where(np.abs(distance) <= RAD, weight[np.clip(distance + RAD, 0, 2 * RAD)], 0.0)
    high, low = split_const(band)
    return np.concatenate([high, low, high], axis=0)


def row_constant():
    weight = taps()
    target = np.arange(EXT)[None, :, None] - HALO
    source = np.arange(ROWS)[None, None, :]
    shift = np.arange(-MAXS, MAXS + 1)[:, None, None]
    distance = source - shift - target
    band = np.where(np.abs(distance) <= RAD, weight[np.clip(distance + RAD, 0, 2 * RAD)], 0.0)
    seen = source - shift
    kinds = []
    for kind in range(3):
        keep = np.ones_like(seen, dtype=bool)
        if kind == 0:
            keep = seen >= 0
        if kind == 2:
            keep = seen < ROWS
        high, low = split_const(np.where(keep, band, 0.0))
        kinds.append(np.concatenate([high, low, high], axis=2))
    return np.stack(kinds)


def level_rows(need, level):
    return jnp.clip(need - 8 * level, 0, 8)


def needs(dy):
    return jnp.clip(RAD + dy, 0, HALO), jnp.clip(RAD - dy, 0, HALO)


def next_start(end):
    return (end & -8) + 16


def split(value):
    high = value.astype(BF16)
    return high, (value - high.astype(F32)).astype(BF16)


def smooth_kernel(part, cuts, meta, plan, *refs):
    pieces = len(cuts)
    vel, colop, rowop, refs = *refs[:3], refs[3:]
    if part == 1:
        early, refs = refs[0], refs[1:]
    strips = 3 if part else 4
    y_refs, refs = refs[:strips], refs[strips:]
    if part:
        mine, theirs, refs = refs[0], refs[1], refs[2:]
    out_up, out_dn = refs[:pieces], refs[pieces:2 * pieces]
    pos_ref, plan_ref, refs = *refs[2 * pieces:2 * pieces + 2], refs[2 * pieces + 2:]
    vel_buf, oper_buf, col_buf, refs = *refs[:3], refs[3:]
    y_bufs, refs = refs[:4], refs[4:]
    if part:
        acc, refs = refs[0], refs[1:]
    xs, stack, up, dn, cursor, load_sem, store_sem, sem = refs
    row = lax.broadcasted_iota(I32, (8, WIDTH), 0)
    lane = lax.broadcasted_iota(I32, (1, WIDTH), 1)
    dot = functools.partial(jnp.dot, preferred_element_type=F32)

    def load(g):
        rows = pl.ds(GROUP * g, GROUP)
        return pltpu.make_async_copy(vel.at[rows], vel_buf.at[rows], load_sem.at[g])

    def store(g, level):
        rows = pl.ds(GROUP * g, GROUP)
        return pltpu.make_async_copy(y_bufs[level].at[rows], y_refs[level].at[rows], store_sem.at[g, level])

    def load_early(g):
        rows = pl.ds(GROUP * g, GROUP)
        return pltpu.make_async_copy(early.at[rows], y_bufs[3].at[rows], store_sem.at[g, 3])

    def add_fields(n, place, u, v):
        phase = meta[2 * SNAPS + n]
        for at_field, field in enumerate((u, v, u * u, v * v, u * v)):
            acc[phase, at_field, place] += field

    def loop(low, high, body):
        lax.fori_loop(low, high, lambda g, carry: (body(g), carry)[1], 0)

    def ends(sums):
        starts, stops = [], []
        for side in range(2):
            start = I32(0)
            for level in range(3):
                starts.append(start)
                start = next_start(start + sums[3 * side + level])
                stops.append(start)
        return starts, stops

    def count_group(g, sums):
        for b in range(GROUP):
            sums = list(sums)
            for side, need in enumerate(needs(meta[GROUP * g + b])):
                for level in range(3):
                    sums[3 * side + level] += level_rows(need, level)
        return tuple(sums)

    tables = [pltpu.make_async_copy(colop, col_buf, sem.at[0]),
              pltpu.make_async_copy(rowop.at[meta[3 * SNAPS]], oper_buf, sem.at[1])]
    zero = (I32(0),) * 6
    if part == 0:
        load(0).start()
        for copy in tables:
            copy.start()
        for g in range(1, 4):
            load(g).start()

        def add_group(g, carry):
            sums, taken, count, going = carry
            sums = count_group(g, sums)
            stops = ends(sums)[1]
            going = going & (jnp.maximum(stops[2], stops[5]) <= cuts[-1]).astype(I32)
            taken = tuple(jnp.where(going > 0, new, old) for new, old in zip(sums, taken))
            return sums, taken, count + going, going

        sums, taken, count, _ = lax.fori_loop(0, GROUPS, add_group, (zero, zero, I32(0), I32(1)))
        begin, end = I32(0), count
        starts = ends(taken)[0]
        rest_starts, rest_stops = ends([whole - some for whole, some in zip(sums, taken)])
        over = I32(0)
        for side in range(2):
            for level in range(3):
                limit = level_cuts(REST_CUTS, level)[-1]
                over = jnp.maximum(over, rest_stops[3 * side + level] - limit)
        for k in range(8):
            plan_ref[k] = rest_starts[k] if k < 6 else count
            plan_ref[8 + k] = over
        loop(4, end, lambda g: load(g).start())
    elif part == 1:
        begin, end = plan[6], I32(GROUPS)
        loop(begin, end, lambda g: load(g).start())
        for copy in tables:
            copy.start()
        loop(0, begin, lambda g: load_early(g).start())
        starts = [plan[k] for k in range(6)]
    else:
        begin, end = I32(0), I32(GROUPS)
        loop(begin, end, lambda g: load(g).start())
        for copy in tables:
            copy.start()
        starts = ends(lax.fori_loop(0, GROUPS, count_group, zero))[0]
    if part:
        acc[...] = jnp.zeros_like(acc)
        for k in range(16):
            plan_ref[k] = I32(GROUPS)
    for k in range(6):
        cursor[k] = starts[k]
    for copy in tables:
        copy.wait()

    def group(g):
        load(g).wait()
        for b in range(GROUP):
            n = GROUP * g + b
            dx = meta[SNAPS + n]
            rolled = pltpu.roll(vel_buf[n].reshape(2 * ROWS, WIDTH), (WIDTH - dx) & (WIDTH - 1), 1)
            moved = lane + dx
            high, low = split(jnp.where((moved >= 0) & (moved < WIDTH), rolled, 0.0))
            rows = slice(2 * ROWS * b, 2 * ROWS * (b + 1))
            xs[rows, 0:WIDTH] = high
            xs[rows, WIDTH:2 * WIDTH] = high
            xs[rows, 2 * WIDTH:3 * WIDTH] = low
        high, low = split(dot(xs[...], col_buf[...]))
        for b in range(GROUP):
            for comp in range(2):
                rows = slice(ROWS * (2 * b + comp), ROWS * (2 * b + comp + 1))
                stack[b, comp, 0:ROWS] = high[rows]
                stack[b, comp, ROWS:2 * ROWS] = high[rows]
                stack[b, comp, 2 * ROWS:3 * ROWS] = low[rows]
        for b in range(GROUP):
            n = GROUP * g + b
            oper = oper_buf[meta[n] + MAXS]
            ext = [dot(oper, stack[b, comp]) for comp in range(2)]
            for level in range(strips):
                for comp in range(2):
                    top = HALO + 8 * level
                    bottom = HALO + ROWS - 8 - 8 * level
                    y_bufs[level][n, 0, comp] = ext[comp][top:top + 8]
                    y_bufs[level][n, 1, comp] = ext[comp][bottom:bottom + 8]
            if part:
                for place in range(2):
                    rows = slice(2 * HALO + 8 * place, 2 * HALO + 8 * place + 8)
                    add_fields(n, place, ext[0][rows], ext[1][rows])
            for side, need in enumerate(needs(meta[n])):
                buffer = (up, dn)[side]
                for level in range(3):
                    slot = 3 * side + level
                    have = level_rows(need, level)
                    here = cursor[slot]
                    cursor[slot] = here + have
                    pos = jnp.minimum(here, cuts[-1] - 16)
                    pos_ref[6 * n + slot] = pos
                    skew = pos & 7
                    base = pl.multiple_of(pos - skew, 8)
                    source = 16 - 8 * level if side == 0 else HALO + ROWS + 8 * level
                    turn = (skew + have) & 7 if side == 0 else skew
                    for comp in range(2):
                        tile = pltpu.roll(ext[comp][source:source + 8], turn, 0)
                        old = buffer[comp, pl.ds(base, 8)]
                        buffer[comp, pl.ds(base, 8)] = jnp.where(row < skew, old, tile)
                        buffer[comp, pl.ds(base + 8, 8)] = tile
        for level in range(strips):
            store(g, level).start()

    loop(begin, end, group)
    copies = []
    low = 0
    for piece, high in enumerate(cuts):
        for side in range(2):
            copies.append(pltpu.make_async_copy(
                (up, dn)[side].at[:, low:high], (out_up, out_dn)[side][piece], sem.at[2 + len(copies)]))
        low = high
    for copy in copies:
        copy.start()
    if part:
        def add_early(g):
            load_early(g).wait()
            for n in range(GROUP):
                for place in range(2):
                    add_fields(GROUP * g + n, place, y_bufs[3][GROUP * g + n, place, 0], y_bufs[3][GROUP * g + n, place, 1])

        if part == 1:
            loop(0, begin, add_early)
        sums_out = [pltpu.make_async_copy(acc.at[HALF:PHASES], theirs, sem.at[2 + len(copies)]),
                    pltpu.make_async_copy(acc.at[0:HALF], mine, sem.at[3 + len(copies)])]
        for copy in sums_out:
            copy.start()
        copies += sums_out
    else:
        for g in range(4):
            pl.when(g >= end)(load(g).wait)

    def stored(g):
        for level in range(strips):
            store(g, level).wait()

    loop(begin, end, stored)
    for copy in copies:
        copy.wait()


def smooth_part(part, meta, plan, velocity, colop, rowop, cuts, early=()):
    pieces = len(cuts)
    sizes = [high - low for low, high in zip((0,) + cuts[:-1], cuts)]
    any_space = pl.BlockSpec(memory_space=pltpu.HBM)
    smem = pl.BlockSpec(memory_space=pltpu.SMEM)
    piece_shapes = [jax.ShapeDtypeStruct((2, size, WIDTH), F32) for size in sizes]
    strip = jax.ShapeDtypeStruct((SNAPS, 2, 2, 8, WIDTH), F32)
    room = cuts[-1] + GAP
    total = jax.ShapeDtypeStruct((HALF, 5, 2, 8, WIDTH), F32)
    strips, sums = (3, 2) if part else (4, 0)
    out = pl.pallas_call(
        functools.partial(smooth_kernel, part, cuts),
        in_specs=[smem] * 2 + [any_space] * (3 + len(early)),
        out_specs=[any_space] * (strips + sums + 2 * pieces) + [smem, smem],
        scratch_shapes=[
            pltpu.VMEM((SNAPS, 2, ROWS, WIDTH), F32),
            pltpu.VMEM((2 * MAXS + 1, EXT, 3 * ROWS), BF16),
            pltpu.VMEM((3 * WIDTH, WIDTH), BF16),
        ] + [pltpu.VMEM((SNAPS, 2, 2, 8, WIDTH), F32)] * 4
        + ([pltpu.VMEM((PHASES, 5, 2, 8, WIDTH), F32)] if part else []) + [
            pltpu.VMEM((GROUP * 2 * ROWS, 3 * WIDTH), BF16),
            pltpu.VMEM((GROUP, 2, 3 * ROWS, WIDTH), BF16),
            pltpu.VMEM((2, room, WIDTH), F32),
            pltpu.VMEM((2, room, WIDTH), F32),
            pltpu.SMEM((8,), I32),
            pltpu.SemaphoreType.DMA((GROUPS,)),
            pltpu.SemaphoreType.DMA((GROUPS, 4)),
            pltpu.SemaphoreType.DMA((4 + 2 * pieces,)),
        ],
        out_shape=[strip] * strips + [total] * sums + piece_shapes * 2
        + [jax.ShapeDtypeStruct((SNAPS * 6,), I32), jax.ShapeDtypeStruct((16,), I32)],
        compiler_params=pltpu.CompilerParams(vmem_limit_bytes=62 * MIB),
        name="smooth_part",
    )(meta, plan, velocity, colop, rowop, *early)
    packs = out[strips + sums:]
    return out[:strips], out[strips:strips + sums], packs[:pieces], packs[pieces:2 * pieces], out[-2], out[-1]


def finish_kernel(levels, cuts, meta, plan, *refs):
    parts, many = len(cuts), len(levels)
    pos_refs, refs = refs[:parts], refs[parts:]
    strips, refs = [refs[many * k:many * (k + 1)] for k in range(parts)], refs[many * parts:]
    pieces = []
    for k in range(parts):
        count = len(cuts[k])
        pieces.append((refs[:count], refs[count:2 * count]))
        refs = refs[2 * count:]
    outs, refs = refs[:2 * many], refs[2 * many:]
    acc, y_buf, *buffers, y_sem, out_sem, sem = refs
    middle = plan[6] if parts == 2 else I32(GROUPS)
    ranges = [(I32(0), middle), (middle, I32(GROUPS))][:parts]

    def loop(low, high, body):
        lax.fori_loop(low, high, lambda g, carry: (body(g), carry)[1], 0)

    def load(k, g, at):
        rows = pl.ds(GROUP * g, GROUP)
        return pltpu.make_async_copy(strips[k][at].at[rows], y_buf.at[at, rows], y_sem.at[at, g])

    packs = [[] for _ in range(parts)]
    total = 0
    for k in range(parts):
        low = 0
        first, last = ranges[k]
        for piece, high in enumerate(cuts[k]):
            for side in range(2):
                begin = pos_refs[k][6 * GROUP * jnp.minimum(first, GROUPS - 1) + 3 * side + levels[0]]
                end = pos_refs[k][6 * (GROUP * jnp.maximum(last, 1) - 1) + 3 * side + levels[-1]] + 16
                for row_at in range(low, high, CHUNK):
                    stop = min(row_at + CHUNK, high)
                    copy = pltpu.make_async_copy(
                        pieces[k][side][piece].at[:, row_at - low:stop - low],
                        buffers[2 * k + side].at[:, row_at:stop], sem.at[total])
                    total += 1
                    packs[k].append((copy, (first < last) & (begin < stop) & (end > row_at)))
            low = high
    for at in range(many):
        for k in range(parts):
            if at == 0:
                for copy, needed in packs[k]:
                    pl.when(needed)(copy.start)
            loop(*ranges[k], lambda g, k=k, at=at: load(k, g, at).start())
    row = lax.broadcasted_iota(I32, (8, WIDTH), 0)

    def one(n, k, at):
        phase = meta[2 * SNAPS + n]
        for place in range(2):
            side = 1 - place
            have = level_rows(needs(meta[n])[side], levels[at])
            pos = pos_refs[k][6 * n + 3 * side + levels[at]]
            skew = pos & 7
            base = pl.multiple_of(pos - skew, 8)
            turn = skew if place == 0 else (skew + have) & 7
            known = jnp.where(meta[3 * SNAPS] == 2 * place, 0, have)
            keep = row < known if place == 0 else row >= 8 - known
            fields = []
            for comp in range(2):
                lower = buffers[2 * k + side][comp, pl.ds(base, 8)]
                upper = buffers[2 * k + side][comp, pl.ds(base + 8, 8)]
                tile = pltpu.roll(jnp.where(row >= skew, lower, upper), (8 - turn) & 7, 0)
                fields.append(y_buf[at, n, place, comp] + jnp.where(keep, tile, 0.0))
            u, v = fields
            for at_field, field in enumerate((u, v, u * u, v * v, u * v)):
                acc[at, phase, at_field, place] += field

    def group(g, k, at):
        load(k, g, at).wait()
        for b in range(GROUP):
            one(GROUP * g + b, k, at)

    stores = []
    for at in range(many):
        acc[at] = jnp.zeros(acc.shape[1:], F32)
        for k in range(parts):
            if at == 0:
                for copy, needed in packs[k]:
                    pl.when(needed)(copy.wait)
            loop(*ranges[k], lambda g, k=k, at=at: group(g, k, at))
        for which, part in enumerate((slice(0, HALF), slice(HALF, PHASES))):
            stores.append(pltpu.make_async_copy(acc.at[at, part], outs[2 * at + which], out_sem.at[len(stores)]))
            stores[-1].start()
    for copy in stores:
        copy.wait()


def finish_levels(levels, meta, plan, parts):
    any_space = pl.BlockSpec(memory_space=pltpu.HBM)
    smem = pl.BlockSpec(memory_space=pltpu.SMEM)
    shape = jax.ShapeDtypeStruct((HALF, 5, 2, 8, WIDTH), F32)
    many = len(levels)
    cuts = [part[2] for part in parts]
    strips = [part[1][level] for part in parts for level in levels]
    packs = [piece for part in parts for side in part[3:5] for piece in side]
    chunks = sum(2 * (-(-(high - low) // CHUNK)) for some in cuts for low, high in zip((0,) + some[:-1], some))
    out = pl.pallas_call(
        functools.partial(finish_kernel, levels, cuts),
        in_specs=[smem] * (2 + len(parts)) + [any_space] * (len(strips) + len(packs)),
        out_specs=[any_space] * (2 * many),
        out_shape=[shape] * (2 * many),
        scratch_shapes=[
            pltpu.VMEM((many, PHASES, 5, 2, 8, WIDTH), F32),
            pltpu.VMEM((many, SNAPS, 2, 2, 8, WIDTH), F32),
        ] + [pltpu.VMEM((2, some[-1] + GAP, WIDTH), F32) for some in cuts for _ in range(2)] + [
            pltpu.SemaphoreType.DMA((many, GROUPS)),
            pltpu.SemaphoreType.DMA((2 * many,)),
            pltpu.SemaphoreType.DMA((chunks,)),
        ],
        compiler_params=pltpu.CompilerParams(vmem_limit_bytes=62 * MIB),
        name="finish_levels",
    )(meta, plan, *[part[0] for part in parts], *strips, *packs)
    return [(out[2 * at], out[2 * at + 1]) for at in range(many)]


def scale_work(levels, message, reply, mines, others, mean, moment, a_buf, b_buf, load_sem, store_sem):
    many = len(levels)
    parts = [(k, slice(start, start + BLOCK)) for k in range(many) for start in range(0, HALF, BLOCK)]
    loads, stores = [], []
    for at, (k, part) in enumerate(parts):
        loads.append([pltpu.make_async_copy(mines[k].at[part], a_buf.at[k, part], load_sem.at[2 * at]),
                      pltpu.make_async_copy(others[k].at[part], b_buf.at[k, part], load_sem.at[2 * at + 1])])
        group = []
        for place in range(2):
            first = 8 * levels[k] if place == 0 else ROWS - 8 - 8 * levels[k]
            rows = slice(first, first + 8)
            for which, (fields, out) in enumerate(((slice(0, 2), mean), (slice(2, 5), moment))):
                group.append(pltpu.make_async_copy(
                    a_buf.at[k, part, fields, place], out.at[part, :, rows], store_sem.at[4 * at + 2 * place + which]))
        stores.append(group)

    def begin():
        for copies in loads:
            for copy in copies:
                copy.start()

    def work():
        for at, (k, part) in enumerate(parts):
            for copy in loads[at]:
                copy.wait()

            def one(p, carry, k=k):
                count = jnp.full((8, WIDTH), message[0, p] + reply[0, HALF + p], I32).astype(F32)
                a_buf[k, p] = (a_buf[k, p] + b_buf[k, p]) * (1.0 / jnp.maximum(count, 1.0))
                return carry

            lax.fori_loop(part.start, part.stop, one, 0, unroll=2)
            for copy in stores[at]:
                copy.start()

    def end():
        for copies in stores:
            for copy in copies:
                copy.wait()

    return begin, work, end


def scale_scratch(many):
    parts = many * HALF // BLOCK
    buffer = pltpu.VMEM((many, HALF, 5, 2, 8, WIDTH), F32)
    return [buffer, buffer, pltpu.SemaphoreType.DMA((2 * parts,)), pltpu.SemaphoreType.DMA((4 * parts,))]


OUTPUTS = [jax.ShapeDtypeStruct((HALF, 2, ROWS, WIDTH), F32), jax.ShapeDtypeStruct((HALF, 3, ROWS, WIDTH), F32)]


def scale_kernel(levels, message, reply, *refs):
    many = len(levels)
    for step in scale_work(levels, message, reply, refs[:many], refs[many:2 * many], *refs[-6:]):
        step()


def scale_levels(levels, counts, pairs, before):
    many = len(levels)
    smem = pl.BlockSpec(memory_space=pltpu.SMEM)
    hbm = pl.BlockSpec(memory_space=pltpu.HBM)
    return pl.pallas_call(
        functools.partial(scale_kernel, levels),
        in_specs=[smem] * 2 + [hbm] * (2 * many + len(before)),
        out_specs=[hbm] * 2,
        out_shape=OUTPUTS,
        scratch_shapes=scale_scratch(many),
        input_output_aliases={2 + 2 * many: 0, 3 + 2 * many: 1} if before else {},
        compiler_params=pltpu.CompilerParams(vmem_limit_bytes=62 * MIB),
        name="scale_levels",
    )(*counts, *[pair[0] for pair in pairs], *[pair[1] for pair in pairs], *before)


def exchange_kernel(up, dn, theirs, message, below, above, other, reply, send_sem, recv_sem):
    snap, tile = lax.axis_index("snap"), lax.axis_index("tile")
    size = lax.axis_size("tile")
    to_up = (snap, lax.rem(tile + size - 1, size))
    to_dn = (snap, lax.rem(tile + 1, size))
    to_core = (1 - snap, tile)
    barrier = pltpu.get_barrier_semaphore()
    for target in (to_up, to_dn, to_core):
        pl.semaphore_signal(barrier, inc=1, device_id=target, device_id_type=pl.DeviceIdType.MESH)
    pl.semaphore_wait(barrier, 3)
    rows = up.shape[1] // SPLIT
    moves = [(theirs, other, to_core), (message, reply, to_core)]
    for at in range(SPLIT):
        part = slice(rows * at, rows * (at + 1))
        moves += [(up.at[:, part], below.at[:, part], to_up), (dn.at[:, part], above.at[:, part], to_dn)]
    copies = []
    for source, landing, target in moves:
        copies.append(pltpu.make_async_remote_copy(
            src_ref=source, dst_ref=landing, send_sem=send_sem.at[len(copies)], recv_sem=recv_sem.at[len(copies)],
            device_id=target, device_id_type=pl.DeviceIdType.MESH))
    for copy in copies:
        copy.start()
    for copy in copies:
        copy.wait()


def exchange(up, dn, theirs, message):
    any_space = pl.BlockSpec(memory_space=pltpu.HBM)
    return pl.pallas_call(
        exchange_kernel,
        in_specs=[any_space] * 4,
        out_specs=[any_space] * 4,
        out_shape=[jax.ShapeDtypeStruct(value.shape, value.dtype) for value in (up, dn, theirs, message)],
        scratch_shapes=[pltpu.SemaphoreType.DMA((2 + 2 * SPLIT,)), pltpu.SemaphoreType.DMA((2 + 2 * SPLIT,))],
        compiler_params=pltpu.CompilerParams(collective_id=0, has_side_effects=True, vmem_limit_bytes=62 * MIB),
        name="exchange",
    )(up, dn, theirs, message)


def to_partner(value):
    return lax.ppermute(value, "snap", [(0, 1), (1, 0)])


def to_above(value):
    size = lax.axis_size("tile")
    return lax.ppermute(value, "tile", [(i + 1, i) for i in range(size - 1)])


def to_below(value):
    size = lax.axis_size("tile")
    return lax.ppermute(value, "tile", [(i, i + 1) for i in range(size - 1)])


def level_cuts(cuts, level):
    return cuts[:level + 1]


def send(up_pieces, dn_pieces):
    from_below = [to_above(piece) for piece in up_pieces]
    from_above = [to_below(piece) for piece in dn_pieces]
    return from_below, from_above


def per_device(velocity, offsets, phase):
    snap = lax.axis_index("snap")
    tile = lax.axis_index("tile")
    dy, dx = offsets[:, 0].astype(I32), offsets[:, 1].astype(I32)
    turned = lax.rem(phase.astype(I32) + PHASES - HALF * snap, PHASES)
    kind = jnp.where(tile == 0, 0, jnp.where(tile == lax.axis_size("tile") - 1, 2, 1)).astype(I32)
    meta = jnp.concatenate([dy, dx, turned, kind[None]])
    colop = jnp.asarray(column_constant())
    rowop = jnp.asarray(row_constant())
    onehot = (turned[:, None] == jnp.arange(PHASES, dtype=I32)[None, :]).astype(I32)
    own = jnp.sum(onehot, axis=0)

    smooth = functools.partial(smooth_part, velocity=velocity, colop=colop, rowop=rowop)

    def full(counts, *_):
        strips, sums, up, dn, positions, plan = smooth(2, meta, meta, cuts=FULL_CUTS)
        below, above = send(up, dn)
        part = (positions, strips, FULL_CUTS, below, above)
        totals = finish_levels((0, 1), meta, plan, [part]) + finish_levels((2,), meta, plan, [part])
        totals = [(mine, to_partner(theirs)) for mine, theirs in (sums, *totals)]
        before = scale_levels((3, 0), counts, totals[:2], ())
        return tuple(scale_levels((1, 2), counts, totals[2:], before))

    def last(counts, mine, other, mean, moment):
        return tuple(scale_levels((2,), counts, [(mine, other)], (mean, moment)))

    strips_a, _, up_a, dn_a, pos_a, plan = smooth(0, meta, meta, cuts=FIRST_CUTS)
    below_a, above_a = send(up_a, dn_a)
    message = jnp.broadcast_to(jnp.concatenate([own, plan[8:], jnp.zeros((48,), I32)])[None], (8, 128))
    strips_b, sums, up_b, dn_b, pos_b, _ = smooth(1, meta, plan, cuts=REST_CUTS, early=(strips_a[3],))
    below_b, above_b, other, reply = exchange(up_b[0], dn_b[0], sums[1], message)
    counts = (message, reply)
    over = jnp.max(jnp.maximum(message, reply)[0:1, PHASES:PHASES + 8])
    parts = [(pos_a, strips_a, FIRST_CUTS, below_a, above_a), (pos_b, strips_b, REST_CUTS, [below_b], [above_b])]
    totals = finish_levels((0, 1), meta, plan, parts) + finish_levels((2,), meta, plan, parts)
    totals = [(mine, to_partner(theirs)) for mine, theirs in totals]
    before = scale_levels((3,), counts, [(sums[0], other)], ())
    before = scale_levels((0, 1), counts, totals[:2], before)
    return lax.cond(over <= 0, last, full, counts, *totals[2], *before)


def solution(mesh):
    in_specs = (P("snap", None, "tile", None), P("snap", None), P("snap"))
    out_specs = (P("snap", None, "tile", None), P("snap", None, "tile", None))
    return jax.shard_map(
        per_device, mesh=mesh, in_specs=in_specs, out_specs=out_specs, check_vma=False
    )
```

```python
import functools

import jax
import jax.numpy as jnp
import numpy as np
from jax import lax
from jax.experimental import pallas as pl
from jax.experimental.pallas import tpu as pltpu
from jax.sharding import PartitionSpec as P

PHASES = 72
HALF = PHASES // 2
RAD = 8
MAXS = 16
HALO = RAD + MAXS
ROWS = 64
WIDTH = 256
SNAPS = 128
EXT = ROWS + 2 * HALO
GROUP = 8
CHUNK = 128
BLOCK = 18
SPLIT = 4
GAP = 16
MIB = 1024 * 1024
FIRST_CUTS = (576,)
REST_CUTS = (1024,)
FULL_CUTS = (3072 + 64,)
GROUPS = SNAPS // 8
F32 = jnp.float32
BF16 = jnp.bfloat16
I32 = jnp.int32


def taps():
    steps = np.arange(2 * RAD + 1, dtype=np.float64) - RAD
    sigma = RAD / 2.0
    values = np.exp(-steps * steps / (2.0 * sigma * sigma))
    return values / values.sum()


def split_const(values):
    high = values.astype(BF16)
    low = (values - high.astype(np.float64)).astype(BF16)
    return high, low


def column_constant():
    weight = taps()
    source = np.arange(WIDTH)[:, None]
    target = np.arange(WIDTH)[None, :]
    distance = source - target
    band = np.where(np.abs(distance) <= RAD, weight[np.clip(distance + RAD, 0, 2 * RAD)], 0.0)
    high, low = split_const(band)
    return np.concatenate([high, low, high], axis=0)


def row_constant():
    weight = taps()
    target = np.arange(EXT)[None, :, None] - HALO
    source = np.arange(ROWS)[None, None, :]
    shift = np.arange(-MAXS, MAXS + 1)[:, None, None]
    distance = source - shift - target
    band = np.where(np.abs(distance) <= RAD, weight[np.clip(distance + RAD, 0, 2 * RAD)], 0.0)
    seen = source - shift
    kinds = []
    for kind in range(3):
        keep = np.ones_like(seen, dtype=bool)
        if kind == 0:
            keep = seen >= 0
        if kind == 2:
            keep = seen < ROWS
        high, low = split_const(np.where(keep, band, 0.0))
        kinds.append(np.concatenate([high, low, high], axis=2))
    return np.stack(kinds)


def level_rows(need, level):
    return jnp.clip(need - 8 * level, 0, 8)


def needs(dy):
    return jnp.clip(RAD + dy, 0, HALO), jnp.clip(RAD - dy, 0, HALO)


def next_start(end):
    return (end & -8) + 16


def split(value):
    high = value.astype(BF16)
    return high, (value - high.astype(F32)).astype(BF16)


def smooth_kernel(part, cuts, meta, plan, *refs):
    pieces = len(cuts)
    vel, colop, rowop, refs = *refs[:3], refs[3:]
    if part == 1:
        early, refs = refs[0], refs[1:]
    strips = 3 if part else 4
    y_refs, refs = refs[:strips], refs[strips:]
    if part:
        mine, theirs, refs = refs[0], refs[1], refs[2:]
    out_up, out_dn = refs[:pieces], refs[pieces:2 * pieces]
    pos_ref, plan_ref, refs = *refs[2 * pieces:2 * pieces + 2], refs[2 * pieces + 2:]
    vel_buf, oper_buf, col_buf, refs = *refs[:3], refs[3:]
    y_bufs, refs = refs[:4], refs[4:]
    if part:
        acc, refs = refs[0], refs[1:]
    xs, stack, up, dn, cursor, load_sem, store_sem, sem = refs
    row = lax.broadcasted_iota(I32, (8, WIDTH), 0)
    lane = lax.broadcasted_iota(I32, (1, WIDTH), 1)
    dot = functools.partial(jnp.dot, preferred_element_type=F32)

    def load(g):
        rows = pl.ds(GROUP * g, GROUP)
        return pltpu.make_async_copy(vel.at[rows], vel_buf.at[rows], load_sem.at[g])

    def store(g, level):
        rows = pl.ds(GROUP * g, GROUP)
        return pltpu.make_async_copy(y_bufs[level].at[rows], y_refs[level].at[rows], store_sem.at[g, level])

    def load_early(g):
        rows = pl.ds(GROUP * g, GROUP)
        return pltpu.make_async_copy(early.at[rows], y_bufs[3].at[rows], store_sem.at[g, 3])

    def add_fields(n, place, u, v):
        phase = meta[2 * SNAPS + n]
        for at_field, field in enumerate((u, v, u * u, v * v, u * v)):
            acc[phase, at_field, place] += field

    def loop(low, high, body):
        lax.fori_loop(low, high, lambda g, carry: (body(g), carry)[1], 0)

    def ends(sums):
        starts, stops = [], []
        for side in range(2):
            start = I32(0)
            for level in range(3):
                starts.append(start)
                start = next_start(start + sums[3 * side + level])
                stops.append(start)
        return starts, stops

    def count_group(g, sums):
        for b in range(GROUP):
            sums = list(sums)
            for side, need in enumerate(needs(meta[GROUP * g + b])):
                for level in range(3):
                    sums[3 * side + level] += level_rows(need, level)
        return tuple(sums)

    tables = [pltpu.make_async_copy(colop, col_buf, sem.at[0]),
              pltpu.make_async_copy(rowop.at[meta[3 * SNAPS]], oper_buf, sem.at[1])]
    zero = (I32(0),) * 6
    if part == 0:
        load(0).start()
        for copy in tables:
            copy.start()
        for g in range(1, 4):
            load(g).start()

        def add_group(g, carry):
            sums, taken, count, going = carry
            sums = count_group(g, sums)
            stops = ends(sums)[1]
            going = going & (jnp.maximum(stops[2], stops[5]) <= cuts[-1]).astype(I32)
            taken = tuple(jnp.where(going > 0, new, old) for new, old in zip(sums, taken))
            return sums, taken, count + going, going

        sums, taken, count, _ = lax.fori_loop(0, GROUPS, add_group, (zero, zero, I32(0), I32(1)))
        begin, end = I32(0), count
        starts = ends(taken)[0]
        rest_starts, rest_stops = ends([whole - some for whole, some in zip(sums, taken)])
        over = I32(0)
        for side in range(2):
            for level in range(3):
                limit = level_cuts(REST_CUTS, level)[-1]
                over = jnp.maximum(over, rest_stops[3 * side + level] - limit)
        for k in range(8):
            plan_ref[k] = rest_starts[k] if k < 6 else count
            plan_ref[8 + k] = over
        loop(4, end, lambda g: load(g).start())
    elif part == 1:
        begin, end = plan[6], I32(GROUPS)
        loop(begin, end, lambda g: load(g).start())
        for copy in tables:
            copy.start()
        loop(0, begin, lambda g: load_early(g).start())
        starts = [plan[k] for k in range(6)]
    else:
        begin, end = I32(0), I32(GROUPS)
        loop(begin, end, lambda g: load(g).start())
        for copy in tables:
            copy.start()
        starts = ends(lax.fori_loop(0, GROUPS, count_group, zero))[0]
    if part:
        acc[...] = jnp.zeros_like(acc)
        for k in range(16):
            plan_ref[k] = I32(GROUPS)
    for k in range(6):
        cursor[k] = starts[k]
    for copy in tables:
        copy.wait()

    def group(g):
        load(g).wait()
        for b in range(GROUP):
            n = GROUP * g + b
            dx = meta[SNAPS + n]
            rolled = pltpu.roll(vel_buf[n].reshape(2 * ROWS, WIDTH), (WIDTH - dx) & (WIDTH - 1), 1)
            moved = lane + dx
            high, low = split(jnp.where((moved >= 0) & (moved < WIDTH), rolled, 0.0))
            rows = slice(2 * ROWS * b, 2 * ROWS * (b + 1))
            xs[rows, 0:WIDTH] = high
            xs[rows, WIDTH:2 * WIDTH] = high
            xs[rows, 2 * WIDTH:3 * WIDTH] = low
        high, low = split(dot(xs[...], col_buf[...]))
        for b in range(GROUP):
            for comp in range(2):
                rows = slice(ROWS * (2 * b + comp), ROWS * (2 * b + comp + 1))
                stack[b, comp, 0:ROWS] = high[rows]
                stack[b, comp, ROWS:2 * ROWS] = high[rows]
                stack[b, comp, 2 * ROWS:3 * ROWS] = low[rows]
        for b in range(GROUP):
            n = GROUP * g + b
            oper = oper_buf[meta[n] + MAXS]
            ext = [dot(oper, stack[b, comp]) for comp in range(2)]
            for level in range(strips):
                for comp in range(2):
                    top = HALO + 8 * level
                    bottom = HALO + ROWS - 8 - 8 * level
                    y_bufs[level][n, 0, comp] = ext[comp][top:top + 8]
                    y_bufs[level][n, 1, comp] = ext[comp][bottom:bottom + 8]
            if part:
                for place in range(2):
                    rows = slice(2 * HALO + 8 * place, 2 * HALO + 8 * place + 8)
                    add_fields(n, place, ext[0][rows], ext[1][rows])
            for side, need in enumerate(needs(meta[n])):
                buffer = (up, dn)[side]
                for level in range(3):
                    slot = 3 * side + level
                    have = level_rows(need, level)
                    here = cursor[slot]
                    cursor[slot] = here + have
                    pos = jnp.minimum(here, cuts[-1] - 16)
                    pos_ref[6 * n + slot] = pos
                    skew = pos & 7
                    base = pl.multiple_of(pos - skew, 8)
                    source = 16 - 8 * level if side == 0 else HALO + ROWS + 8 * level
                    turn = (skew + have) & 7 if side == 0 else skew
                    for comp in range(2):
                        tile = pltpu.roll(ext[comp][source:source + 8], turn, 0)
                        old = buffer[comp, pl.ds(base, 8)]
                        buffer[comp, pl.ds(base, 8)] = jnp.where(row < skew, old, tile)
                        buffer[comp, pl.ds(base + 8, 8)] = tile
        for level in range(strips):
            store(g, level).start()

    loop(begin, end, group)
    copies = []
    low = 0
    for piece, high in enumerate(cuts):
        for side in range(2):
            copies.append(pltpu.make_async_copy(
                (up, dn)[side].at[:, low:high], (out_up, out_dn)[side][piece], sem.at[2 + len(copies)]))
        low = high
    for copy in copies:
        copy.start()
    if part:
        def add_early(g):
            load_early(g).wait()
            for n in range(GROUP):
                for place in range(2):
                    add_fields(GROUP * g + n, place, y_bufs[3][GROUP * g + n, place, 0], y_bufs[3][GROUP * g + n, place, 1])

        if part == 1:
            loop(0, begin, add_early)
        sums_out = [pltpu.make_async_copy(acc.at[HALF:PHASES], theirs, sem.at[2 + len(copies)]),
                    pltpu.make_async_copy(acc.at[0:HALF], mine, sem.at[3 + len(copies)])]
        for copy in sums_out:
            copy.start()
        copies += sums_out
    else:
        for g in range(4):
            pl.when(g >= end)(load(g).wait)

    def stored(g):
        for level in range(strips):
            store(g, level).wait()

    loop(begin, end, stored)
    for copy in copies:
        copy.wait()


def smooth_part(part, meta, plan, velocity, colop, rowop, cuts, early=()):
    pieces = len(cuts)
    sizes = [high - low for low, high in zip((0,) + cuts[:-1], cuts)]
    any_space = pl.BlockSpec(memory_space=pltpu.HBM)
    smem = pl.BlockSpec(memory_space=pltpu.SMEM)
    piece_shapes = [jax.ShapeDtypeStruct((2, size, WIDTH), F32) for size in sizes]
    strip = jax.ShapeDtypeStruct((SNAPS, 2, 2, 8, WIDTH), F32)
    room = cuts[-1] + GAP
    total = jax.ShapeDtypeStruct((HALF, 5, 2, 8, WIDTH), F32)
    strips, sums = (3, 2) if part else (4, 0)
    out = pl.pallas_call(
        functools.partial(smooth_kernel, part, cuts),
        in_specs=[smem] * 2 + [any_space] * (3 + len(early)),
        out_specs=[any_space] * (strips + sums + 2 * pieces) + [smem, smem],
        scratch_shapes=[
            pltpu.VMEM((SNAPS, 2, ROWS, WIDTH), F32),
            pltpu.VMEM((2 * MAXS + 1, EXT, 3 * ROWS), BF16),
            pltpu.VMEM((3 * WIDTH, WIDTH), BF16),
        ] + [pltpu.VMEM((SNAPS, 2, 2, 8, WIDTH), F32)] * 4
        + ([pltpu.VMEM((PHASES, 5, 2, 8, WIDTH), F32)] if part else []) + [
            pltpu.VMEM((GROUP * 2 * ROWS, 3 * WIDTH), BF16),
            pltpu.VMEM((GROUP, 2, 3 * ROWS, WIDTH), BF16),
            pltpu.VMEM((2, room, WIDTH), F32),
            pltpu.VMEM((2, room, WIDTH), F32),
            pltpu.SMEM((8,), I32),
            pltpu.SemaphoreType.DMA((GROUPS,)),
            pltpu.SemaphoreType.DMA((GROUPS, 4)),
            pltpu.SemaphoreType.DMA((4 + 2 * pieces,)),
        ],
        out_shape=[strip] * strips + [total] * sums + piece_shapes * 2
        + [jax.ShapeDtypeStruct((SNAPS * 6,), I32), jax.ShapeDtypeStruct((16,), I32)],
        compiler_params=pltpu.CompilerParams(vmem_limit_bytes=62 * MIB),
        name="smooth_part",
    )(meta, plan, velocity, colop, rowop, *early)
    packs = out[strips + sums:]
    return out[:strips], out[strips:strips + sums], packs[:pieces], packs[pieces:2 * pieces], out[-2], out[-1]


def finish_kernel(levels, cuts, meta, plan, *refs):
    parts, many = len(cuts), len(levels)
    pos_refs, refs = refs[:parts], refs[parts:]
    strips, refs = [refs[many * k:many * (k + 1)] for k in range(parts)], refs[many * parts:]
    pieces = []
    for k in range(parts):
        count = len(cuts[k])
        pieces.append((refs[:count], refs[count:2 * count]))
        refs = refs[2 * count:]
    outs, refs = refs[:2 * many], refs[2 * many:]
    acc, y_buf, *buffers, y_sem, out_sem, sem = refs
    middle = plan[6] if parts == 2 else I32(GROUPS)
    ranges = [(I32(0), middle), (middle, I32(GROUPS))][:parts]

    def loop(low, high, body):
        lax.fori_loop(low, high, lambda g, carry: (body(g), carry)[1], 0)

    def load(k, g, at):
        rows = pl.ds(GROUP * g, GROUP)
        return pltpu.make_async_copy(strips[k][at].at[rows], y_buf.at[at, rows], y_sem.at[at, g])

    packs = [[] for _ in range(parts)]
    total = 0
    for k in range(parts):
        low = 0
        first, last = ranges[k]
        for piece, high in enumerate(cuts[k]):
            for side in range(2):
                begin = pos_refs[k][6 * GROUP * jnp.minimum(first, GROUPS - 1) + 3 * side + levels[0]]
                end = pos_refs[k][6 * (GROUP * jnp.maximum(last, 1) - 1) + 3 * side + levels[-1]] + 16
                for row_at in range(low, high, CHUNK):
                    stop = min(row_at + CHUNK, high)
                    copy = pltpu.make_async_copy(
                        pieces[k][side][piece].at[:, row_at - low:stop - low],
                        buffers[2 * k + side].at[:, row_at:stop], sem.at[total])
                    total += 1
                    packs[k].append((copy, (first < last) & (begin < stop) & (end > row_at)))
            low = high
    for at in range(many):
        for k in range(parts):
            if at == 0:
                for copy, needed in packs[k]:
                    pl.when(needed)(copy.start)
            loop(*ranges[k], lambda g, k=k, at=at: load(k, g, at).start())
    row = lax.broadcasted_iota(I32, (8, WIDTH), 0)

    def one(n, k, at):
        phase = meta[2 * SNAPS + n]
        for place in range(2):
            side = 1 - place
            have = level_rows(needs(meta[n])[side], levels[at])
            pos = pos_refs[k][6 * n + 3 * side + levels[at]]
            skew = pos & 7
            base = pl.multiple_of(pos - skew, 8)
            turn = skew if place == 0 else (skew + have) & 7
            known = jnp.where(meta[3 * SNAPS] == 2 * place, 0, have)
            keep = row < known if place == 0 else row >= 8 - known
            fields = []
            for comp in range(2):
                lower = buffers[2 * k + side][comp, pl.ds(base, 8)]
                upper = buffers[2 * k + side][comp, pl.ds(base + 8, 8)]
                tile = pltpu.roll(jnp.where(row >= skew, lower, upper), (8 - turn) & 7, 0)
                fields.append(y_buf[at, n, place, comp] + jnp.where(keep, tile, 0.0))
            u, v = fields
            for at_field, field in enumerate((u, v, u * u, v * v, u * v)):
                acc[at, phase, at_field, place] += field

    def group(g, k, at):
        load(k, g, at).wait()
        for b in range(GROUP):
            one(GROUP * g + b, k, at)

    stores = []
    for at in range(many):
        acc[at] = jnp.zeros(acc.shape[1:], F32)
        for k in range(parts):
            if at == 0:
                for copy, needed in packs[k]:
                    pl.when(needed)(copy.wait)
            loop(*ranges[k], lambda g, k=k, at=at: group(g, k, at))
        for which, part in enumerate((slice(0, HALF), slice(HALF, PHASES))):
            stores.append(pltpu.make_async_copy(acc.at[at, part], outs[2 * at + which], out_sem.at[len(stores)]))
            stores[-1].start()
    for copy in stores:
        copy.wait()


def finish_levels(levels, meta, plan, parts):
    any_space = pl.BlockSpec(memory_space=pltpu.HBM)
    smem = pl.BlockSpec(memory_space=pltpu.SMEM)
    shape = jax.ShapeDtypeStruct((HALF, 5, 2, 8, WIDTH), F32)
    many = len(levels)
    cuts = [part[2] for part in parts]
    strips = [part[1][level] for part in parts for level in levels]
    packs = [piece for part in parts for side in part[3:5] for piece in side]
    chunks = sum(2 * (-(-(high - low) // CHUNK)) for some in cuts for low, high in zip((0,) + some[:-1], some))
    out = pl.pallas_call(
        functools.partial(finish_kernel, levels, cuts),
        in_specs=[smem] * (2 + len(parts)) + [any_space] * (len(strips) + len(packs)),
        out_specs=[any_space] * (2 * many),
        out_shape=[shape] * (2 * many),
        scratch_shapes=[
            pltpu.VMEM((many, PHASES, 5, 2, 8, WIDTH), F32),
            pltpu.VMEM((many, SNAPS, 2, 2, 8, WIDTH), F32),
        ] + [pltpu.VMEM((2, some[-1] + GAP, WIDTH), F32) for some in cuts for _ in range(2)] + [
            pltpu.SemaphoreType.DMA((many, GROUPS)),
            pltpu.SemaphoreType.DMA((2 * many,)),
            pltpu.SemaphoreType.DMA((chunks,)),
        ],
        compiler_params=pltpu.CompilerParams(vmem_limit_bytes=62 * MIB),
        name="finish_levels",
    )(meta, plan, *[part[0] for part in parts], *strips, *packs)
    return [(out[2 * at], out[2 * at + 1]) for at in range(many)]


def scale_work(levels, message, reply, mines, others, mean, moment, a_buf, b_buf, load_sem, store_sem):
    many = len(levels)
    parts = [(k, slice(start, start + BLOCK)) for k in range(many) for start in range(0, HALF, BLOCK)]
    loads, stores = [], []
    for at, (k, part) in enumerate(parts):
        loads.append([pltpu.make_async_copy(mines[k].at[part], a_buf.at[k, part], load_sem.at[2 * at])])
        if others[k] is not None:
            loads[-1].append(pltpu.make_async_copy(others[k].at[part], b_buf.at[k, part], load_sem.at[2 * at + 1]))
        group = []
        if moment is None:
            stores.append([pltpu.make_async_copy(a_buf.at[k, part], mean.at[part], store_sem.at[4 * at])])
            continue
        for place in range(2):
            first = 8 * levels[k] if place == 0 else ROWS - 8 - 8 * levels[k]
            rows = slice(first, first + 8)
            for which, (fields, out) in enumerate(((slice(0, 2), mean), (slice(2, 5), moment))):
                group.append(pltpu.make_async_copy(
                    a_buf.at[k, part, fields, place], out.at[part, :, rows], store_sem.at[4 * at + 2 * place + which]))
        stores.append(group)

    def begin():
        for copies in loads:
            for copy in copies:
                copy.start()

    def work():
        for at, (k, part) in enumerate(parts):
            for copy in loads[at]:
                copy.wait()

            def one(p, carry, k=k):
                count = jnp.full((8, WIDTH), message[0, p] + reply[0, HALF + p], I32).astype(F32)
                a_buf[k, p] = (a_buf[k, p] + b_buf[k, p]) * (1.0 / jnp.maximum(count, 1.0))
                return carry

            if others[k] is not None:
                lax.fori_loop(part.start, part.stop, one, 0, unroll=2)
            for copy in stores[at]:
                copy.start()

    def end():
        for copies in stores:
            for copy in copies:
                copy.wait()

    return begin, work, end


def scale_scratch(many):
    parts = many * HALF // BLOCK
    buffer = pltpu.VMEM((many, HALF, 5, 2, 8, WIDTH), F32)
    return [buffer, buffer, pltpu.SemaphoreType.DMA((2 * parts,)), pltpu.SemaphoreType.DMA((4 * parts,))]


OUTPUTS = [jax.ShapeDtypeStruct((HALF, 2, ROWS, WIDTH), F32), jax.ShapeDtypeStruct((HALF, 3, ROWS, WIDTH), F32)]


def scale_kernel(levels, ready, message, reply, *refs):
    many = len(levels)
    pairs, mines, others = list(refs), [], []
    for level in levels:
        mines.append(pairs.pop(0))
        others.append(None if level == 3 and ready else pairs.pop(0))
    for step in scale_work(levels, message, reply, mines, others, *refs[-6:]):
        step()


def scale_levels(levels, counts, pairs, before, ready=False):
    many = len(levels)
    sums = [value for pair in pairs for value in pair]
    smem = pl.BlockSpec(memory_space=pltpu.SMEM)
    hbm = pl.BlockSpec(memory_space=pltpu.HBM)
    return pl.pallas_call(
        functools.partial(scale_kernel, levels, ready),
        in_specs=[smem] * 2 + [hbm] * (len(sums) + len(before)),
        out_specs=[hbm] * 2,
        out_shape=OUTPUTS,
        scratch_shapes=scale_scratch(many),
        input_output_aliases={2 + len(sums): 0, 3 + len(sums): 1} if before else {},
        compiler_params=pltpu.CompilerParams(vmem_limit_bytes=62 * MIB),
        name="scale_levels",
    )(*counts, *sums, *before)


def exchange_kernel(up, dn, mine, theirs, message, counts, below, above, other, reply, middle, reply_counts, *refs):
    *scratch, sem, send_sem, recv_sem = refs
    snap, tile = lax.axis_index("snap"), lax.axis_index("tile")
    size = lax.axis_size("tile")
    to_up = (snap, lax.rem(tile + size - 1, size))
    to_dn = (snap, lax.rem(tile + 1, size))
    to_core = (1 - snap, tile)
    barrier = pltpu.get_barrier_semaphore()
    for target in (to_up, to_dn, to_core):
        pl.semaphore_signal(barrier, inc=1, device_id=target, device_id_type=pl.DeviceIdType.MESH)
    pl.semaphore_wait(barrier, 3)
    rows = up.shape[1] // SPLIT
    moves = [(theirs, other, to_core), (message, reply, to_core)]
    for at in range(SPLIT):
        part = slice(rows * at, rows * (at + 1))
        moves += [(up.at[:, part], below.at[:, part], to_up), (dn.at[:, part], above.at[:, part], to_dn)]
    copies = []
    for source, landing, target in moves:
        copies.append(pltpu.make_async_remote_copy(
            src_ref=source, dst_ref=landing, send_sem=send_sem.at[len(copies)], recv_sem=recv_sem.at[len(copies)],
            device_id=target, device_id_type=pl.DeviceIdType.MESH))
    for copy in copies:
        copy.start()
    for copy in copies[:2]:
        copy.wait()
    fetch = pltpu.make_async_copy(reply, reply_counts, sem.at[0])
    fetch.start()
    fetch.wait()
    for step in scale_work((3,), counts, reply_counts, [mine], [other], middle, None, *scratch):
        step()
    for copy in copies[2:]:
        copy.wait()


def exchange(up, dn, sums, message):
    hbm = pl.BlockSpec(memory_space=pltpu.HBM)
    sends = (up, dn, sums[1], message)
    return pl.pallas_call(
        exchange_kernel,
        in_specs=[hbm] * 5 + [pl.BlockSpec(memory_space=pltpu.SMEM)],
        out_specs=[hbm] * 5,
        out_shape=[jax.ShapeDtypeStruct(value.shape, value.dtype) for value in (*sends, sums[0])],
        scratch_shapes=[pltpu.SMEM((8, 128), I32)] + scale_scratch(1) + [
            pltpu.SemaphoreType.DMA((1,)),
            pltpu.SemaphoreType.DMA((2 + 2 * SPLIT,)),
            pltpu.SemaphoreType.DMA((2 + 2 * SPLIT,)),
        ],
        compiler_params=pltpu.CompilerParams(collective_id=0, has_side_effects=True, vmem_limit_bytes=62 * MIB),
        name="exchange",
    )(up, dn, *sums, message, message)


def to_partner(value):
    return lax.ppermute(value, "snap", [(0, 1), (1, 0)])


def to_above(value):
    size = lax.axis_size("tile")
    return lax.ppermute(value, "tile", [(i + 1, i) for i in range(size - 1)])


def to_below(value):
    size = lax.axis_size("tile")
    return lax.ppermute(value, "tile", [(i, i + 1) for i in range(size - 1)])


def level_cuts(cuts, level):
    return cuts[:level + 1]


def send(up_pieces, dn_pieces):
    from_below = [to_above(piece) for piece in up_pieces]
    from_above = [to_below(piece) for piece in dn_pieces]
    return from_below, from_above


def per_device(velocity, offsets, phase):
    snap = lax.axis_index("snap")
    tile = lax.axis_index("tile")
    dy, dx = offsets[:, 0].astype(I32), offsets[:, 1].astype(I32)
    turned = lax.rem(phase.astype(I32) + PHASES - HALF * snap, PHASES)
    kind = jnp.where(tile == 0, 0, jnp.where(tile == lax.axis_size("tile") - 1, 2, 1)).astype(I32)
    meta = jnp.concatenate([dy, dx, turned, kind[None]])
    colop = jnp.asarray(column_constant())
    rowop = jnp.asarray(row_constant())
    onehot = (turned[:, None] == jnp.arange(PHASES, dtype=I32)[None, :]).astype(I32)
    own = jnp.sum(onehot, axis=0)

    smooth = functools.partial(smooth_part, velocity=velocity, colop=colop, rowop=rowop)

    def full(counts, *_):
        strips, sums, up, dn, positions, plan = smooth(2, meta, meta, cuts=FULL_CUTS)
        below, above = send(up, dn)
        part = (positions, strips, FULL_CUTS, below, above)
        totals = finish_levels((0, 1), meta, plan, [part]) + finish_levels((2,), meta, plan, [part])
        totals = [(mine, to_partner(theirs)) for mine, theirs in (sums, *totals)]
        before = scale_levels((3, 0), counts, totals[:2], ())
        return tuple(scale_levels((1, 2), counts, totals[2:], before))

    def last(counts, mine, other, mean, moment):
        return tuple(scale_levels((2,), counts, [(mine, other)], (mean, moment)))

    strips_a, _, up_a, dn_a, pos_a, plan = smooth(0, meta, meta, cuts=FIRST_CUTS)
    below_a, above_a = send(up_a, dn_a)
    message = jnp.broadcast_to(jnp.concatenate([own, plan[8:], jnp.zeros((48,), I32)])[None], (8, 128))
    strips_b, sums, up_b, dn_b, pos_b, _ = smooth(1, meta, plan, cuts=REST_CUTS, early=(strips_a[3],))
    below_b, above_b, _, reply, middle = exchange(up_b[0], dn_b[0], sums, message)
    counts = (message, reply)
    over = jnp.max(jnp.maximum(message, reply)[0:1, PHASES:PHASES + 8])
    parts = [(pos_a, strips_a, FIRST_CUTS, below_a, above_a), (pos_b, strips_b, REST_CUTS, [below_b], [above_b])]
    totals = finish_levels((0, 1), meta, plan, parts) + finish_levels((2,), meta, plan, parts)
    totals = [(mine, to_partner(theirs)) for mine, theirs in totals]
    before = scale_levels((3, 0, 1), counts, [(middle,), *totals[:2]], (), True)
    return lax.cond(over <= 0, last, full, counts, *totals[2], *before)


def solution(mesh):
    in_specs = (P("snap", None, "tile", None), P("snap", None), P("snap"))
    out_specs = (P("snap", None, "tile", None), P("snap", None, "tile", None))
    return jax.shard_map(
        per_device, mesh=mesh, in_specs=in_specs, out_specs=out_specs, check_vma=False
    )
```
